32 devices in a mesh: strips: 2 (over y), spax: 16 (over z, x, core).
Axes of the slice: x: 2, y: 2, z: 4, core: 2. Of those that a mesh axis runs over, the one named last changes fastest.
Arguments:
- cube: float32 [4096, 3584], P('strips', 'spax'), parts along dimension 0, may hold values from -6 to 6
- templates: float32 [256, 3584], replicated, may hold values from -0.5 to 6.5
- bin_id: int32 [4096], P('strips'), parts along dimension 0, may hold values from 0 to 511, never falling along the last dimension, each value on 1 to 16 neighbouring positions
- owner_bins: int32 [1024], P('strips'), parts along dimension 0, may hold values from 0 to 511, each once
- line_start: int32 [8, 4096], P(None, 'strips'), parts along dimension 1, may hold values from 0 to 3536
- line_width: int32 [8, 4096], P(None, 'strips'), parts along dimension 1, may hold values from 9 to 48
Outputs:
- weights: float32 [1024, 256], P(('strips', 'spax')), parts along dimension 0
- moments: float32 [24, 4096], P(None, ('strips', 'spax')), parts along dimension 1
The draws below stay inside these ranges and needn't reach their ends.
There are 2 independent parts, one for each index of `strips`. The reference program is written for one: setup_inputs(seed, part) draws one part's arguments, and reference() takes and returns one part's arrays. A program takes and returns all parts, laid end to end along the dimension named above; an argument that names none is the same for every part. Nothing has to cross between parts.
All inputs are finite; a program needn't handle non-finite values.
Results may differ from the reference program's by a relative error of at most 0.0003.
Values sent between devices are 32-bit elements; how exact they have to be, the bound alone decides.
No kernel may reach another device: no remote copies, remote signals or barrier semaphores. Data moves between devices by JAX's collectives and lax.ppermute only.
A program may use at most 128 MiB of HBM per device.

```python
import math
import jax
import jax.numpy as jnp
import numpy as np
from jax import lax

L = 3584
K = 256
NL = 8
WMAX = 48
MOST = 16
S = 2048
B = 512


def draw_templates(key, part):
    key = jax.random.fold_in(key, 11)
    center_key, noise_key, height_key = jax.random.split(key, 3)
    profile_width = 1.3 / K
    noise_level = 0.0775 * 6.0 * math.sqrt(math.pi * profile_width / 2.0)
    jitter = jax.random.uniform(center_key, (K,), jnp.float32, -0.4, 0.4)
    height = jax.random.uniform(height_key, (K, 1), jnp.float32, 5.0, 6.0)
    noise = jnp.clip(jax.random.normal(noise_key, (K, L), jnp.float32), -4.0, 4.0)
    centers = (jnp.arange(K, dtype=jnp.float32) + 0.5 + jitter) / K
    grid = (jnp.arange(L, dtype=jnp.float32) + 0.5) / L
    offset = (grid[None, :] - centers[:, None]) / profile_width
    profile = height / (1.0 + offset * offset)
    return profile + noise_level * noise


def with_ends(array, rng, low, top_value):
    extent = array.shape
    index_at = [jax.random.randint(jax.random.fold_in(rng, axis), (), 0, extent[axis]) for axis in range(len(extent))]
    array = array.at[tuple(index_at)].set(low)
    longest = extent.index(max(extent))
    index_at[longest] = (index_at[longest] + 1) % extent[longest]
    return array.at[tuple(index_at)].set(top_value)


def block_levels(stream_key, shape, pieces, least, top_value):
    gain, own = 1.0, jax.random.fold_in(stream_key, 6)
    for axis_at, blocks in pieces:
        heights = jnp.exp(jax.random.uniform(jax.random.fold_in(own, axis_at), (blocks,), jnp.float32, least / len(pieces), top_value / len(pieces)))
        gain = gain * jnp.repeat(heights, shape[axis_at] // blocks).reshape([-1 if axis == axis_at else 1 for axis in range(len(shape))])
    return gain


def split_up(number_of, total, bound, skew):
    portions = [(1 << 20) // math.isqrt(rank ** skew) + 1 for rank in range(2, number_of + 1)]
    rest, holding = total - bound - (number_of - 1), [1] * (number_of - 1)
    while rest > 0:
        candidates = [i for i in range(number_of - 1) if holding[i] < bound]
        pool, left = sum([portions[i] for i in candidates]), rest
        for i in candidates:
            more = min(bound - holding[i], max(1, left * portions[i] // pool), rest)
            holding[i] = holding[i] + more
            rest = rest - more
    return np.array([bound] + holding)


def ragged(rng, count, total, most, skew):
    if count == 2:
        one = jax.random.randint(rng, (), max(1, total - most), min(most, total - 1) + 1)
        return jnp.stack([one, total - one])
    tallies = jnp.asarray(split_up(count, total, most, skew), jnp.int32)
    pairs = (count - 1) // 2
    source_of, sink = tallies[1:1 + 2 * pairs:2], tallies[2:2 + 2 * pairs:2]
    margin = jnp.minimum(source_of - 1, most - sink)
    passed = jax.random.randint(jax.random.fold_in(rng, 1), (pairs,), 0, 1 << 20) % (margin + 1)
    tallies = tallies.at[1:1 + 2 * pairs:2].set(source_of - passed).at[2:2 + 2 * pairs:2].set(sink + passed)
    return tallies[jax.random.permutation(jax.random.fold_in(rng, 2), count)]


def centred(key, dims, scale, most, cuts=(), kind=jnp.bfloat16):
    values = jax.random.normal(key, dims, jnp.float32) * scale
    if len(cuts) > 0:
        values = block_levels(key, dims, cuts, -0.22, 0.18) * values
    return jnp.clip(values, min=-most, max=most).astype(kind)


def setup_inputs(seed: int = 0, part: int = 0) -> dict:
    streams_of = jax.random.split(jax.random.key(seed), 7)
    part_splits = jax.random.split(jax.random.fold_in(streams_of[6], part), 7)
    cube = centred(part_splits[0], (S, L), 1.0, 6.0, ((1, 16),), jnp.float32)
    templates = draw_templates(jax.random.fold_in(streams_of[6], 71), part)
    bin_id = jnp.searchsorted(jnp.cumsum(ragged(part_splits[2], B, S, MOST, 2)), jnp.arange(S), side="right").astype(jnp.int32)
    owner_bins = jax.random.permutation(part_splits[3], B).astype(jnp.int32)
    line_start = with_ends(jax.random.randint(part_splits[4], (NL, S), 0, L - WMAX + 1), jax.random.fold_in(part_splits[4], 1), 0, L - WMAX).astype(jnp.int32)
    line_width = with_ends(jax.random.randint(part_splits[5], (NL, S), WMAX // 6 + 1, WMAX + 1), jax.random.fold_in(part_splits[5], 1), WMAX // 6 + 1, WMAX).astype(jnp.int32)
    return {"cube": cube, "templates": templates, "bin_id": bin_id, "owner_bins": owner_bins, "line_start": line_start, "line_width": line_width}


def line_moments(residual, wave_index, starts, widths):
    zeroth = []
    first = []
    second = []
    for line in range(starts.shape[0]):
        begin = starts[line][:, None]
        span = widths[line][:, None]
        inside = (wave_index[None, :] >= begin) & (wave_index[None, :] < begin + span)
        masked = jnp.where(inside, residual, jnp.zeros_like(residual))
        velocity = (2.0 * (wave_index[None, :] - begin).astype(jnp.float32) + 1.0) / span.astype(jnp.float32) - 1.0
        weighted = masked * velocity
        zeroth.append(jnp.sum(masked, axis=1))
        first.append(jnp.sum(weighted, axis=1))
        second.append(jnp.sum(weighted * velocity, axis=1))
    return jnp.stack(zeroth + first + second, axis=0)

def reference(cube, templates, bin_id, owner_bins, line_start, line_width):
    total_bins = owner_bins.shape[0]
    spaxels = cube.shape[0]
    counts = jax.ops.segment_sum(jnp.ones((spaxels,), jnp.float32), bin_id, total_bins)
    bin_means = jax.ops.segment_sum(cube, bin_id, total_bins) / counts[:, None]
    slot_means = jnp.take(bin_means, owner_bins, axis=0)
    gram = jnp.dot(templates, templates.T, precision=lax.Precision.HIGHEST) / L
    factor = jnp.linalg.cholesky(gram)
    projections = jnp.dot(slot_means, templates.T, precision=lax.Precision.HIGHEST) / L
    weights = jax.scipy.linalg.cho_solve((factor, True), projections.T).T
    continua = jnp.dot(weights, templates, precision=lax.Precision.HIGHEST)
    slot_of_bin = jnp.zeros((total_bins,), jnp.int32).at[owner_bins].set(jnp.arange(total_bins, dtype=jnp.int32))
    residual = cube - jnp.take(continua, jnp.take(slot_of_bin, bin_id), axis=0)
    wave_index = jnp.arange(L, dtype=jnp.int32)
    sums = line_moments(residual, wave_index, line_start, line_width)
    divisor = jnp.concatenate([line_width, line_width, line_width], axis=0).astype(jnp.float32)
    return (weights, sums / divisor)
```

```python
import functools

import jax
import jax.numpy as jnp
from jax import lax
from jax.experimental import pallas as pl
from jax.experimental.pallas import tpu as pltpu
from jax.sharding import PartitionSpec as P

HIGHEST = lax.Precision.HIGHEST
F32 = jnp.float32
BF16 = jnp.bfloat16
LANES = 128
SUB = 8
VMEM_LIMIT = 48 * 1024 * 1024

NT = (((1,), (1,)), ((), ()))
NN = (((1,), (0,)), ((), ()))


def split3(x):
    hi = x.astype(BF16)
    rest = x - hi.astype(F32)
    mid = rest.astype(BF16)
    low = (rest - mid.astype(F32)).astype(BF16)
    return hi, mid, low


def dot(a, b, dims):
    return lax.dot_general(a, b, dims, preferred_element_type=F32)


def dot_f32(a, b, dims):
    return lax.dot_general(a, b, dims, precision=HIGHEST, preferred_element_type=F32)


def project_kernel(device_ref, bins_ref, owner_ref, cube_ref, templates_ref, out_ref, *, chunk):
    width, spaxels = cube_ref.shape
    slots = owner_ref.shape[0]
    full_width = templates_ref.shape[1]
    owner = owner_ref[...]
    sums = jnp.zeros((slots, width), F32)
    counts = jnp.zeros((slots, LANES), F32)
    for at in range(0, spaxels, chunk):
        here = owner == bins_ref[:, at : at + chunk]
        ones = jnp.where(here, 1.0, 0.0)
        for lane in range(0, chunk, LANES):
            counts = counts + ones[:, lane : lane + LANES]
        member = ones.astype(BF16)
        for part in split3(cube_ref[:, at : at + chunk]):
            sums = sums + dot(member, part, NT)
    means = sums / jnp.sum(counts, axis=1, keepdims=True)
    first = device_ref[0] * width
    window = min(full_width, -(-(width + LANES - 1) // LANES) * LANES)
    base = jnp.minimum(first // LANES * LANES, full_width - window)
    held = templates_ref[:, pl.ds(pl.multiple_of(base, LANES), window)]
    mine = pltpu.roll(held, window - (first - base), 1)[:, :width]
    out_ref[...] = dot_f32(means, mine, NT) * (1.0 / full_width)


def project(device, bins, owner, cube, templates):
    width, spaxels = cube.shape
    slots = owner.shape[0]
    block = min(slots, 512)
    whole = lambda i: (0, 0)
    return pl.pallas_call(
        functools.partial(project_kernel, chunk=min(spaxels, 512)),
        grid=(slots // block,),
        in_specs=[
            pl.BlockSpec(memory_space=pltpu.SMEM),
            pl.BlockSpec((1, spaxels), whole),
            pl.BlockSpec((block, 1), lambda i: (i, 0)),
            pl.BlockSpec((width, spaxels), whole),
            pl.BlockSpec(templates.shape, whole),
        ],
        out_specs=pl.BlockSpec((block, templates.shape[0]), lambda i: (i, 0)),
        out_shape=jax.ShapeDtypeStruct((slots, templates.shape[0]), F32),
        compiler_params=pltpu.CompilerParams(vmem_limit_bytes=VMEM_LIMIT),
        name="project",
    )(device, bins, owner, cube, templates)


def invert_tile(tile):
    size = tile.shape[0]
    count = size // SUB
    lanes = lax.broadcasted_iota(jnp.int32, (SUB, size), 1)
    rows_at = lax.broadcasted_iota(jnp.int32, (SUB, size), 0)
    rows = [tile[i * SUB : (i + 1) * SUB, :] for i in range(count)]
    for k in range(count):
        block = rows[k]
        first = k * SUB
        a = {}
        for i in range(SUB):
            for j in range(i, SUB):
                a[i, j] = jnp.broadcast_to(block[i : i + 1, first + j : first + j + 1], (SUB, size))

        def at(i, j):
            return a[(i, j) if i <= j else (j, i)]

        for p in range(SUB):
            inverse = 1.0 / a[p, p]
            others = [i for i in range(SUB) if i != p]
            scaled = {i: at(i, p) * inverse for i in others}
            old = {i: at(i, p) for i in others}
            for i in others:
                for j in others:
                    if i <= j:
                        a[i, j] = a[i, j] - scaled[i] * old[j]
            for i in others:
                a[(i, p) if i <= p else (p, i)] = scaled[i]
            a[p, p] = -inverse
        columns = []
        for j in range(SUB):
            column = at(0, j)
            for i in range(1, SUB):
                column = jnp.where(rows_at == i, at(i, j), column)
            columns.append(column)
        swept = jnp.zeros((SUB, size), F32)
        for j in range(SUB):
            swept = swept - columns[j] * jnp.broadcast_to(block[j : j + 1, :], (SUB, size))
        for j in range(SUB):
            swept = jnp.where(lanes == first + j, columns[j], swept)
        inside = (lanes >= first) & (lanes < first + SUB)
        for i in range(count):
            if i == k:
                continue
            new = jnp.where(inside, 0.0, rows[i])
            for j in range(SUB):
                spread = jnp.broadcast_to(rows[i][:, first + j : first + j + 1], (SUB, size))
                new = new - spread * jnp.broadcast_to(swept[j : j + 1, :], (SUB, size))
            rows[i] = new
        rows[k] = swept
    return -jnp.concatenate(rows, axis=0)


def gram_kernel(templates_ref, gram_ref, first_ref, *, chunk):
    count, full_width = templates_ref.shape
    even = jnp.zeros((count, count), F32)
    mixed = jnp.zeros((count, count), F32)
    for at in range(0, full_width, chunk):
        hi, mid, low = split3(templates_ref[:, at : at + chunk])
        even = even + (dot(hi, hi, NT) + dot(mid, mid, NT))
        mixed = mixed + (dot(hi, mid, NT) + dot(hi, low, NT))
    gram = (even + (mixed + mixed.T)) * (1.0 / full_width)
    gram_ref[...] = gram
    first_ref[...] = invert_tile(gram[:LANES, :LANES])


def finish_kernel(gram_ref, first_ref, out_ref):
    first = first_ref[...]
    side = gram_ref[:LANES, LANES:]
    half = dot_f32(first, side, NN)
    schur = gram_ref[LANES:, LANES:] - dot_f32(side.T, half, NN)
    last = invert_tile(schur)
    cross = dot_f32(half, last, NN)
    out_ref[:LANES, :LANES] = first + dot_f32(cross, half, NT)
    out_ref[:LANES, LANES:] = -cross
    out_ref[LANES:, :LANES] = -cross.T
    out_ref[LANES:, LANES:] = last


def in_vmem(kernel, shapes, name, *arrays):
    return pl.pallas_call(
        kernel,
        out_shape=shapes,
        compiler_params=pltpu.CompilerParams(vmem_limit_bytes=VMEM_LIMIT),
        name=name,
    )(*arrays)


def window_sums(read, rows, first, begin, span, unroll):
    lines = begin.shape[0]
    sub = lax.broadcasted_iota(jnp.int32, (SUB, LANES), 0)
    spans = [jnp.broadcast_to(span[j : j + 1], (SUB, LANES)).astype(F32) for j in range(lines)]
    offsets = [
        (2 * (first + sub - jnp.broadcast_to(begin[j : j + 1], (SUB, LANES))) + 1).astype(F32) - spans[j]
        for j in range(lines)
    ]

    def add(block, shift, sums):
        size = block.shape[0]
        out = []
        for j in range(lines):
            m = offsets[j][:size] + shift
            masked = jnp.where(jnp.abs(m) < spans[j][:size], block, 0.0)
            weighted = masked * m
            out += [sums[3 * j] + masked, sums[3 * j + 1] + weighted, sums[3 * j + 2] + weighted * m]
        return out

    def step(i, sums):
        for u in range(unroll):
            row = (i * unroll + u) * SUB
            shift = (2 * row) if isinstance(row, int) else (2 * row).astype(F32)
            sums = add(read(row, SUB), shift, sums)
        return sums

    sums = [jnp.zeros((SUB, LANES), F32)] * (3 * lines)
    full = rows // SUB
    if full > unroll:
        sums = lax.fori_loop(0, full // unroll, step, sums)
        done = full // unroll * unroll
    else:
        done = 0
    for i in range(done, full):
        sums = add(read(i * SUB, SUB), 2.0 * i * SUB, sums)
    out = [jnp.sum(x, axis=0, keepdims=True) for x in sums]
    if rows % SUB:
        zero = jnp.zeros((rows % SUB, LANES), F32)
        tail = add(read(full * SUB, rows % SUB), 2.0 * full * SUB, [zero] * (3 * lines))
        out = [x + jnp.sum(y, axis=0, keepdims=True) for x, y in zip(out, tail)]
    return [out[3 * j + k] for k in range(3) for j in range(lines)]


def cube_kernel(device_ref, begin_ref, span_ref, cube_ref, out_ref):
    width = cube_ref.shape[0]
    first = device_ref[0] * width

    def tile(i, carry):
        lanes = pl.ds(pl.multiple_of(i * LANES, LANES), LANES)
        sums = window_sums(
            lambda row, size: cube_ref[pl.ds(row, size), lanes],
            width,
            first,
            begin_ref[:, lanes],
            span_ref[:, lanes],
            28,
        )
        for r, value in enumerate(sums):
            out_ref[r : r + 1, lanes] = value
        return carry

    lax.fori_loop(0, cube_ref.shape[1] // LANES, tile, 0)


def cube_windows(device, begin, span, cube):
    vmem = pl.BlockSpec(memory_space=pltpu.VMEM)
    return pl.pallas_call(
        cube_kernel,
        in_specs=[pl.BlockSpec(memory_space=pltpu.SMEM), vmem, vmem, vmem],
        out_specs=vmem,
        out_shape=jax.ShapeDtypeStruct((3 * begin.shape[0], cube.shape[1]), F32),
        compiler_params=pltpu.CompilerParams(vmem_limit_bytes=VMEM_LIMIT),
        name="cube_windows",
    )(device, begin, span, cube)


def owner_kernel(
    bins_ref, owner_ref, begin_ref, span_ref, projections_ref, inverse_ref, rows_ref,
    weights_ref, out_ref, continuum_ref,
):
    inverse = inverse_ref[...]
    weights_ref[...] = dot_f32(projections_ref[: weights_ref.shape[0], :], inverse, NN)
    member = jnp.where(bins_ref[...] == owner_ref[...], 1.0, 0.0).astype(BF16)
    picked = jnp.zeros((bins_ref.shape[0], inverse.shape[0]), F32)
    for part in split3(projections_ref[...]):
        picked = picked + dot(member, part, NN)
    spaxel_weights = dot_f32(picked, inverse, NN)
    full_width = rows_ref.shape[0]
    step = 512
    for at in range(0, full_width, step):
        continuum_ref[at : at + step, :] = dot_f32(rows_ref[at : at + step, :], spaxel_weights, NT)
    sums = window_sums(
        lambda row, size: continuum_ref[pl.ds(pl.multiple_of(row, SUB), size), :],
        full_width,
        0,
        begin_ref[...],
        span_ref[...],
        28,
    )
    for r, value in enumerate(sums):
        out_ref[r : r + 1, :] = value


def owned(bins, owner, begin, span, projections, inverse, rows, own_slots):
    return pl.pallas_call(
        owner_kernel,
        out_shape=(
            jax.ShapeDtypeStruct((own_slots, inverse.shape[0]), F32),
            jax.ShapeDtypeStruct((3 * begin.shape[0], bins.shape[0]), F32),
        ),
        scratch_shapes=[pltpu.VMEM((rows.shape[0], bins.shape[0]), F32)],
        compiler_params=pltpu.CompilerParams(vmem_limit_bytes=VMEM_LIMIT),
        name="owned",
    )(bins, owner, begin, span, projections, inverse, rows)


def shards(cube, templates, bin_id, owner_bins, line_start, line_width):
    devices = lax.axis_size("spax")
    device = lax.axis_index("spax")
    spaxels = cube.shape[0]
    total_bins = owner_bins.shape[0]
    own_spaxels = spaxels // devices
    own_slots = total_bins // devices
    here = device.reshape(1).astype(jnp.int32)
    columns = cube.T

    partial = project(here, bin_id[None, :], owner_bins[:, None], columns, templates)
    received = lax.all_to_all(partial.reshape(devices, own_slots, -1), "spax", 0, 0)
    mine = jnp.sum(received, axis=0)

    partial_sums = cube_windows(here, line_start, line_width, columns)
    cube_sums = lax.psum_scatter(partial_sums, "spax", scatter_dimension=1, tiled=True)

    count = templates.shape[0]
    gram, first = in_vmem(
        functools.partial(gram_kernel, chunk=512),
        (jax.ShapeDtypeStruct((count, count), F32), jax.ShapeDtypeStruct((LANES, LANES), F32)),
        "gram",
        templates,
    )
    inverse = in_vmem(finish_kernel, jax.ShapeDtypeStruct((count, count), F32), "finish", gram, first)

    blocks = [mine]
    for k in range(1, devices):
        blocks.append(lax.ppermute(mine, "spax", [(d, d ^ k) for d in range(devices)]))
    projections = jnp.concatenate(blocks, axis=0)
    order = device ^ jnp.arange(devices, dtype=jnp.int32)
    owner_row = jnp.take(owner_bins.reshape(devices, own_slots), order, axis=0).reshape(1, total_bins)

    own = lambda x: lax.dynamic_slice_in_dim(x, device * own_spaxels, own_spaxels, x.ndim - 1)
    begin, span = own(line_start), own(line_width)
    weights, continuum_sums = owned(
        own(bin_id)[:, None], owner_row, begin, span, projections, inverse, templates.T, own_slots
    )
    scale = span.astype(F32)
    divisor = jnp.concatenate([scale, scale * scale, scale * scale * scale], axis=0)
    return (weights, (cube_sums - continuum_sums) / divisor)


def solution(mesh):
    placed = (
        P("strips", "spax"),
        P(),
        P("strips"),
        P("strips"),
        P(None, "strips"),
        P(None, "strips"),
    )
    return jax.shard_map(
        shards,
        mesh=mesh,
        in_specs=placed,
        out_specs=(P(("strips", "spax"), None), P(None, ("strips", "spax"))),
        check_vma=False,
    )
```

```python
import functools

import jax
import jax.numpy as jnp
from jax import lax
from jax.experimental import pallas as pl
from jax.experimental.pallas import tpu as pltpu
from jax.sharding import PartitionSpec as P

HIGHEST = lax.Precision.HIGHEST
F32 = jnp.float32
BF16 = jnp.bfloat16
LANES = 128
SUB = 8
VMEM_LIMIT = 20 * 1024 * 1024

NT = (((1,), (1,)), ((), ()))
NN = (((1,), (0,)), ((), ()))


def split3(x):
    hi = x.astype(BF16)
    rest = x - hi.astype(F32)
    mid = rest.astype(BF16)
    low = (rest - mid.astype(F32)).astype(BF16)
    return hi, mid, low


def dot(a, b, dims):
    return lax.dot_general(a, b, dims, preferred_element_type=F32)


def dot_f32(a, b, dims):
    return lax.dot_general(a, b, dims, precision=HIGHEST, preferred_element_type=F32)


def template_window(width, full_width):
    return min(full_width, -(-(width + LANES - 1) // LANES) * LANES)


def project_kernel(
    device_ref, bins_ref, owner_ref, cube_ref, templates_ref, out_ref,
    held_ref, window_ref, cube_sem, window_sem, *, chunk,
):
    width, spaxels = cube_ref.shape
    slots = owner_ref.shape[1]
    full_width = templates_ref.shape[1]
    first = device_ref[0] * width
    window = window_ref.shape[1]
    base = pl.multiple_of(jnp.minimum(first // LANES * LANES, full_width - window), LANES)
    chunks = spaxels // chunk

    def cube_copy(i):
        lanes = pl.ds(i * chunk, chunk)
        return pltpu.make_async_copy(cube_ref.at[:, lanes], held_ref.at[:, lanes], cube_sem.at[i])

    window_copy = pltpu.make_async_copy(templates_ref.at[:, pl.ds(base, window)], window_ref, window_sem)

    @pl.when(pl.program_id(0) == 0)
    def _():
        for i in range(chunks):
            cube_copy(i).start()
        window_copy.start()

    owner = jnp.broadcast_to(owner_ref[...], (SUB, slots)).T[:, :1]
    sums = jnp.zeros((slots, width), F32)
    counts = jnp.zeros((slots, LANES), F32)
    for i in range(chunks):
        here = owner == bins_ref[:, i * chunk : (i + 1) * chunk]
        ones = jnp.where(here, 1.0, 0.0)
        for lane in range(0, chunk, LANES):
            counts = counts + ones[:, lane : lane + LANES]
        member = ones.astype(BF16)

        @pl.when(pl.program_id(0) == 0)
        def _(i=i):
            cube_copy(i).wait()

        for part in split3(held_ref[:, i * chunk : (i + 1) * chunk]):
            sums = sums + dot(member, part, NT)
    means = sums / jnp.sum(counts, axis=1, keepdims=True)

    @pl.when(pl.program_id(0) == 0)
    def _():
        window_copy.wait()

    mine = pltpu.roll(window_ref[...], window - (first - base), 1)[:, :width]
    out_ref[...] = dot_f32(means, mine, NT) * (1.0 / full_width)


def project(device, bins, owner, cube, templates):
    width, spaxels = cube.shape
    slots = owner.shape[1]
    block = min(slots, 512)
    chunk = min(spaxels, 512)
    count, full_width = templates.shape
    return pl.pallas_call(
        functools.partial(project_kernel, chunk=chunk),
        grid=(slots // block,),
        in_specs=[
            pl.BlockSpec(memory_space=pltpu.SMEM),
            pl.BlockSpec((1, spaxels), lambda i: (0, 0)),
            pl.BlockSpec((1, block), lambda i: (0, i)),
            pl.BlockSpec(memory_space=pl.ANY),
            pl.BlockSpec(memory_space=pl.ANY),
        ],
        out_specs=pl.BlockSpec((block, count), lambda i: (i, 0)),
        out_shape=jax.ShapeDtypeStruct((slots, count), F32),
        scratch_shapes=[
            pltpu.VMEM((width, spaxels), F32),
            pltpu.VMEM((count, template_window(width, full_width)), F32),
            pltpu.SemaphoreType.DMA((spaxels // chunk,)),
            pltpu.SemaphoreType.DMA,
        ],
        compiler_params=pltpu.CompilerParams(vmem_limit_bytes=VMEM_LIMIT),
        name="project",
    )(device, bins, owner, cube, templates)


def invert_tile(tile):
    size = tile.shape[0]
    count = size // SUB
    lanes = lax.broadcasted_iota(jnp.int32, (SUB, size), 1)
    rows_at = lax.broadcasted_iota(jnp.int32, (SUB, size), 0)
    rows = [tile[i * SUB : (i + 1) * SUB, :] for i in range(count)]
    for k in range(count):
        block = rows[k]
        first = k * SUB
        a = {}
        for i in range(SUB):
            for j in range(i, SUB):
                a[i, j] = jnp.broadcast_to(block[i : i + 1, first + j : first + j + 1], (SUB, size))

        def at(i, j):
            return a[(i, j) if i <= j else (j, i)]

        for p in range(SUB):
            inverse = 1.0 / a[p, p]
            others = [i for i in range(SUB) if i != p]
            scaled = {i: at(i, p) * inverse for i in others}
            old = {i: at(i, p) for i in others}
            for i in others:
                for j in others:
                    if i <= j:
                        a[i, j] = a[i, j] - scaled[i] * old[j]
            for i in others:
                a[(i, p) if i <= p else (p, i)] = scaled[i]
            a[p, p] = -inverse
        columns = []
        for j in range(SUB):
            column = at(0, j)
            for i in range(1, SUB):
                column = jnp.where(rows_at == i, at(i, j), column)
            columns.append(column)
        swept = jnp.zeros((SUB, size), F32)
        for j in range(SUB):
            swept = swept - columns[j] * jnp.broadcast_to(block[j : j + 1, :], (SUB, size))
        for j in range(SUB):
            swept = jnp.where(lanes == first + j, columns[j], swept)
        inside = (lanes >= first) & (lanes < first + SUB)
        for i in range(count):
            if i == k:
                continue
            new = jnp.where(inside, 0.0, rows[i])
            for j in range(SUB):
                spread = jnp.broadcast_to(rows[i][:, first + j : first + j + 1], (SUB, size))
                new = new - spread * jnp.broadcast_to(swept[j : j + 1, :], (SUB, size))
            rows[i] = new
        rows[k] = swept
    return -jnp.concatenate(rows, axis=0)


def gram_kernel(templates_ref, gram_ref, first_ref, *, chunk):
    count, full_width = templates_ref.shape
    even = jnp.zeros((count, count), F32)
    mixed = jnp.zeros((count, count), F32)
    for at in range(0, full_width, chunk):
        hi, mid, low = split3(templates_ref[:, at : at + chunk])
        even = even + (dot(hi, hi, NT) + dot(mid, mid, NT))
        mixed = mixed + (dot(hi, mid, NT) + dot(hi, low, NT))
    gram = (even + (mixed + mixed.T)) * (1.0 / full_width)
    gram_ref[...] = gram
    first_ref[...] = invert_tile(gram[:LANES, :LANES])


def finish_kernel(gram_ref, first_ref, out_ref):
    first = first_ref[...]
    side = gram_ref[:LANES, LANES:]
    half = dot_f32(first, side, NN)
    schur = gram_ref[LANES:, LANES:] - dot_f32(side.T, half, NN)
    last = invert_tile(schur)
    cross = dot_f32(half, last, NN)
    out_ref[:LANES, :LANES] = first + dot_f32(cross, half, NT)
    out_ref[:LANES, LANES:] = -cross
    out_ref[LANES:, :LANES] = -cross.T
    out_ref[LANES:, LANES:] = last


def in_vmem(kernel, shapes, name, *arrays):
    return pl.pallas_call(
        kernel,
        out_shape=shapes,
        compiler_params=pltpu.CompilerParams(vmem_limit_bytes=VMEM_LIMIT),
        name=name,
    )(*arrays)


def window_sums(read, rows, first, begin, span):
    lines = begin.shape[0]
    sub = lax.broadcasted_iota(jnp.int32, (SUB, LANES), 0)
    spans = [jnp.broadcast_to(span[j : j + 1], (SUB, LANES)).astype(F32) for j in range(lines)]
    offsets = [
        (2 * (first + sub - jnp.broadcast_to(begin[j : j + 1], (SUB, LANES))) + 1).astype(F32) - spans[j]
        for j in range(lines)
    ]

    def add(block, shift, sums):
        size = block.shape[0]
        out = []
        for j in range(lines):
            m = offsets[j][:size] + shift
            masked = jnp.where(jnp.abs(m) < spans[j][:size], block, 0.0)
            weighted = masked * m
            out += [sums[3 * j] + masked, sums[3 * j + 1] + weighted, sums[3 * j + 2] + weighted * m]
        return out

    full = rows // SUB
    out = [jnp.zeros((1, LANES), F32)] * (3 * lines)
    if full:
        sums = [jnp.zeros((SUB, LANES), F32)] * (3 * lines)
        for i in range(full):
            sums = add(read(i * SUB, SUB), 2.0 * i * SUB, sums)
        out = [jnp.sum(x, axis=0, keepdims=True) for x in sums]
    if rows % SUB:
        sums = [jnp.zeros((rows % SUB, LANES), F32)] * (3 * lines)
        sums = add(read(full * SUB, rows % SUB), 2.0 * full * SUB, sums)
        out = [x + jnp.sum(y, axis=0, keepdims=True) for x, y in zip(out, sums)]
    return [out[3 * j + k] for k in range(3) for j in range(lines)]


def cube_kernel(device_ref, begin_ref, span_ref, cube_ref, out_ref, *, head):
    width = cube_ref.shape[0]
    own = cube_ref.shape[1] // out_ref.shape[0]
    tiles = own // LANES

    def owner(i, carry):
        for t in range(tiles):
            lanes = pl.ds(pl.multiple_of(i * own + t * LANES, LANES), LANES)
            sums = window_sums(
                lambda row, size: cube_ref[pl.ds(row, size), lanes],
                width,
                device_ref[0] * width,
                begin_ref[:, lanes],
                span_ref[:, lanes],
            )
            for r, value in enumerate(sums):
                out_ref[i, head + t * len(sums) + r : head + t * len(sums) + r + 1, :] = value
        return carry

    lax.fori_loop(0, out_ref.shape[0], owner, 0)


def cube_windows(device, begin, span, cube, devices, head):
    vmem = pl.BlockSpec(memory_space=pltpu.VMEM)
    tail = 3 * begin.shape[0] * (cube.shape[1] // devices // LANES)
    return pl.pallas_call(
        functools.partial(cube_kernel, head=head),
        in_specs=[pl.BlockSpec(memory_space=pltpu.SMEM), vmem, vmem, vmem],
        out_specs=vmem,
        out_shape=jax.ShapeDtypeStruct((devices, head + tail, LANES), F32),
        compiler_params=pltpu.CompilerParams(vmem_limit_bytes=VMEM_LIMIT),
        name="cube_windows",
    )(device, begin, span, cube)


def pack_kernel(received_ref, sums_ref, out_ref):
    total = received_ref[0]
    for i in range(1, received_ref.shape[0]):
        total = total + received_ref[i]
    slots, count = total.shape
    for half in range(count // LANES):
        value = total[:, half * LANES : (half + 1) * LANES]
        for i in range(received_ref.shape[0]):
            out_ref[i, half * slots : (half + 1) * slots, :] = value
    head = slots * (count // LANES)
    out_ref[:, head:, :] = sums_ref[:, head:, :]


def owner_kernel(
    device_ref, starts_ref, bins_ref, owner_ref, begin_ref, span_ref, received_ref, inverse_ref, templates_ref,
    weights_ref, out_ref, continuum_ref,
):
    devices = received_ref.shape[0]
    own_slots, count = weights_ref.shape
    halves = count // LANES
    head = own_slots * halves
    own = begin_ref.shape[1]
    lines = begin_ref.shape[0]
    inverse = inverse_ref[...]
    device = device_ref[0]

    mine = jnp.concatenate(
        [received_ref[device, h * own_slots : (h + 1) * own_slots, :] for h in range(halves)], axis=1
    )
    weights_ref[...] = dot_f32(mine, inverse, NN)

    bins = jnp.broadcast_to(bins_ref[...], (SUB, own)).T[:, :1]
    member = jnp.where(bins == owner_ref[...], 1.0, 0.0).astype(BF16)
    picked = []
    for h in range(halves):
        block = received_ref[:, h * own_slots : (h + 1) * own_slots, :].reshape(devices * own_slots, LANES)
        hi, mid, low = split3(block)
        picked.append(dot(member, hi, NN) + (dot(member, mid, NN) + dot(member, low, NN)))
    spaxel_weights = dot_f32(jnp.concatenate(picked, axis=1), inverse, NN)

    full_width = templates_ref.shape[1]
    step = 512
    for at in range(0, full_width, step):
        value = dot_f32(spaxel_weights, templates_ref[:, at : at + step], NN)
        for t in range(step // LANES):
            continuum_ref[at // LANES + t] = value[:, t * LANES : (t + 1) * LANES]
    continuum_ref[full_width // LANES] = jnp.zeros((own, LANES), F32)

    begin = begin_ref[...]
    span = span_ref[...].astype(F32)
    centre = 2.0 * (begin - begin // LANES * LANES).astype(F32) + span - 1.0
    pad = jnp.zeros((LANES - 2 * lines, own), F32)
    columns = jnp.concatenate([centre, span, pad], axis=0).T
    continuum_lanes = lax.broadcasted_iota(jnp.int32, (SUB, LANES), 1)
    twice = (2 * continuum_lanes).astype(F32)
    rows_at = lax.broadcasted_iota(jnp.int32, (SUB, LANES), 0)
    found = []
    for g in range(own // SUB):
        rows = slice(g * SUB, (g + 1) * SUB)
        result = jnp.zeros((SUB, LANES), F32)
        for j in range(lines):
            left = right = None
            for r in range(SUB):
                tile = starts_ref[j, g * SUB + r] // LANES
                a = continuum_ref[tile, rows, :]
                b = continuum_ref[tile + 1, rows, :]
                left = a if left is None else jnp.where(rows_at == r, a, left)
                right = b if right is None else jnp.where(rows_at == r, b, right)
            width = jnp.broadcast_to(columns[rows, lines + j : lines + j + 1], (SUB, LANES))
            m = twice - jnp.broadcast_to(columns[rows, j : j + 1], (SUB, LANES))
            n = m + 2.0 * LANES
            left = jnp.where(jnp.abs(m) < width, left, 0.0)
            right = jnp.where(jnp.abs(n) < width, right, 0.0)
            left_m = left * m
            right_n = right * n
            for k, term in enumerate((left + right, left_m + right_n, left_m * m + right_n * n)):
                total = jnp.sum(term, axis=1, keepdims=True)
                result = jnp.where(continuum_lanes == k * lines + j, total, result)
        found.append(result)
    continuum_sums = jnp.concatenate(found, axis=0).T[: 3 * lines, :]

    cube_sums = received_ref[0, head:, :]
    for i in range(1, devices):
        cube_sums = cube_sums + received_ref[i, head:, :]
    scale = jnp.concatenate([span, span * span, span * span * span], axis=0)
    out_ref[...] = (cube_sums - continuum_sums) / scale


def owned(device, starts, bins, owner, begin, span, received, inverse, templates, own_slots):
    vmem = pl.BlockSpec(memory_space=pltpu.VMEM)
    smem = pl.BlockSpec(memory_space=pltpu.SMEM)
    own = begin.shape[1]
    return pl.pallas_call(
        owner_kernel,
        in_specs=[smem, smem] + [vmem] * 7,
        out_shape=(
            jax.ShapeDtypeStruct((own_slots, inverse.shape[0]), F32),
            jax.ShapeDtypeStruct((3 * begin.shape[0], own), F32),
        ),
        scratch_shapes=[pltpu.VMEM((templates.shape[1] // LANES + 1, own, LANES), F32)],
        compiler_params=pltpu.CompilerParams(vmem_limit_bytes=VMEM_LIMIT),
        name="owned",
    )(device, starts, bins, owner, begin, span, received, inverse, templates)


def shards(cube, templates, bin_id, owner_bins, line_start, line_width):
    devices = lax.axis_size("spax")
    device = lax.axis_index("spax")
    spaxels = cube.shape[0]
    total_bins = owner_bins.shape[0]
    count = templates.shape[0]
    own_spaxels = spaxels // devices
    own_slots = total_bins // devices
    here = device.reshape(1).astype(jnp.int32)
    columns = cube.T
    bins = bin_id[None, :]
    owner = owner_bins[None, :]

    partial = project(here, bins, owner, columns, templates)
    received = lax.all_to_all(partial.reshape(devices, own_slots, count), "spax", 0, 0)

    head = own_slots * (count // LANES)
    sums = cube_windows(here, line_start, line_width, columns, devices, head)
    gram, first = in_vmem(
        functools.partial(gram_kernel, chunk=512),
        (jax.ShapeDtypeStruct((count, count), F32), jax.ShapeDtypeStruct((LANES, LANES), F32)),
        "gram",
        templates,
    )
    received, sums, gram, first = lax.optimization_barrier((received, sums, gram, first))
    parcel = in_vmem(pack_kernel, jax.ShapeDtypeStruct(sums.shape, F32), "pack", received, sums)
    parcel, gram, first = lax.optimization_barrier((parcel, gram, first))
    arrived = lax.all_to_all(parcel, "spax", 0, 0)
    inverse = in_vmem(finish_kernel, jax.ShapeDtypeStruct((count, count), F32), "finish", gram, first)

    own = lambda x: lax.dynamic_slice_in_dim(x, device * own_spaxels, own_spaxels, 1)
    begin, span = own(line_start), own(line_width)
    return owned(here, begin, own(bins), owner, begin, span, arrived, inverse, templates, own_slots)


def solution(mesh):
    placed = (
        P("strips", "spax"),
        P(),
        P("strips"),
        P("strips"),
        P(None, "strips"),
        P(None, "strips"),
    )
    return jax.shard_map(
        shards,
        mesh=mesh,
        in_specs=placed,
        out_specs=(P(("strips", "spax"), None), P(None, ("strips", "spax"))),
        check_vma=False,
    )
```

```python
import functools

import jax
import jax.numpy as jnp
from jax import lax
from jax.experimental import pallas as pl
from jax.experimental.pallas import tpu as pltpu
from jax.sharding import PartitionSpec as P

HIGHEST = lax.Precision.HIGHEST
F32 = jnp.float32
BF16 = jnp.bfloat16
LANES = 128
SUB = 8
VMEM_LIMIT = 20 * 1024 * 1024

NT = (((1,), (1,)), ((), ()))
NN = (((1,), (0,)), ((), ()))


def split3(x):
    hi = x.astype(BF16)
    rest = x - hi.astype(F32)
    mid = rest.astype(BF16)
    low = (rest - mid.astype(F32)).astype(BF16)
    return hi, mid, low


def dot(a, b, dims):
    return lax.dot_general(a, b, dims, preferred_element_type=F32)


def dot_f32(a, b, dims):
    return lax.dot_general(a, b, dims, precision=HIGHEST, preferred_element_type=F32)


def template_window(width, full_width):
    return min(full_width, -(-(width + LANES - 1) // LANES) * LANES)


def project_kernel(
    device_ref, bins_ref, owner_ref, cube_ref, templates_ref, out_ref,
    held_ref, window_ref, bins_held_ref, owner_held_ref, cube_sem, window_sem, small_sem, *, chunk,
):
    width, spaxels = cube_ref.shape
    slots = out_ref.shape[0]
    full_width = templates_ref.shape[1]
    first = device_ref[0] * width
    window = window_ref.shape[1]
    base = pl.multiple_of(jnp.minimum(first // LANES * LANES, full_width - window), LANES)
    chunks = spaxels // chunk

    def cube_copy(i):
        lanes = pl.ds(i * chunk, chunk)
        return pltpu.make_async_copy(cube_ref.at[:, lanes], held_ref.at[:, lanes], cube_sem.at[i])

    window_copy = pltpu.make_async_copy(templates_ref.at[:, pl.ds(base, window)], window_ref, window_sem)

    small_copies = [
        pltpu.make_async_copy(bins_ref, bins_held_ref, small_sem.at[0]),
        pltpu.make_async_copy(owner_ref, owner_held_ref, small_sem.at[1]),
    ]

    @pl.when(pl.program_id(0) == 0)
    def _():
        for copy in small_copies:
            copy.start()
        for i in range(chunks):
            cube_copy(i).start()
        window_copy.start()
        for copy in small_copies:
            copy.wait()

    owner = owner_held_ref[:, pl.ds(pl.multiple_of(pl.program_id(0) * slots, LANES), slots)]
    owner = jnp.broadcast_to(owner, (SUB, slots)).T[:, :1]
    sums = jnp.zeros((slots, width), F32)
    counts = jnp.zeros((slots, LANES), F32)
    for i in range(chunks):
        here = owner == bins_held_ref[:, i * chunk : (i + 1) * chunk]
        ones = jnp.where(here, 1.0, 0.0)
        for lane in range(0, chunk, LANES):
            counts = counts + ones[:, lane : lane + LANES]
        member = ones.astype(BF16)

        @pl.when(pl.program_id(0) == 0)
        def _(i=i):
            cube_copy(i).wait()

        for part in split3(held_ref[:, i * chunk : (i + 1) * chunk]):
            sums = sums + dot(member, part, NT)
    means = sums / jnp.sum(counts, axis=1, keepdims=True)

    @pl.when(pl.program_id(0) == 0)
    def _():
        window_copy.wait()

    mine = pltpu.roll(window_ref[...], window - (first - base), 1)[:, :width]
    out_ref[...] = dot_f32(means, mine, NT) * (1.0 / full_width)


def project(device, bins, owner, cube, templates):
    width, spaxels = cube.shape
    slots = owner.shape[1]
    block = min(slots, 512)
    chunk = min(spaxels, 512)
    count, full_width = templates.shape
    return pl.pallas_call(
        functools.partial(project_kernel, chunk=chunk),
        grid=(slots // block,),
        in_specs=[
            pl.BlockSpec(memory_space=pltpu.SMEM),
            pl.BlockSpec(memory_space=pltpu.HBM),
            pl.BlockSpec(memory_space=pltpu.HBM),
            pl.BlockSpec(memory_space=pltpu.HBM),
            pl.BlockSpec(memory_space=pltpu.HBM),
        ],
        out_specs=pl.BlockSpec((block, count), lambda i: (i, 0)),
        out_shape=jax.ShapeDtypeStruct((slots, count), F32),
        scratch_shapes=[
            pltpu.VMEM((width, spaxels), F32),
            pltpu.VMEM((count, template_window(width, full_width)), F32),
            pltpu.VMEM(bins.shape, jnp.int32),
            pltpu.VMEM(owner.shape, jnp.int32),
            pltpu.SemaphoreType.DMA((spaxels // chunk,)),
            pltpu.SemaphoreType.DMA,
            pltpu.SemaphoreType.DMA((2,)),
        ],
        compiler_params=pltpu.CompilerParams(vmem_limit_bytes=VMEM_LIMIT),
        name="project",
    )(device, bins, owner, cube, templates)


def reciprocal(x):
    r = pl.reciprocal(x, approx=True)
    r = r * (2.0 - x * r)
    return r * (2.0 - x * r)


def invert_tile(tile):
    size = tile.shape[0]
    count = size // SUB
    lanes = lax.broadcasted_iota(jnp.int32, (SUB, size), 1)
    rows_at = lax.broadcasted_iota(jnp.int32, (SUB, size), 0)
    rows = [tile[i * SUB : (i + 1) * SUB, :] for i in range(count)]
    for k in range(count):
        block = rows[k]
        first = k * SUB
        a = {}
        for i in range(SUB):
            for j in range(i, SUB):
                a[i, j] = jnp.broadcast_to(block[i : i + 1, first + j : first + j + 1], (SUB, size))

        def at(i, j):
            return (i, j) if i <= j else (j, i)

        for p in range(0, SUB, 2):
            q = p + 1
            pp, pq, qq = a[p, p], a[p, q], a[q, q]
            inverse = reciprocal(pp * qq - pq * pq)
            others = [i for i in range(SUB) if i not in (p, q)]
            old = {i: (a[at(i, p)], a[at(i, q)]) for i in others}
            new = {
                i: ((u * qq - v * pq) * inverse, (v * pp - u * pq) * inverse) for i, (u, v) in old.items()
            }
            for i in others:
                for j in others:
                    if i <= j:
                        a[i, j] = a[i, j] - new[i][0] * old[j][0] - new[i][1] * old[j][1]
            for i in others:
                a[at(i, p)], a[at(i, q)] = new[i]
            a[p, p], a[p, q], a[q, q] = -(qq * inverse), pq * inverse, -(pp * inverse)
        columns = []
        for j in range(SUB):
            column = a[at(0, j)]
            for i in range(1, SUB):
                column = jnp.where(rows_at == i, a[at(i, j)], column)
            columns.append(column)
        terms = [columns[j] * jnp.broadcast_to(block[j : j + 1, :], (SUB, size)) for j in range(SUB)]
        while len(terms) > 1:
            terms = [x + y for x, y in zip(terms[::2], terms[1::2])]
        swept = -terms[0]
        for j in range(SUB):
            swept = jnp.where(lanes == first + j, columns[j], swept)
        inside = (lanes >= first) & (lanes < first + SUB)
        spread_rows = [jnp.broadcast_to(swept[j : j + 1, :], (SUB, size)) for j in range(SUB)]
        order = list(range(k + 1, count)) + list(range(k))
        for i in order:
            terms = [
                jnp.broadcast_to(rows[i][:, first + j : first + j + 1], (SUB, size)) * spread_rows[j]
                for j in range(SUB)
            ]
            while len(terms) > 1:
                terms = [x + y for x, y in zip(terms[::2], terms[1::2])]
            rows[i] = jnp.where(inside, 0.0, rows[i]) - terms[0]
        rows[k] = swept
    return -jnp.concatenate(rows, axis=0)


def gram_kernel(templates_ref, gram_ref, first_ref, scale_ref, held_ref, sem, *, chunk):
    count, full_width = templates_ref.shape

    def copy(i):
        lanes = pl.ds(i * chunk, chunk)
        return pltpu.make_async_copy(templates_ref.at[:, lanes], held_ref.at[:, lanes], sem.at[i])

    for i in range(full_width // chunk):
        copy(i).start()
    even = jnp.zeros((count, count), F32)
    mixed = jnp.zeros((count, count), F32)
    for i in range(full_width // chunk):
        copy(i).wait()
        hi, mid, low = split3(held_ref[:, i * chunk : (i + 1) * chunk])
        even = even + (dot(hi, hi, NT) + dot(mid, mid, NT))
        mixed = mixed + (dot(hi, mid, NT) + dot(hi, low, NT))
    gram = (even + (mixed + mixed.T)) * (1.0 / full_width)
    same = lax.broadcasted_iota(jnp.int32, gram.shape, 0) == lax.broadcasted_iota(jnp.int32, gram.shape, 1)
    diagonal = jnp.where(same, gram, 0.0)
    row = lax.rsqrt(jnp.sum(diagonal, axis=0, keepdims=True))
    column = lax.rsqrt(jnp.sum(diagonal, axis=1, keepdims=True))
    gram = gram * row * column
    scale_ref[...] = row
    gram_ref[...] = gram
    first_ref[...] = invert_tile(gram[:LANES, :LANES])


def gram_inverse(templates, chunk):
    count, full_width = templates.shape
    return pl.pallas_call(
        functools.partial(gram_kernel, chunk=chunk),
        in_specs=[pl.BlockSpec(memory_space=pltpu.HBM)],
        out_shape=(
            jax.ShapeDtypeStruct((count, count), F32),
            jax.ShapeDtypeStruct((LANES, LANES), F32),
            jax.ShapeDtypeStruct((1, count), F32),
        ),
        scratch_shapes=[
            pltpu.VMEM((count, full_width), F32),
            pltpu.SemaphoreType.DMA((full_width // chunk,)),
        ],
        compiler_params=pltpu.CompilerParams(vmem_limit_bytes=VMEM_LIMIT),
        name="gram",
    )(templates)


def finish_kernel(gram_ref, first_ref, scale_ref, out_ref):
    first = first_ref[...]
    side = gram_ref[:LANES, LANES:]
    half = dot_f32(first, side, NN)
    schur = gram_ref[LANES:, LANES:] - dot_f32(side.T, half, NN)
    last = invert_tile(schur)
    cross = dot_f32(half, last, NN)
    row = scale_ref[...]
    column = jnp.broadcast_to(row, (SUB, row.shape[1])).T[:, :1]
    near, far = row[:, :LANES], row[:, LANES:]
    out_ref[:LANES, :LANES] = (first + dot_f32(cross, half, NT)) * near * column[:LANES]
    out_ref[:LANES, LANES:] = -cross * far * column[:LANES]
    out_ref[LANES:, :LANES] = -cross.T * near * column[LANES:]
    out_ref[LANES:, LANES:] = last * far * column[LANES:]


def in_vmem(kernel, shapes, name, *arrays):
    return pl.pallas_call(
        kernel,
        out_shape=shapes,
        compiler_params=pltpu.CompilerParams(vmem_limit_bytes=VMEM_LIMIT),
        name=name,
    )(*arrays)


def window_sums(read, rows, first, begin, span):
    lines = begin.shape[0]
    sub = lax.broadcasted_iota(jnp.int32, (SUB, LANES), 0)
    spans = [jnp.broadcast_to(span[j : j + 1], (SUB, LANES)).astype(F32) for j in range(lines)]
    offsets = [
        (2 * (first + sub - jnp.broadcast_to(begin[j : j + 1], (SUB, LANES))) + 1).astype(F32) - spans[j]
        for j in range(lines)
    ]

    def add(block, shift, sums):
        size = block.shape[0]
        out = []
        for j in range(lines):
            m = offsets[j][:size] + shift
            masked = jnp.where(jnp.abs(m) < spans[j][:size], block, 0.0)
            weighted = masked * m
            out += [sums[3 * j] + masked, sums[3 * j + 1] + weighted, sums[3 * j + 2] + weighted * m]
        return out

    full = rows // SUB
    out = [jnp.zeros((1, LANES), F32)] * (3 * lines)
    if full:
        sums = [jnp.zeros((SUB, LANES), F32)] * (3 * lines)
        for i in range(full):
            sums = add(read(i * SUB, SUB), 2.0 * i * SUB, sums)
        out = [jnp.sum(x, axis=0, keepdims=True) for x in sums]
    if rows % SUB:
        sums = [jnp.zeros((rows % SUB, LANES), F32)] * (3 * lines)
        sums = add(read(full * SUB, rows % SUB), 2.0 * full * SUB, sums)
        out = [x + jnp.sum(y, axis=0, keepdims=True) for x, y in zip(out, sums)]
    return [out[3 * j + k] for k in range(3) for j in range(lines)]


def cube_kernel(
    device_ref, begin_ref, span_ref, cube_ref, same_ref, other_ref,
    begins_ref, spans_ref, held_ref, lines_sem, cube_sem,
):
    width = cube_ref.shape[0]
    owners = 2 * same_ref.shape[0]
    device = device_ref[0]

    def tile_copy(i):
        lanes = pl.ds(pl.multiple_of(i * LANES, LANES), LANES)
        return pltpu.make_async_copy(cube_ref.at[:, lanes], held_ref.at[i], cube_sem.at[i])

    line_copies = [
        pltpu.make_async_copy(begin_ref, begins_ref, lines_sem.at[0]),
        pltpu.make_async_copy(span_ref, spans_ref, lines_sem.at[1]),
    ]
    for copy in line_copies:
        copy.start()
    for i in range(owners):
        tile_copy(i).start()
    for copy in line_copies:
        copy.wait()

    def owner(i, carry):
        tile_copy(i).wait()
        lanes = pl.ds(pl.multiple_of(i * LANES, LANES), LANES)
        sums = window_sums(
            lambda row, size: held_ref[i, row : row + size, :],
            width,
            device * width,
            begins_ref[:, lanes],
            spans_ref[:, lanes],
        )
        value = jnp.concatenate(sums, axis=0)
        same = i % 2 == device % 2

        @pl.when(same)
        def _():
            same_ref[i // 2] = value

        @pl.when(jnp.logical_not(same))
        def _():
            other_ref[i // 2] = value

        return carry

    lax.fori_loop(0, owners, owner, 0)


def cube_windows(device, begin, span, cube, devices):
    hbm = pl.BlockSpec(memory_space=pltpu.HBM)
    width, spaxels = cube.shape
    half = jax.ShapeDtypeStruct((devices // 2, 3 * begin.shape[0], LANES), F32)
    return pl.pallas_call(
        cube_kernel,
        in_specs=[pl.BlockSpec(memory_space=pltpu.SMEM), hbm, hbm, hbm],
        out_shape=(half, half),
        scratch_shapes=[
            pltpu.VMEM(begin.shape, jnp.int32),
            pltpu.VMEM(span.shape, jnp.int32),
            pltpu.VMEM((devices, width, LANES), F32),
            pltpu.SemaphoreType.DMA((2,)),
            pltpu.SemaphoreType.DMA((devices,)),
        ],
        compiler_params=pltpu.CompilerParams(vmem_limit_bytes=VMEM_LIMIT),
        name="cube_windows",
    )(device, begin, span, cube)


def pack_kernel(received_ref, same_ref, other_ref, out_ref):
    total = received_ref[0]
    for i in range(1, received_ref.shape[0]):
        total = total + received_ref[i]
    slots, count = total.shape
    for half in range(count // LANES):
        value = total[:, half * LANES : (half + 1) * LANES]
        for i in range(out_ref.shape[0]):
            out_ref[i, half * slots : (half + 1) * slots, :] = value
    head = slots * (count // LANES)
    out_ref[:, head:, :] = same_ref[...] + other_ref[...]


def owner_kernel(
    device_ref, starts_ref, bins_ref, owner_ref, begin_ref, span_ref, near_ref, far_ref, inverse_ref, templates_ref,
    weights_ref, out_ref, held_ref, continuum_ref, bins_held_ref, owner_held_ref, sem, small_sem, *, chunk,
):
    chips = near_ref.shape[0]
    own_slots, count = weights_ref.shape
    halves = count // LANES
    head = own_slots * halves
    own = begin_ref.shape[1]
    lines = begin_ref.shape[0]
    full_width = templates_ref.shape[1]
    device = device_ref[0]

    def copy(i):
        lanes = pl.ds(i * chunk, chunk)
        return pltpu.make_async_copy(templates_ref.at[:, lanes], held_ref.at[:, lanes], sem.at[i])

    own_bins = bins_ref.at[:, pl.ds(pl.multiple_of(device * own, LANES), own)]
    small_copies = [
        pltpu.make_async_copy(own_bins, bins_held_ref, small_sem.at[0]),
        pltpu.make_async_copy(owner_ref, owner_held_ref, small_sem.at[1]),
    ]
    for small in small_copies:
        small.start()
    for i in range(full_width // chunk):
        copy(i).start()

    inverse = inverse_ref[...]
    chip, core = device // 2, device % 2
    mine = jnp.concatenate([near_ref[chip, h * own_slots : (h + 1) * own_slots, :] for h in range(halves)], axis=1)
    weights_ref[...] = dot_f32(mine, inverse, NN)

    for small in small_copies:
        small.wait()
    bins = jnp.broadcast_to(bins_held_ref[...], (SUB, own)).T[:, :1]
    member = jnp.where(bins == owner_held_ref[...], 1.0, 0.0).astype(BF16)
    picked = []
    for h in range(halves):
        rows = slice(h * own_slots, (h + 1) * own_slots)
        blocks = []
        for i in range(chips):
            near, far = near_ref[i, rows, :], far_ref[i, rows, :]
            blocks += [jnp.where(core == 0, near, far), jnp.where(core == 0, far, near)]
        hi, mid, low = split3(jnp.concatenate(blocks, axis=0))
        picked.append(dot(member, hi, NN) + (dot(member, mid, NN) + dot(member, low, NN)))
    spaxel_weights = dot_f32(jnp.concatenate(picked, axis=1), inverse, NN)

    hi, mid, low = split3(spaxel_weights)
    all_parts = jnp.concatenate([hi, mid, low], axis=0)
    for i in range(full_width // chunk):
        copy(i).wait()
        first, second, third = split3(held_ref[:, i * chunk : (i + 1) * chunk])
        by_first = dot(all_parts, first, NN)
        by_second = dot(all_parts[: 2 * own], second, NN)
        by_third = dot(hi, third, NN)
        value = by_first[:own] + (
            (by_first[own : 2 * own] + by_second[:own]) + (by_first[2 * own :] + by_second[own:] + by_third)
        )
        for t in range(chunk // LANES):
            continuum_ref[i * (chunk // LANES) + t] = value[:, t * LANES : (t + 1) * LANES]
    continuum_ref[full_width // LANES] = jnp.zeros((own, LANES), F32)

    begin = begin_ref[...]
    span = span_ref[...].astype(F32)
    centre = 2.0 * (begin & (LANES - 1)).astype(F32) + span - 1.0
    pad = jnp.zeros((LANES - 2 * lines, own), F32)
    columns = jnp.concatenate([centre, span, pad], axis=0).T
    lanes = lax.broadcasted_iota(jnp.int32, (SUB, LANES), 1)
    twice = (2 * lanes).astype(F32)
    rows_at = lax.broadcasted_iota(jnp.int32, (SUB, LANES), 0)
    at_row = [rows_at == r for r in range(SUB)]
    found = []
    for g in range(own // SUB):
        rows = slice(g * SUB, (g + 1) * SUB)
        result = jnp.zeros((SUB, LANES), F32)
        for j in range(lines):
            left = right = None
            for r in range(SUB):
                tile = lax.shift_right_logical(starts_ref[j, g * SUB + r], 7)
                a = continuum_ref[tile, rows, :]
                b = continuum_ref[tile + 1, rows, :]
                left = a if left is None else jnp.where(at_row[r], a, left)
                right = b if right is None else jnp.where(at_row[r], b, right)
            width = jnp.broadcast_to(columns[rows, lines + j : lines + j + 1], (SUB, LANES))
            m = twice - jnp.broadcast_to(columns[rows, j : j + 1], (SUB, LANES))
            n = m + 2.0 * LANES
            left = jnp.where(jnp.abs(m) < width, left, 0.0)
            right = jnp.where(jnp.abs(n) < width, right, 0.0)
            left_m = left * m
            right_n = right * n
            for k, term in enumerate((left + right, left_m + right_n, left_m * m + right_n * n)):
                total = jnp.sum(term, axis=1, keepdims=True)
                result = jnp.where(lanes == k * lines + j, total, result)
        found.append(result)
    continuum_sums = jnp.concatenate(found, axis=0).T[: 3 * lines, :]

    cube_sums = near_ref[0, head:, :]
    for i in range(1, chips):
        cube_sums = cube_sums + near_ref[i, head:, :]
    scale = jnp.concatenate([span, span * span, span * span * span], axis=0)
    out_ref[...] = (cube_sums - continuum_sums) / scale


def owned(device, bins, owner, begin, span, near, far, inverse, templates, own_slots, chunk):
    vmem = pl.BlockSpec(memory_space=pltpu.VMEM)
    smem = pl.BlockSpec(memory_space=pltpu.SMEM)
    hbm = pl.BlockSpec(memory_space=pltpu.HBM)
    own = begin.shape[1]
    count, full_width = templates.shape
    return pl.pallas_call(
        functools.partial(owner_kernel, chunk=chunk),
        in_specs=[smem, smem, hbm, hbm] + [vmem] * 5 + [hbm],
        out_shape=(
            jax.ShapeDtypeStruct((own_slots, count), F32),
            jax.ShapeDtypeStruct((3 * begin.shape[0], own), F32),
        ),
        scratch_shapes=[
            pltpu.VMEM((count, full_width), F32),
            pltpu.VMEM((full_width // LANES + 1, own, LANES), F32),
            pltpu.VMEM((1, own), jnp.int32),
            pltpu.VMEM(owner.shape, jnp.int32),
            pltpu.SemaphoreType.DMA((full_width // chunk,)),
            pltpu.SemaphoreType.DMA((2,)),
        ],
        compiler_params=pltpu.CompilerParams(vmem_limit_bytes=VMEM_LIMIT),
        name="owned",
    )(device, begin, bins, owner, begin, span, near, far, inverse, templates)


def shards(cube, templates, bin_id, owner_bins, line_start, line_width):
    devices = lax.axis_size("spax")
    device = lax.axis_index("spax")
    spaxels = cube.shape[0]
    total_bins = owner_bins.shape[0]
    count = templates.shape[0]
    own_spaxels = spaxels // devices
    own_slots = total_bins // devices
    here = device.reshape(1).astype(jnp.int32)
    templates = pltpu.with_memory_space_constraint(templates, pltpu.HBM)
    columns = pltpu.with_memory_space_constraint(cube.T, pltpu.HBM)
    begins = pltpu.with_memory_space_constraint(line_start, pltpu.HBM)
    spans = pltpu.with_memory_space_constraint(line_width, pltpu.HBM)
    bins = pltpu.with_memory_space_constraint(bin_id[None, :], pltpu.HBM)
    owner = pltpu.with_memory_space_constraint(owner_bins[None, :], pltpu.HBM)
    cores = [list(range(core, devices, 2)) for core in range(2)]
    swap = [(d, d ^ 1) for d in range(devices)]

    partial = project(here, bins, owner, columns, templates)
    partial, here_after = lax.optimization_barrier((partial, here))
    received = lax.all_to_all(partial.reshape(devices, own_slots, count), "spax", 0, 0)

    same, other = cube_windows(here_after, begins, spans, columns, devices)
    other = lax.ppermute(other, "spax", swap)
    gram, first, scale = gram_inverse(templates, 512)
    received, same, other, gram, first, scale = lax.optimization_barrier(
        (received, same, other, gram, first, scale)
    )
    head = own_slots * (count // LANES)
    parcel = in_vmem(
        pack_kernel,
        jax.ShapeDtypeStruct((devices // 2, head + same.shape[1], LANES), F32),
        "pack",
        received,
        same,
        other,
    )
    parcel, gram, first, scale = lax.optimization_barrier((parcel, gram, first, scale))
    near = lax.all_to_all(parcel, "spax", 0, 0, axis_index_groups=cores)
    inverse = in_vmem(finish_kernel, jax.ShapeDtypeStruct((count, count), F32), "finish", gram, first, scale)
    far = lax.ppermute(near, "spax", swap)

    own = lambda x: lax.dynamic_slice_in_dim(x, device * own_spaxels, own_spaxels, 1)
    return owned(here, bins, owner, own(line_start), own(line_width), near, far, inverse, templates, own_slots, 512)


def solution(mesh):
    placed = (
        P("strips", "spax"),
        P(),
        P("strips"),
        P("strips"),
        P(None, "strips"),
        P(None, "strips"),
    )
    return jax.shard_map(
        shards,
        mesh=mesh,
        in_specs=placed,
        out_specs=(P(("strips", "spax"), None), P(None, ("strips", "spax"))),
        check_vma=False,
    )
```

```python
import functools

import jax
import jax.numpy as jnp
from jax import lax
from jax.experimental import pallas as pl
from jax.experimental.pallas import tpu as pltpu
from jax.sharding import PartitionSpec as P

HIGHEST = lax.Precision.HIGHEST
F32 = jnp.float32
BF16 = jnp.bfloat16
LANES = 128
SUB = 8
VMEM_LIMIT = 20 * 1024 * 1024

NT = (((1,), (1,)), ((), ()))
NN = (((1,), (0,)), ((), ()))


def split3(x):
    hi = x.astype(BF16)
    rest = x - hi.astype(F32)
    mid = rest.astype(BF16)
    low = (rest - mid.astype(F32)).astype(BF16)
    return hi, mid, low


def dot(a, b, dims):
    return lax.dot_general(a, b, dims, preferred_element_type=F32)


def dot_f32(a, b, dims):
    return lax.dot_general(a, b, dims, precision=HIGHEST, preferred_element_type=F32)


def template_window(width, full_width):
    return min(full_width, -(-(width + LANES - 1) // LANES) * LANES)


def project_kernel(
    device_ref, bins_ref, owner_ref, cube_ref, templates_ref, out_ref,
    held_ref, window_ref, bins_held_ref, owner_held_ref, cube_sem, window_sem, small_sem, *, chunk,
):
    width, spaxels = cube_ref.shape
    slots = out_ref.shape[0]
    full_width = templates_ref.shape[1]
    first = device_ref[0] * width
    window = window_ref.shape[1]
    base = pl.multiple_of(jnp.minimum(first // LANES * LANES, full_width - window), LANES)
    chunks = spaxels // chunk

    def cube_copy(i):
        lanes = pl.ds(i * chunk, chunk)
        return pltpu.make_async_copy(cube_ref.at[:, lanes], held_ref.at[:, lanes], cube_sem.at[i])

    window_copy = pltpu.make_async_copy(templates_ref.at[:, pl.ds(base, window)], window_ref, window_sem)

    small_copies = [
        pltpu.make_async_copy(bins_ref, bins_held_ref, small_sem.at[0]),
        pltpu.make_async_copy(owner_ref, owner_held_ref, small_sem.at[1]),
    ]

    @pl.when(pl.program_id(0) == 0)
    def _():
        for copy in small_copies:
            copy.start()
        for i in range(chunks):
            cube_copy(i).start()
        window_copy.start()
        for copy in small_copies:
            copy.wait()

    owner = owner_held_ref[:, pl.ds(pl.multiple_of(pl.program_id(0) * slots, LANES), slots)]
    owner = jnp.broadcast_to(owner, (SUB, slots)).T[:, :1]
    sums = jnp.zeros((slots, width), F32)
    counts = jnp.zeros((slots, LANES), F32)
    for i in range(chunks):
        here = owner == bins_held_ref[:, i * chunk : (i + 1) * chunk]
        ones = jnp.where(here, 1.0, 0.0)
        for lane in range(0, chunk, LANES):
            counts = counts + ones[:, lane : lane + LANES]
        member = ones.astype(BF16)

        @pl.when(pl.program_id(0) == 0)
        def _(i=i):
            cube_copy(i).wait()

        for part in split3(held_ref[:, i * chunk : (i + 1) * chunk]):
            sums = sums + dot(member, part, NT)
    means = sums / jnp.sum(counts, axis=1, keepdims=True)

    @pl.when(pl.program_id(0) == 0)
    def _():
        window_copy.wait()

    mine = pltpu.roll(window_ref[...], window - (first - base), 1)[:, :width]
    out_ref[...] = dot_f32(means, mine, NT) * (1.0 / full_width)


def project(device, bins, owner, cube, templates):
    width, spaxels = cube.shape
    slots = owner.shape[1]
    block = min(slots, 512)
    chunk = min(spaxels, 512)
    count, full_width = templates.shape
    return pl.pallas_call(
        functools.partial(project_kernel, chunk=chunk),
        grid=(slots // block,),
        in_specs=[
            pl.BlockSpec(memory_space=pltpu.SMEM),
            pl.BlockSpec(memory_space=pltpu.HBM),
            pl.BlockSpec(memory_space=pltpu.HBM),
            pl.BlockSpec(memory_space=pltpu.HBM),
            pl.BlockSpec(memory_space=pltpu.HBM),
        ],
        out_specs=pl.BlockSpec((block, count), lambda i: (i, 0)),
        out_shape=jax.ShapeDtypeStruct((slots, count), F32),
        scratch_shapes=[
            pltpu.VMEM((width, spaxels), F32),
            pltpu.VMEM((count, template_window(width, full_width)), F32),
            pltpu.VMEM(bins.shape, jnp.int32),
            pltpu.VMEM(owner.shape, jnp.int32),
            pltpu.SemaphoreType.DMA((spaxels // chunk,)),
            pltpu.SemaphoreType.DMA,
            pltpu.SemaphoreType.DMA((2,)),
        ],
        compiler_params=pltpu.CompilerParams(vmem_limit_bytes=VMEM_LIMIT),
        name="project",
    )(device, bins, owner, cube, templates)


def reciprocal(x):
    r = pl.reciprocal(x, approx=True)
    r = r * (2.0 - x * r)
    return r * (2.0 - x * r)


def invert_tile(tile):
    size = tile.shape[0]
    count = size // SUB
    lanes = lax.broadcasted_iota(jnp.int32, (SUB, size), 1)
    rows_at = lax.broadcasted_iota(jnp.int32, (SUB, size), 0)
    rows = [tile[i * SUB : (i + 1) * SUB, :] for i in range(count)]
    for k in range(count):
        block = rows[k]
        first = k * SUB
        a = {}
        for i in range(SUB):
            for j in range(i, SUB):
                a[i, j] = jnp.broadcast_to(block[i : i + 1, first + j : first + j + 1], (SUB, size))

        def at(i, j):
            return (i, j) if i <= j else (j, i)

        for p in range(0, SUB, 2):
            q = p + 1
            pp, pq, qq = a[p, p], a[p, q], a[q, q]
            inverse = reciprocal(pp * qq - pq * pq)
            others = [i for i in range(SUB) if i not in (p, q)]
            old = {i: (a[at(i, p)], a[at(i, q)]) for i in others}
            new = {
                i: ((u * qq - v * pq) * inverse, (v * pp - u * pq) * inverse) for i, (u, v) in old.items()
            }
            for i in others:
                for j in others:
                    if i <= j:
                        a[i, j] = a[i, j] - new[i][0] * old[j][0] - new[i][1] * old[j][1]
            for i in others:
                a[at(i, p)], a[at(i, q)] = new[i]
            a[p, p], a[p, q], a[q, q] = -(qq * inverse), pq * inverse, -(pp * inverse)
        columns = []
        for j in range(SUB):
            column = a[at(0, j)]
            for i in range(1, SUB):
                column = jnp.where(rows_at == i, a[at(i, j)], column)
            columns.append(column)
        terms = [columns[j] * jnp.broadcast_to(block[j : j + 1, :], (SUB, size)) for j in range(SUB)]
        while len(terms) > 1:
            terms = [x + y for x, y in zip(terms[::2], terms[1::2])]
        swept = -terms[0]
        for j in range(SUB):
            swept = jnp.where(lanes == first + j, columns[j], swept)
        inside = (lanes >= first) & (lanes < first + SUB)
        spread_rows = [jnp.broadcast_to(swept[j : j + 1, :], (SUB, size)) for j in range(SUB)]
        order = list(range(k + 1, count)) + list(range(k))
        for i in order:
            terms = [
                jnp.broadcast_to(rows[i][:, first + j : first + j + 1], (SUB, size)) * spread_rows[j]
                for j in range(SUB)
            ]
            while len(terms) > 1:
                terms = [x + y for x, y in zip(terms[::2], terms[1::2])]
            rows[i] = jnp.where(inside, 0.0, rows[i]) - terms[0]
        rows[k] = swept
    return -jnp.concatenate(rows, axis=0)


def gram_kernel(templates_ref, gram_ref, scale_ref, held_ref, sem, *, chunk):
    count, full_width = templates_ref.shape

    def copy(i):
        lanes = pl.ds(i * chunk, chunk)
        return pltpu.make_async_copy(templates_ref.at[:, lanes], held_ref.at[:, lanes], sem.at[i])

    for i in range(full_width // chunk):
        copy(i).start()
    even = jnp.zeros((count, count), F32)
    mixed = jnp.zeros((count, count), F32)
    for i in range(full_width // chunk):
        copy(i).wait()
        hi, mid, low = split3(held_ref[:, i * chunk : (i + 1) * chunk])
        even = even + (dot(hi, hi, NT) + dot(mid, mid, NT))
        mixed = mixed + (dot(hi, mid, NT) + dot(hi, low, NT))
    gram = (even + (mixed + mixed.T)) * (1.0 / full_width)
    same = lax.broadcasted_iota(jnp.int32, gram.shape, 0) == lax.broadcasted_iota(jnp.int32, gram.shape, 1)
    diagonal = jnp.where(same, gram, 0.0)
    row = lax.rsqrt(jnp.sum(diagonal, axis=0, keepdims=True))
    column = lax.rsqrt(jnp.sum(diagonal, axis=1, keepdims=True))
    gram = gram * row * column
    scale_ref[...] = row
    gram_ref[...] = gram


def scaled_gram(templates, chunk):
    count, full_width = templates.shape
    return pl.pallas_call(
        functools.partial(gram_kernel, chunk=chunk),
        in_specs=[pl.BlockSpec(memory_space=pltpu.HBM)],
        out_shape=(
            jax.ShapeDtypeStruct((count, count), F32),
            jax.ShapeDtypeStruct((1, count), F32),
        ),
        scratch_shapes=[
            pltpu.VMEM((count, full_width), F32),
            pltpu.SemaphoreType.DMA((full_width // chunk,)),
        ],
        compiler_params=pltpu.CompilerParams(vmem_limit_bytes=VMEM_LIMIT),
        name="gram",
    )(templates)


def invert_kernel(gram_ref, scale_ref, out_ref):
    first = invert_tile(gram_ref[:LANES, :LANES])
    side = gram_ref[:LANES, LANES:]
    half = dot_f32(first, side, NN)
    schur = gram_ref[LANES:, LANES:] - dot_f32(side.T, half, NN)
    last = invert_tile(schur)
    cross = dot_f32(half, last, NN)
    row = scale_ref[...]
    column = jnp.broadcast_to(row, (SUB, row.shape[1])).T[:, :1]
    near, far = row[:, :LANES], row[:, LANES:]
    out_ref[:LANES, :LANES] = (first + dot_f32(cross, half, NT)) * near * column[:LANES]
    out_ref[:LANES, LANES:] = -cross * far * column[:LANES]
    out_ref[LANES:, :LANES] = -cross.T * near * column[LANES:]
    out_ref[LANES:, LANES:] = last * far * column[LANES:]


def in_vmem(kernel, shapes, name, *arrays):
    return pl.pallas_call(
        kernel,
        out_shape=shapes,
        compiler_params=pltpu.CompilerParams(vmem_limit_bytes=VMEM_LIMIT),
        name=name,
    )(*arrays)


def window_sums(read, rows, first, begin, span):
    lines = begin.shape[0]
    sub = lax.broadcasted_iota(jnp.int32, (SUB, LANES), 0)
    spans = [jnp.broadcast_to(span[j : j + 1], (SUB, LANES)).astype(F32) for j in range(lines)]
    offsets = [
        (2 * (first + sub - jnp.broadcast_to(begin[j : j + 1], (SUB, LANES))) + 1).astype(F32) - spans[j]
        for j in range(lines)
    ]

    def add(block, shift, sums):
        size = block.shape[0]
        out = []
        for j in range(lines):
            m = offsets[j][:size] + shift
            masked = jnp.where(jnp.abs(m) < spans[j][:size], block, 0.0)
            weighted = masked * m
            out += [sums[3 * j] + masked, sums[3 * j + 1] + weighted, sums[3 * j + 2] + weighted * m]
        return out

    full = rows // SUB
    out = [jnp.zeros((1, LANES), F32)] * (3 * lines)
    if full:
        sums = [jnp.zeros((SUB, LANES), F32)] * (3 * lines)
        for i in range(full):
            sums = add(read(i * SUB, SUB), 2.0 * i * SUB, sums)
        out = [jnp.sum(x, axis=0, keepdims=True) for x in sums]
    if rows % SUB:
        sums = [jnp.zeros((rows % SUB, LANES), F32)] * (3 * lines)
        sums = add(read(full * SUB, rows % SUB), 2.0 * full * SUB, sums)
        out = [x + jnp.sum(y, axis=0, keepdims=True) for x, y in zip(out, sums)]
    return [out[3 * j + k] for k in range(3) for j in range(lines)]


def cube_kernel(
    device_ref, begin_ref, span_ref, cube_ref, out_ref, begins_ref, spans_ref, held_ref, lines_sem, cube_sem,
):
    width = cube_ref.shape[0]
    owners = out_ref.shape[0]
    device = device_ref[0]

    def tile_copy(i):
        lanes = pl.ds(pl.multiple_of(i * LANES, LANES), LANES)
        return pltpu.make_async_copy(cube_ref.at[:, lanes], held_ref.at[i], cube_sem.at[i])

    line_copies = [
        pltpu.make_async_copy(begin_ref, begins_ref, lines_sem.at[0]),
        pltpu.make_async_copy(span_ref, spans_ref, lines_sem.at[1]),
    ]
    for copy in line_copies:
        copy.start()
    for i in range(owners):
        tile_copy(i).start()
    for copy in line_copies:
        copy.wait()

    def owner(i, carry):
        tile_copy(i).wait()
        lanes = pl.ds(pl.multiple_of(i * LANES, LANES), LANES)
        sums = window_sums(
            lambda row, size: held_ref[i, row : row + size, :],
            width,
            device * width,
            begins_ref[:, lanes],
            spans_ref[:, lanes],
        )
        for r, value in enumerate(sums):
            out_ref[i, r : r + 1, :] = value
        return carry

    lax.fori_loop(0, owners, owner, 0)


def cube_windows(device, begin, span, cube, devices):
    hbm = pl.BlockSpec(memory_space=pltpu.HBM)
    return pl.pallas_call(
        cube_kernel,
        in_specs=[pl.BlockSpec(memory_space=pltpu.SMEM), hbm, hbm, hbm],
        out_shape=jax.ShapeDtypeStruct((devices, 3 * begin.shape[0], LANES), F32),
        scratch_shapes=[
            pltpu.VMEM(begin.shape, jnp.int32),
            pltpu.VMEM(span.shape, jnp.int32),
            pltpu.VMEM((devices, cube.shape[0], LANES), F32),
            pltpu.SemaphoreType.DMA((2,)),
            pltpu.SemaphoreType.DMA((devices,)),
        ],
        compiler_params=pltpu.CompilerParams(vmem_limit_bytes=VMEM_LIMIT),
        name="cube_windows",
    )(device, begin, span, cube)


def pack_kernel(received_ref, sums_ref, out_ref):
    total = received_ref[0]
    for i in range(1, received_ref.shape[0]):
        total = total + received_ref[i]
    slots = total.shape[0]
    for i in range(out_ref.shape[0]):
        half = i % 2
        out_ref[i, :slots, :] = total[:, half * LANES : (half + 1) * LANES]
    out_ref[:, slots:, :] = sums_ref[...]


def owner_kernel(
    device_ref, bins_ref, owner_ref, begin_ref, span_ref, near_ref, far_ref, inverse_ref, templates_ref,
    weights_ref, out_ref,
    held_ref, continuum_ref, bins_held_ref, owner_held_ref, begins_ref, spans_ref, starts_ref, sem, small_sem,
    *, chunk,
):
    devices = near_ref.shape[0]
    slots = weights_ref.shape[0]
    own = bins_held_ref.shape[1]
    lines = begin_ref.shape[0]
    full_width = templates_ref.shape[1]
    device = device_ref[0]
    own_lanes = pl.ds(pl.multiple_of(device * own, LANES), own)

    def copy(i):
        lanes = pl.ds(i * chunk, chunk)
        return pltpu.make_async_copy(templates_ref.at[:, lanes], held_ref.at[:, lanes], sem.at[i])

    small_copies = [
        pltpu.make_async_copy(bins_ref.at[:, own_lanes], bins_held_ref, small_sem.at[0]),
        pltpu.make_async_copy(owner_ref, owner_held_ref, small_sem.at[1]),
        pltpu.make_async_copy(begin_ref.at[:, own_lanes], begins_ref, small_sem.at[2]),
        pltpu.make_async_copy(span_ref.at[:, own_lanes], spans_ref, small_sem.at[3]),
        pltpu.make_async_copy(begin_ref.at[:, own_lanes], starts_ref, small_sem.at[4]),
    ]
    for small in small_copies:
        small.start()
    for i in range(full_width // chunk):
        copy(i).start()

    inverse = inverse_ref[...]
    low_first = device % 2 == 0

    def halves(near, far):
        return jnp.where(low_first, near, far), jnp.where(low_first, far, near)

    mine = jnp.concatenate(halves(near_ref[device, :slots, :], far_ref[device, :slots, :]), axis=1)
    weights_ref[...] = dot_f32(mine, inverse, NN)

    for small in small_copies:
        small.wait()
    bins = jnp.broadcast_to(bins_held_ref[...], (SUB, own)).T[:, :1]
    member = jnp.where(bins == owner_held_ref[...], 1.0, 0.0).astype(BF16)
    picked = []
    for half in (near_ref, far_ref):
        hi, mid, low = split3(half[:, :slots, :].reshape(devices * slots, LANES))
        picked.append(dot(member, hi, NN) + (dot(member, mid, NN) + dot(member, low, NN)))
    spaxel_weights = dot_f32(jnp.concatenate(halves(*picked), axis=1), inverse, NN)

    for i in range(full_width // chunk):
        copy(i).wait()
        value = dot_f32(spaxel_weights, held_ref[:, i * chunk : (i + 1) * chunk], NN)
        for t in range(chunk // LANES):
            continuum_ref[i * (chunk // LANES) + t] = value[:, t * LANES : (t + 1) * LANES]
    continuum_ref[full_width // LANES] = jnp.zeros((own, LANES), F32)

    begin = begins_ref[...]
    span = spans_ref[...].astype(F32)
    centre = 2.0 * (begin & (LANES - 1)).astype(F32) + span - 1.0
    rows_at = lax.broadcasted_iota(jnp.int32, (SUB, LANES), 0)
    at_row = [rows_at == r for r in range(SUB)]
    twice = 2.0 * lax.broadcasted_iota(jnp.int32, (LANES, own), 0).astype(F32)
    sums = [None] * (3 * lines)
    for j in range(lines):
        picks = ([], [])
        for g in range(own // SUB):
            rows = slice(g * SUB, (g + 1) * SUB)
            left = right = None
            for r in range(SUB):
                tile = lax.shift_right_logical(starts_ref[j, g * SUB + r], 7)
                a = continuum_ref[tile, rows, :]
                b = continuum_ref[tile + 1, rows, :]
                left = a if left is None else jnp.where(at_row[r], a, left)
                right = b if right is None else jnp.where(at_row[r], b, right)
            picks[0].append(left)
            picks[1].append(right)
        terms = None
        for side in range(2):
            block = jnp.concatenate(picks[side], axis=0).T
            m = twice + (2.0 * LANES * side - centre[j : j + 1])
            masked = jnp.where(jnp.abs(m) < span[j : j + 1], block, 0.0)
            weighted = masked * m
            new = [masked, weighted, weighted * m]
            terms = new if terms is None else [x + y for x, y in zip(terms, new)]
        for k in range(3):
            sums[k * lines + j] = jnp.sum(terms[k], axis=0, keepdims=True)
    continuum_sums = jnp.concatenate(sums, axis=0)

    cube_sums = near_ref[0, slots:, :]
    for i in range(1, devices):
        cube_sums = cube_sums + near_ref[i, slots:, :]
    scale = jnp.concatenate([span, span * span, span * span * span], axis=0)
    out_ref[...] = (cube_sums - continuum_sums) / scale


def owned(device, bins, owner, begin, span, near, far, inverse, templates, own_slots, own, chunk):
    vmem = pl.BlockSpec(memory_space=pltpu.VMEM)
    hbm = pl.BlockSpec(memory_space=pltpu.HBM)
    count, full_width = templates.shape
    lines = begin.shape[0]
    return pl.pallas_call(
        functools.partial(owner_kernel, chunk=chunk),
        in_specs=[pl.BlockSpec(memory_space=pltpu.SMEM)] + [hbm] * 4 + [vmem] * 3 + [hbm],
        out_shape=(
            jax.ShapeDtypeStruct((own_slots, count), F32),
            jax.ShapeDtypeStruct((3 * lines, own), F32),
        ),
        scratch_shapes=[
            pltpu.VMEM((count, full_width), F32),
            pltpu.VMEM((full_width // LANES + 1, own, LANES), F32),
            pltpu.VMEM((1, own), jnp.int32),
            pltpu.VMEM(owner.shape, jnp.int32),
            pltpu.VMEM((lines, own), jnp.int32),
            pltpu.VMEM((lines, own), jnp.int32),
            pltpu.SMEM((lines, own), jnp.int32),
            pltpu.SemaphoreType.DMA((full_width // chunk,)),
            pltpu.SemaphoreType.DMA((5,)),
        ],
        compiler_params=pltpu.CompilerParams(vmem_limit_bytes=VMEM_LIMIT),
        name="owned",
    )(device, bins, owner, begin, span, near, far, inverse, templates)


def shards(cube, templates, bin_id, owner_bins, line_start, line_width):
    devices = lax.axis_size("spax")
    device = lax.axis_index("spax")
    spaxels = cube.shape[0]
    total_bins = owner_bins.shape[0]
    count = templates.shape[0]
    own_spaxels = spaxels // devices
    own_slots = total_bins // devices
    here = device.reshape(1).astype(jnp.int32)
    pin = lambda x: pltpu.with_memory_space_constraint(x, pltpu.HBM)
    templates, columns = pin(templates), pin(cube.T)
    begin, span = pin(line_start), pin(line_width)
    bins, owner = pin(bin_id[None, :]), pin(owner_bins[None, :])

    partial = project(here, bins, owner, columns, templates)
    partial, here_after = lax.optimization_barrier((partial, here))
    received = lax.all_to_all(partial.reshape(devices, own_slots, count), "spax", 0, 0)

    sums = cube_windows(here_after, begin, span, columns, devices)
    gram, scale = scaled_gram(templates, 512)
    received, sums, gram, scale = lax.optimization_barrier((received, sums, gram, scale))
    parcel = in_vmem(
        pack_kernel,
        jax.ShapeDtypeStruct((devices, own_slots + sums.shape[1], LANES), F32),
        "pack",
        received,
        sums,
    )
    parcel, gram, scale = lax.optimization_barrier((parcel, gram, scale))
    near = lax.all_to_all(parcel, "spax", 0, 0)
    inverse = in_vmem(invert_kernel, jax.ShapeDtypeStruct((count, count), F32), "invert", gram, scale)
    far = lax.ppermute(near, "spax", [(d, d ^ 1) for d in range(devices)])
    return owned(
        here, bins, owner, begin, span, near, far, inverse, templates, own_slots, own_spaxels, 512
    )


def solution(mesh):
    placed = (
        P("strips", "spax"),
        P(),
        P("strips"),
        P("strips"),
        P(None, "strips"),
        P(None, "strips"),
    )
    return jax.shard_map(
        shards,
        mesh=mesh,
        in_specs=placed,
        out_specs=(P(("strips", "spax"), None), P(None, ("strips", "spax"))),
        check_vma=False,
    )
```

```python
import functools

import jax
import jax.numpy as jnp
from jax import lax
from jax.experimental import pallas as pl
from jax.experimental.pallas import tpu as pltpu
from jax.sharding import PartitionSpec as P

HIGHEST = lax.Precision.HIGHEST
F32 = jnp.float32
BF16 = jnp.bfloat16
LANES = 128
SUB = 8
VMEM_LIMIT = 20 * 1024 * 1024

NT = (((1,), (1,)), ((), ()))
NN = (((1,), (0,)), ((), ()))


def split3(x):
    hi = x.astype(BF16)
    rest = x - hi.astype(F32)
    mid = rest.astype(BF16)
    low = (rest - mid.astype(F32)).astype(BF16)
    return hi, mid, low


def dot(a, b, dims):
    return lax.dot_general(a, b, dims, preferred_element_type=F32)


def dot_f32(a, b, dims):
    return lax.dot_general(a, b, dims, precision=HIGHEST, preferred_element_type=F32)


def template_window(width, full_width):
    return min(full_width, -(-(width + LANES - 1) // LANES) * LANES)


def project_kernel(
    device_ref, bins_ref, owner_ref, cube_ref, templates_ref, keep_ref, send_ref,
    held_ref, window_ref, bins_held_ref, owner_held_ref, cube_sem, window_sem, small_sem, *, chunk,
):
    width, spaxels = cube_ref.shape
    slots = keep_ref.shape[0]
    full_width = templates_ref.shape[1]
    first = device_ref[0] * width
    window = window_ref.shape[1]
    base = pl.multiple_of(jnp.minimum(first // LANES * LANES, full_width - window), LANES)
    chunks = spaxels // chunk

    def cube_copy(i):
        lanes = pl.ds(i * chunk, chunk)
        return pltpu.make_async_copy(cube_ref.at[:, lanes], held_ref.at[:, lanes], cube_sem.at[i])

    window_copy = pltpu.make_async_copy(templates_ref.at[:, pl.ds(base, window)], window_ref, window_sem)

    small_copies = [
        pltpu.make_async_copy(bins_ref, bins_held_ref, small_sem.at[0]),
        pltpu.make_async_copy(owner_ref, owner_held_ref, small_sem.at[1]),
    ]

    @pl.when(pl.program_id(0) == 0)
    def _():
        for copy in small_copies:
            copy.start()
        for i in range(chunks):
            cube_copy(i).start()
        window_copy.start()
        for copy in small_copies:
            copy.wait()

    owner = owner_held_ref[:, pl.ds(pl.multiple_of(pl.program_id(0) * slots, LANES), slots)]
    owner = jnp.broadcast_to(owner, (SUB, slots)).T[:, :1]
    sums = jnp.zeros((slots, width), F32)
    counts = jnp.zeros((slots, LANES), F32)
    for i in range(chunks):
        here = owner == bins_held_ref[:, i * chunk : (i + 1) * chunk]
        ones = jnp.where(here, 1.0, 0.0)
        for lane in range(0, chunk, LANES):
            counts = counts + ones[:, lane : lane + LANES]
        member = ones.astype(BF16)

        @pl.when(pl.program_id(0) == 0)
        def _(i=i):
            cube_copy(i).wait()

        for part in split3(held_ref[:, i * chunk : (i + 1) * chunk]):
            sums = sums + dot(member, part, NT)
    means = sums / jnp.sum(counts, axis=1, keepdims=True)

    @pl.when(pl.program_id(0) == 0)
    def _():
        window_copy.wait()

    mine = pltpu.roll(window_ref[...], window - (first - base), 1)[:, :width]
    projections = dot_f32(means, mine, NT) * (1.0 / full_width)
    low, high = projections[:, :LANES], projections[:, LANES:]
    low_kept = device_ref[0] % 2 == 0
    keep_ref[...] = jnp.where(low_kept, low, high)
    send_ref[...] = jnp.where(low_kept, high, low)


def project(device, bins, owner, cube, templates):
    width, spaxels = cube.shape
    slots = owner.shape[1]
    block = min(slots, 512)
    chunk = min(spaxels, 512)
    count, full_width = templates.shape
    return pl.pallas_call(
        functools.partial(project_kernel, chunk=chunk),
        grid=(slots // block,),
        in_specs=[
            pl.BlockSpec(memory_space=pltpu.SMEM),
            pl.BlockSpec(memory_space=pltpu.HBM),
            pl.BlockSpec(memory_space=pltpu.HBM),
            pl.BlockSpec(memory_space=pltpu.HBM),
            pl.BlockSpec(memory_space=pltpu.HBM),
        ],
        out_specs=[pl.BlockSpec((block, LANES), lambda i: (i, 0))] * 2,
        out_shape=[jax.ShapeDtypeStruct((slots, LANES), F32)] * 2,
        scratch_shapes=[
            pltpu.VMEM((width, spaxels), F32),
            pltpu.VMEM((count, template_window(width, full_width)), F32),
            pltpu.VMEM(bins.shape, jnp.int32),
            pltpu.VMEM(owner.shape, jnp.int32),
            pltpu.SemaphoreType.DMA((spaxels // chunk,)),
            pltpu.SemaphoreType.DMA,
            pltpu.SemaphoreType.DMA((2,)),
        ],
        compiler_params=pltpu.CompilerParams(vmem_limit_bytes=VMEM_LIMIT),
        name="project",
    )(device, bins, owner, cube, templates)


def reciprocal(x):
    r = pl.reciprocal(x, approx=True)
    r = r * (2.0 - x * r)
    return r * (2.0 - x * r)


def invert_tile(tile):
    size = tile.shape[0]
    count = size // SUB
    lanes = lax.broadcasted_iota(jnp.int32, (SUB, size), 1)
    rows_at = lax.broadcasted_iota(jnp.int32, (SUB, size), 0)
    rows = [tile[i * SUB : (i + 1) * SUB, :] for i in range(count)]
    for k in range(count):
        block = rows[k]
        first = k * SUB
        a = {}
        for i in range(SUB):
            for j in range(i, SUB):
                a[i, j] = jnp.broadcast_to(block[i : i + 1, first + j : first + j + 1], (SUB, size))

        def at(i, j):
            return (i, j) if i <= j else (j, i)

        for p in range(0, SUB, 2):
            q = p + 1
            pp, pq, qq = a[p, p], a[p, q], a[q, q]
            inverse = reciprocal(pp * qq - pq * pq)
            others = [i for i in range(SUB) if i not in (p, q)]
            old = {i: (a[at(i, p)], a[at(i, q)]) for i in others}
            new = {
                i: ((u * qq - v * pq) * inverse, (v * pp - u * pq) * inverse) for i, (u, v) in old.items()
            }
            for i in others:
                for j in others:
                    if i <= j:
                        a[i, j] = a[i, j] - new[i][0] * old[j][0] - new[i][1] * old[j][1]
            for i in others:
                a[at(i, p)], a[at(i, q)] = new[i]
            a[p, p], a[p, q], a[q, q] = -(qq * inverse), pq * inverse, -(pp * inverse)
        columns = []
        for j in range(SUB):
            column = a[at(0, j)]
            for i in range(1, SUB):
                column = jnp.where(rows_at == i, a[at(i, j)], column)
            columns.append(column)
        terms = [columns[j] * jnp.broadcast_to(block[j : j + 1, :], (SUB, size)) for j in range(SUB)]
        while len(terms) > 1:
            terms = [x + y for x, y in zip(terms[::2], terms[1::2])]
        swept = -terms[0]
        for j in range(SUB):
            swept = jnp.where(lanes == first + j, columns[j], swept)
        inside = (lanes >= first) & (lanes < first + SUB)
        spread_rows = [jnp.broadcast_to(swept[j : j + 1, :], (SUB, size)) for j in range(SUB)]
        order = list(range(k + 1, count)) + list(range(k))
        for i in order:
            terms = [
                jnp.broadcast_to(rows[i][:, first + j : first + j + 1], (SUB, size)) * spread_rows[j]
                for j in range(SUB)
            ]
            while len(terms) > 1:
                terms = [x + y for x, y in zip(terms[::2], terms[1::2])]
            rows[i] = jnp.where(inside, 0.0, rows[i]) - terms[0]
        rows[k] = swept
    return -jnp.concatenate(rows, axis=0)


def gram_kernel(templates_ref, gram_ref, scale_ref, held_ref, sem, *, chunk):
    count, full_width = templates_ref.shape

    def copy(i):
        lanes = pl.ds(i * chunk, chunk)
        return pltpu.make_async_copy(templates_ref.at[:, lanes], held_ref.at[:, lanes], sem.at[i])

    for i in range(full_width // chunk):
        copy(i).start()
    even = jnp.zeros((count, count), F32)
    mixed = jnp.zeros((count, count), F32)
    for i in range(full_width // chunk):
        copy(i).wait()
        hi, mid, low = split3(held_ref[:, i * chunk : (i + 1) * chunk])
        even = even + (dot(hi, hi, NT) + dot(mid, mid, NT))
        mixed = mixed + (dot(hi, mid, NT) + dot(hi, low, NT))
    gram = (even + (mixed + mixed.T)) * (1.0 / full_width)
    same = lax.broadcasted_iota(jnp.int32, gram.shape, 0) == lax.broadcasted_iota(jnp.int32, gram.shape, 1)
    diagonal = jnp.where(same, gram, 0.0)
    row = lax.rsqrt(jnp.sum(diagonal, axis=0, keepdims=True))
    column = lax.rsqrt(jnp.sum(diagonal, axis=1, keepdims=True))
    gram = gram * row * column
    scale_ref[...] = row
    gram_ref[...] = gram


def scaled_gram(templates, chunk):
    count, full_width = templates.shape
    return pl.pallas_call(
        functools.partial(gram_kernel, chunk=chunk),
        in_specs=[pl.BlockSpec(memory_space=pltpu.HBM)],
        out_shape=(
            jax.ShapeDtypeStruct((count, count), F32),
            jax.ShapeDtypeStruct((1, count), F32),
        ),
        scratch_shapes=[
            pltpu.VMEM((count, full_width), F32),
            pltpu.SemaphoreType.DMA((full_width // chunk,)),
        ],
        compiler_params=pltpu.CompilerParams(vmem_limit_bytes=VMEM_LIMIT),
        name="gram",
    )(templates)


def invert_kernel(gram_ref, scale_ref, out_ref):
    first = invert_tile(gram_ref[:LANES, :LANES])
    side = gram_ref[:LANES, LANES:]
    half = dot_f32(first, side, NN)
    schur = gram_ref[LANES:, LANES:] - dot_f32(side.T, half, NN)
    last = invert_tile(schur)
    cross = dot_f32(half, last, NN)
    row = scale_ref[...]
    column = jnp.broadcast_to(row, (SUB, row.shape[1])).T[:, :1]
    near, far = row[:, :LANES], row[:, LANES:]
    out_ref[:LANES, :LANES] = (first + dot_f32(cross, half, NT)) * near * column[:LANES]
    out_ref[:LANES, LANES:] = -cross * far * column[:LANES]
    out_ref[LANES:, :LANES] = -cross.T * near * column[LANES:]
    out_ref[LANES:, LANES:] = last * far * column[LANES:]


def in_vmem(kernel, shapes, name, *arrays):
    return pl.pallas_call(
        kernel,
        out_shape=shapes,
        compiler_params=pltpu.CompilerParams(vmem_limit_bytes=VMEM_LIMIT),
        name=name,
    )(*arrays)


def window_sums(read, rows, first, begin, span):
    lines = begin.shape[0]
    sub = lax.broadcasted_iota(jnp.int32, (SUB, LANES), 0)
    spans = [jnp.broadcast_to(span[j : j + 1], (SUB, LANES)).astype(F32) for j in range(lines)]
    offsets = [
        (2 * (first + sub - jnp.broadcast_to(begin[j : j + 1], (SUB, LANES))) + 1).astype(F32) - spans[j]
        for j in range(lines)
    ]

    def add(block, shift, sums):
        size = block.shape[0]
        out = []
        for j in range(lines):
            m = offsets[j][:size] + shift
            masked = jnp.where(jnp.abs(m) < spans[j][:size], block, 0.0)
            weighted = masked * m
            out += [sums[3 * j] + masked, sums[3 * j + 1] + weighted, sums[3 * j + 2] + weighted * m]
        return out

    full = rows // SUB
    out = [jnp.zeros((1, LANES), F32)] * (3 * lines)
    if full:
        sums = [jnp.zeros((SUB, LANES), F32)] * (3 * lines)
        for i in range(full):
            sums = add(read(i * SUB, SUB), 2.0 * i * SUB, sums)
        out = [jnp.sum(x, axis=0, keepdims=True) for x in sums]
    if rows % SUB:
        sums = [jnp.zeros((rows % SUB, LANES), F32)] * (3 * lines)
        sums = add(read(full * SUB, rows % SUB), 2.0 * full * SUB, sums)
        out = [x + jnp.sum(y, axis=0, keepdims=True) for x, y in zip(out, sums)]
    return [out[3 * j + k] for k in range(3) for j in range(lines)]


def cube_kernel(
    device_ref, begin_ref, span_ref, cube_ref, out_ref, begins_ref, spans_ref, held_ref, lines_sem, cube_sem,
):
    width = cube_ref.shape[0]
    owners = out_ref.shape[0]
    device = device_ref[0]

    def tile_copy(i):
        lanes = pl.ds(pl.multiple_of(i * LANES, LANES), LANES)
        return pltpu.make_async_copy(cube_ref.at[:, lanes], held_ref.at[i], cube_sem.at[i])

    line_copies = [
        pltpu.make_async_copy(begin_ref, begins_ref, lines_sem.at[0]),
        pltpu.make_async_copy(span_ref, spans_ref, lines_sem.at[1]),
    ]
    for copy in line_copies:
        copy.start()
    for i in range(owners):
        tile_copy(i).start()
    for copy in line_copies:
        copy.wait()

    def owner(i, carry):
        tile_copy(i).wait()
        lanes = pl.ds(pl.multiple_of(i * LANES, LANES), LANES)
        sums = window_sums(
            lambda row, size: held_ref[i, row : row + size, :],
            width,
            device * width,
            begins_ref[:, lanes],
            spans_ref[:, lanes],
        )
        for r, value in enumerate(sums):
            out_ref[i, r : r + 1, :] = value
        return carry

    lax.fori_loop(0, owners, owner, 0)


def cube_windows(device, begin, span, cube, devices):
    hbm = pl.BlockSpec(memory_space=pltpu.HBM)
    return pl.pallas_call(
        cube_kernel,
        in_specs=[pl.BlockSpec(memory_space=pltpu.SMEM), hbm, hbm, hbm],
        out_shape=jax.ShapeDtypeStruct((devices, 3 * begin.shape[0], LANES), F32),
        scratch_shapes=[
            pltpu.VMEM(begin.shape, jnp.int32),
            pltpu.VMEM(span.shape, jnp.int32),
            pltpu.VMEM((devices, cube.shape[0], LANES), F32),
            pltpu.SemaphoreType.DMA((2,)),
            pltpu.SemaphoreType.DMA((devices,)),
        ],
        compiler_params=pltpu.CompilerParams(vmem_limit_bytes=VMEM_LIMIT),
        name="cube_windows",
    )(device, begin, span, cube)


def add_kernel(x_ref, y_ref, out_ref):
    out_ref[...] = x_ref[...] + y_ref[...]


def pack_kernel(received_ref, sums_ref, out_ref):
    slots = received_ref.shape[1]
    for half in range(2):
        total = received_ref[half]
        for i in range(half + 2, received_ref.shape[0], 2):
            total = total + received_ref[i]
        for i in range(half, out_ref.shape[0], 2):
            out_ref[i, :slots, :] = total
    out_ref[:, slots:, :] = sums_ref[...]


def owner_kernel(
    device_ref, bins_ref, owner_ref, begin_ref, span_ref, near_ref, far_ref, inverse_ref, templates_ref,
    weights_ref, out_ref,
    held_ref, continuum_ref, bins_held_ref, owner_held_ref, begins_ref, spans_ref, starts_ref, sem, small_sem,
    *, chunk,
):
    devices = near_ref.shape[0]
    slots = weights_ref.shape[0]
    own = bins_held_ref.shape[1]
    lines = begin_ref.shape[0]
    full_width = templates_ref.shape[1]
    device = device_ref[0]
    own_lanes = pl.ds(pl.multiple_of(device * own, LANES), own)

    def copy(i):
        lanes = pl.ds(i * chunk, chunk)
        return pltpu.make_async_copy(templates_ref.at[:, lanes], held_ref.at[:, lanes], sem.at[i])

    small_copies = [
        pltpu.make_async_copy(bins_ref.at[:, own_lanes], bins_held_ref, small_sem.at[0]),
        pltpu.make_async_copy(owner_ref, owner_held_ref, small_sem.at[1]),
        pltpu.make_async_copy(begin_ref.at[:, own_lanes], begins_ref, small_sem.at[2]),
        pltpu.make_async_copy(span_ref.at[:, own_lanes], spans_ref, small_sem.at[3]),
        pltpu.make_async_copy(begin_ref.at[:, own_lanes], starts_ref, small_sem.at[4]),
    ]
    for small in small_copies:
        small.start()
    for i in range(full_width // chunk):
        copy(i).start()

    inverse = inverse_ref[...]
    low_first = device % 2 == 0

    def halves(near, far):
        return jnp.where(low_first, near, far), jnp.where(low_first, far, near)

    mine = jnp.concatenate(halves(near_ref[device, :slots, :], far_ref[device, :slots, :]), axis=1)
    weights_ref[...] = dot_f32(mine, inverse, NN)

    for small in small_copies:
        small.wait()
    bins = jnp.broadcast_to(bins_held_ref[...], (SUB, own)).T[:, :1]
    member = jnp.where(bins == owner_held_ref[...], 1.0, 0.0).astype(BF16)
    picked = []
    for half in (near_ref, far_ref):
        hi, mid, low = split3(half[:, :slots, :].reshape(devices * slots, LANES))
        picked.append(dot(member, hi, NN) + (dot(member, mid, NN) + dot(member, low, NN)))
    spaxel_weights = dot_f32(jnp.concatenate(halves(*picked), axis=1), inverse, NN)

    for i in range(full_width // chunk):
        copy(i).wait()
        value = dot_f32(spaxel_weights, held_ref[:, i * chunk : (i + 1) * chunk], NN)
        for t in range(chunk // LANES):
            continuum_ref[i * (chunk // LANES) + t] = value[:, t * LANES : (t + 1) * LANES]
    continuum_ref[full_width // LANES] = jnp.zeros((own, LANES), F32)

    begin = begins_ref[...]
    span = spans_ref[...].astype(F32)
    centre = 2.0 * (begin & (LANES - 1)).astype(F32) + span - 1.0
    rows_at = lax.broadcasted_iota(jnp.int32, (SUB, LANES), 0)
    at_row = [rows_at == r for r in range(SUB)]
    twice = 2.0 * lax.broadcasted_iota(jnp.int32, (LANES, own), 0).astype(F32)
    sums = [None] * (3 * lines)
    for j in range(lines):
        picks = ([], [])
        for g in range(own // SUB):
            rows = slice(g * SUB, (g + 1) * SUB)
            left = right = None
            for r in range(SUB):
                tile = lax.shift_right_logical(starts_ref[j, g * SUB + r], 7)
                a = continuum_ref[tile, rows, :]
                b = continuum_ref[tile + 1, rows, :]
                left = a if left is None else jnp.where(at_row[r], a, left)
                right = b if right is None else jnp.where(at_row[r], b, right)
            picks[0].append(left)
            picks[1].append(right)
        terms = None
        for side in range(2):
            block = jnp.concatenate(picks[side], axis=0).T
            m = twice + (2.0 * LANES * side - centre[j : j + 1])
            masked = jnp.where(jnp.abs(m) < span[j : j + 1], block, 0.0)
            weighted = masked * m
            new = [masked, weighted, weighted * m]
            terms = new if terms is None else [x + y for x, y in zip(terms, new)]
        for k in range(3):
            sums[k * lines + j] = jnp.sum(terms[k], axis=0, keepdims=True)
    continuum_sums = jnp.concatenate(sums, axis=0)

    cube_sums = near_ref[0, slots:, :]
    for i in range(1, devices):
        cube_sums = cube_sums + near_ref[i, slots:, :]
    scale = jnp.concatenate([span, span * span, span * span * span], axis=0)
    out_ref[...] = (cube_sums - continuum_sums) / scale


def owned(device, bins, owner, begin, span, near, far, inverse, templates, own_slots, own, chunk):
    vmem = pl.BlockSpec(memory_space=pltpu.VMEM)
    hbm = pl.BlockSpec(memory_space=pltpu.HBM)
    count, full_width = templates.shape
    lines = begin.shape[0]
    return pl.pallas_call(
        functools.partial(owner_kernel, chunk=chunk),
        in_specs=[pl.BlockSpec(memory_space=pltpu.SMEM)] + [hbm] * 4 + [vmem] * 3 + [hbm],
        out_shape=(
            jax.ShapeDtypeStruct((own_slots, count), F32),
            jax.ShapeDtypeStruct((3 * lines, own), F32),
        ),
        scratch_shapes=[
            pltpu.VMEM((count, full_width), F32),
            pltpu.VMEM((full_width // LANES + 1, own, LANES), F32),
            pltpu.VMEM((1, own), jnp.int32),
            pltpu.VMEM(owner.shape, jnp.int32),
            pltpu.VMEM((lines, own), jnp.int32),
            pltpu.VMEM((lines, own), jnp.int32),
            pltpu.SMEM((lines, own), jnp.int32),
            pltpu.SemaphoreType.DMA((full_width // chunk,)),
            pltpu.SemaphoreType.DMA((5,)),
        ],
        compiler_params=pltpu.CompilerParams(vmem_limit_bytes=VMEM_LIMIT),
        name="owned",
    )(device, bins, owner, begin, span, near, far, inverse, templates)


def shards(cube, templates, bin_id, owner_bins, line_start, line_width):
    devices = lax.axis_size("spax")
    device = lax.axis_index("spax")
    spaxels = cube.shape[0]
    total_bins = owner_bins.shape[0]
    count = templates.shape[0]
    own_spaxels = spaxels // devices
    own_slots = total_bins // devices
    here = device.reshape(1).astype(jnp.int32)
    pin = lambda x: pltpu.with_memory_space_constraint(x, pltpu.HBM)
    raw_templates = templates
    templates, columns = pin(templates), pin(cube.T)
    begin, span = pin(line_start), pin(line_width)
    bins, owner = pin(bin_id[None, :]), pin(owner_bins[None, :])

    swap = [(d, d ^ 1) for d in range(devices)]
    keep, send = project(here, bins, owner, columns, templates)
    swapped = lax.ppermute(send, "spax", swap)
    partial = in_vmem(add_kernel, jax.ShapeDtypeStruct(keep.shape, F32), "add", keep, swapped)
    partial, here_after, later = lax.optimization_barrier((partial, here, raw_templates))
    later = pin(later)
    received = lax.all_to_all(partial.reshape(devices, own_slots, LANES), "spax", 0, 0)

    sums = cube_windows(here_after, begin, span, columns, devices)
    gram, scale = scaled_gram(later, 512)
    received, sums, gram, scale = lax.optimization_barrier((received, sums, gram, scale))
    parcel = in_vmem(
        pack_kernel,
        jax.ShapeDtypeStruct((devices, own_slots + sums.shape[1], LANES), F32),
        "pack",
        received,
        sums,
    )
    parcel, gram, scale = lax.optimization_barrier((parcel, gram, scale))
    near = lax.all_to_all(parcel, "spax", 0, 0)
    inverse = in_vmem(invert_kernel, jax.ShapeDtypeStruct((count, count), F32), "invert", gram, scale)
    near, inverse = lax.optimization_barrier((near, inverse))
    far = lax.ppermute(near, "spax", swap)
    return owned(
        here, bins, owner, begin, span, near, far, inverse, later, own_slots, own_spaxels, 512
    )


def solution(mesh):
    placed = (
        P("strips", "spax"),
        P(),
        P("strips"),
        P("strips"),
        P(None, "strips"),
        P(None, "strips"),
    )
    return jax.shard_map(
        shards,
        mesh=mesh,
        in_specs=placed,
        out_specs=(P(("strips", "spax"), None), P(None, ("strips", "spax"))),
        check_vma=False,
    )
```

```python
import functools

import jax
import jax.numpy as jnp
from jax import lax
from jax.experimental import pallas as pl
from jax.experimental.pallas import tpu as pltpu
from jax.sharding import PartitionSpec as P

HIGHEST = lax.Precision.HIGHEST
F32 = jnp.float32
BF16 = jnp.bfloat16
LANES = 128
SUB = 8
VMEM_LIMIT = 20 * 1024 * 1024

NT = (((1,), (1,)), ((), ()))
NN = (((1,), (0,)), ((), ()))


def split3(x):
    hi = x.astype(BF16)
    rest = x - hi.astype(F32)
    mid = rest.astype(BF16)
    low = (rest - mid.astype(F32)).astype(BF16)
    return hi, mid, low


def dot(a, b, dims):
    return lax.dot_general(a, b, dims, preferred_element_type=F32)


def dot_f32(a, b, dims):
    return lax.dot_general(a, b, dims, precision=HIGHEST, preferred_element_type=F32)


def template_window(width, full_width):
    return min(full_width, -(-(width + LANES - 1) // LANES) * LANES)


def project_kernel(
    device_ref, bins_ref, owner_ref, cube_ref, templates_ref, keep_ref, send_ref,
    held_ref, window_ref, bins_held_ref, owner_held_ref, cube_sem, window_sem, small_sem, *, chunk,
):
    width, spaxels = cube_ref.shape
    slots = keep_ref.shape[0]
    full_width = templates_ref.shape[1]
    first = device_ref[0] * width
    window = window_ref.shape[1]
    base = pl.multiple_of(jnp.minimum(first // LANES * LANES, full_width - window), LANES)
    chunks = spaxels // chunk

    def cube_copy(i):
        lanes = pl.ds(i * chunk, chunk)
        return pltpu.make_async_copy(cube_ref.at[:, lanes], held_ref.at[:, lanes], cube_sem.at[i])

    window_copy = pltpu.make_async_copy(templates_ref.at[:, pl.ds(base, window)], window_ref, window_sem)

    small_copies = [
        pltpu.make_async_copy(bins_ref, bins_held_ref, small_sem.at[0]),
        pltpu.make_async_copy(owner_ref, owner_held_ref, small_sem.at[1]),
    ]

    @pl.when(pl.program_id(0) == 0)
    def _():
        for copy in small_copies:
            copy.start()
        for i in range(chunks):
            cube_copy(i).start()
        window_copy.start()
        for copy in small_copies:
            copy.wait()

    owner = owner_held_ref[:, pl.ds(pl.multiple_of(pl.program_id(0) * slots, LANES), slots)]
    owner = jnp.broadcast_to(owner, (SUB, slots)).T[:, :1]
    sums = jnp.zeros((slots, width), F32)
    counts = jnp.zeros((slots, LANES), F32)
    for i in range(chunks):
        here = owner == bins_held_ref[:, i * chunk : (i + 1) * chunk]
        ones = jnp.where(here, 1.0, 0.0)
        for lane in range(0, chunk, LANES):
            counts = counts + ones[:, lane : lane + LANES]
        member = ones.astype(BF16)

        @pl.when(pl.program_id(0) == 0)
        def _(i=i):
            cube_copy(i).wait()

        for part in split3(held_ref[:, i * chunk : (i + 1) * chunk]):
            sums = sums + dot(member, part, NT)
    means = sums / jnp.sum(counts, axis=1, keepdims=True)

    @pl.when(pl.program_id(0) == 0)
    def _():
        window_copy.wait()

    mine = pltpu.roll(window_ref[...], window - (first - base), 1)[:, :width]
    projections = dot_f32(means, mine, NT) * (1.0 / full_width)
    low, high = projections[:, :LANES], projections[:, LANES:]
    low_kept = device_ref[0] % 2 == 0
    keep_ref[...] = jnp.where(low_kept, low, high)
    send_ref[...] = jnp.where(low_kept, high, low)


def project(device, bins, owner, cube, templates):
    width, spaxels = cube.shape
    slots = owner.shape[1]
    block = min(slots, 512)
    chunk = min(spaxels, 512)
    count, full_width = templates.shape
    return pl.pallas_call(
        functools.partial(project_kernel, chunk=chunk),
        grid=(slots // block,),
        in_specs=[
            pl.BlockSpec(memory_space=pltpu.SMEM),
            pl.BlockSpec(memory_space=pltpu.HBM),
            pl.BlockSpec(memory_space=pltpu.HBM),
            pl.BlockSpec(memory_space=pltpu.HBM),
            pl.BlockSpec(memory_space=pltpu.HBM),
        ],
        out_specs=[pl.BlockSpec((block, LANES), lambda i: (i, 0))] * 2,
        out_shape=[jax.ShapeDtypeStruct((slots, LANES), F32)] * 2,
        scratch_shapes=[
            pltpu.VMEM((width, spaxels), F32),
            pltpu.VMEM((count, template_window(width, full_width)), F32),
            pltpu.VMEM(bins.shape, jnp.int32),
            pltpu.VMEM(owner.shape, jnp.int32),
            pltpu.SemaphoreType.DMA((spaxels // chunk,)),
            pltpu.SemaphoreType.DMA,
            pltpu.SemaphoreType.DMA((2,)),
        ],
        compiler_params=pltpu.CompilerParams(vmem_limit_bytes=VMEM_LIMIT),
        name="project",
    )(device, bins, owner, cube, templates)


def reciprocal(x):
    r = pl.reciprocal(x, approx=True)
    r = r * (2.0 - x * r)
    return r * (2.0 - x * r)


def invert_tile(tile):
    size = tile.shape[0]
    count = size // SUB
    lanes = lax.broadcasted_iota(jnp.int32, (SUB, size), 1)
    rows_at = lax.broadcasted_iota(jnp.int32, (SUB, size), 0)
    rows = [tile[i * SUB : (i + 1) * SUB, :] for i in range(count)]
    for k in range(count):
        block = rows[k]
        first = k * SUB
        columns = [
            jnp.broadcast_to(block[:, first + j : first + j + 1], (SUB, size)) for j in range(SUB)
        ]

        for p in range(0, SUB, 2):
            q = p + 1
            of_p = [jnp.broadcast_to(column[p : p + 1, :], (SUB, size)) for column in columns]
            of_q = [jnp.broadcast_to(column[q : q + 1, :], (SUB, size)) for column in columns]
            pp, pq, qq = of_p[p], of_p[q], of_q[q]
            inverse = reciprocal(pp * qq - pq * pq)
            x, y, z = qq * inverse, -(pq * inverse), pp * inverse
            by_p = (columns[p] * qq - columns[q] * pq) * inverse
            by_q = (columns[q] * pp - columns[p] * pq) * inverse
            at_p, at_q = rows_at == p, rows_at == q
            take_p = jnp.where(at_p, 1.0 - x, jnp.where(at_q, -y, by_p))
            take_q = jnp.where(at_q, 1.0 - z, jnp.where(at_p, -y, by_q))
            for j in range(SUB):
                if j not in (p, q):
                    columns[j] = (columns[j] - take_p * of_p[j]) - take_q * of_q[j]
            columns[p] = jnp.where(at_p, -x, jnp.where(at_q, -y, by_p))
            columns[q] = jnp.where(at_q, -z, jnp.where(at_p, -y, by_q))
        terms = [columns[j] * jnp.broadcast_to(block[j : j + 1, :], (SUB, size)) for j in range(SUB)]
        while len(terms) > 1:
            terms = [x + y for x, y in zip(terms[::2], terms[1::2])]
        swept = -terms[0]
        for j in range(SUB):
            swept = jnp.where(lanes == first + j, columns[j], swept)
        inside = (lanes >= first) & (lanes < first + SUB)
        spread_rows = [jnp.broadcast_to(swept[j : j + 1, :], (SUB, size)) for j in range(SUB)]
        order = list(range(k + 1, count)) + list(range(k))
        for i in order:
            terms = [
                jnp.broadcast_to(rows[i][:, first + j : first + j + 1], (SUB, size)) * spread_rows[j]
                for j in range(SUB)
            ]
            while len(terms) > 1:
                terms = [x + y for x, y in zip(terms[::2], terms[1::2])]
            rows[i] = jnp.where(inside, 0.0, rows[i]) - terms[0]
        rows[k] = swept
    return -jnp.concatenate(rows, axis=0)


def gram_kernel(templates_ref, gram_ref, scale_ref, held_ref, sem, *, chunk):
    count, full_width = templates_ref.shape

    def copy(i):
        lanes = pl.ds(i * chunk, chunk)
        return pltpu.make_async_copy(templates_ref.at[:, lanes], held_ref.at[:, lanes], sem.at[i])

    for i in range(full_width // chunk):
        copy(i).start()
    even = jnp.zeros((count, count), F32)
    mixed = jnp.zeros((count, count), F32)
    for i in range(full_width // chunk):
        copy(i).wait()
        hi, mid, low = split3(held_ref[:, i * chunk : (i + 1) * chunk])
        even = even + (dot(hi, hi, NT) + dot(mid, mid, NT))
        mixed = mixed + (dot(hi, mid, NT) + dot(hi, low, NT))
    gram = (even + (mixed + mixed.T)) * (1.0 / full_width)
    same = lax.broadcasted_iota(jnp.int32, gram.shape, 0) == lax.broadcasted_iota(jnp.int32, gram.shape, 1)
    diagonal = jnp.where(same, gram, 0.0)
    row = lax.rsqrt(jnp.sum(diagonal, axis=0, keepdims=True))
    column = lax.rsqrt(jnp.sum(diagonal, axis=1, keepdims=True))
    gram = gram * row * column
    scale_ref[...] = row
    gram_ref[...] = gram


def scaled_gram(templates, chunk):
    count, full_width = templates.shape
    return pl.pallas_call(
        functools.partial(gram_kernel, chunk=chunk),
        in_specs=[pl.BlockSpec(memory_space=pltpu.HBM)],
        out_shape=(
            jax.ShapeDtypeStruct((count, count), F32),
            jax.ShapeDtypeStruct((1, count), F32),
        ),
        scratch_shapes=[
            pltpu.VMEM((count, full_width), F32),
            pltpu.SemaphoreType.DMA((full_width // chunk,)),
        ],
        compiler_params=pltpu.CompilerParams(vmem_limit_bytes=VMEM_LIMIT),
        name="gram",
    )(templates)


def invert_kernel(
    gram_ref, scale_ref, templates_ref, out_ref, hi_ref, mid_ref, low_ref, held_ref, sem, *, chunk,
):
    full_width = templates_ref.shape[1]

    def copy(i):
        lanes = pl.ds(i * chunk, chunk)
        return pltpu.make_async_copy(templates_ref.at[:, lanes], held_ref.at[:, lanes], sem.at[i])

    for i in range(full_width // chunk):
        copy(i).start()
    first = invert_tile(gram_ref[:LANES, :LANES])
    side = gram_ref[:LANES, LANES:]
    half = dot_f32(first, side, NN)
    schur = gram_ref[LANES:, LANES:] - dot_f32(side.T, half, NN)
    last = invert_tile(schur)
    cross = dot_f32(half, last, NN)
    row = scale_ref[...]
    column = jnp.broadcast_to(row, (SUB, row.shape[1])).T[:, :1]
    near, far = row[:, :LANES], row[:, LANES:]
    out_ref[:LANES, :LANES] = (first + dot_f32(cross, half, NT)) * near * column[:LANES]
    out_ref[:LANES, LANES:] = -cross * far * column[:LANES]
    out_ref[LANES:, :LANES] = -cross.T * near * column[LANES:]
    out_ref[LANES:, LANES:] = last * far * column[LANES:]

    inverse = out_ref[...]
    for i in range(full_width // chunk):
        copy(i).wait()
        lanes = slice(i * chunk, (i + 1) * chunk)
        hi_ref[:, lanes], mid_ref[:, lanes], low_ref[:, lanes] = split3(dot_f32(inverse, held_ref[:, lanes], NN))


def invert(gram, scale, templates, chunk):
    vmem = pl.BlockSpec(memory_space=pltpu.VMEM)
    count, full_width = templates.shape
    part = jax.ShapeDtypeStruct((count, full_width), BF16)
    return pl.pallas_call(
        functools.partial(invert_kernel, chunk=chunk),
        in_specs=[vmem, vmem, pl.BlockSpec(memory_space=pltpu.HBM)],
        out_shape=(jax.ShapeDtypeStruct((count, count), F32), part, part, part),
        scratch_shapes=[
            pltpu.VMEM((count, full_width), F32),
            pltpu.SemaphoreType.DMA((full_width // chunk,)),
        ],
        compiler_params=pltpu.CompilerParams(vmem_limit_bytes=VMEM_LIMIT),
        name="invert",
    )(gram, scale, templates)


def in_vmem(kernel, shapes, name, *arrays):
    return pl.pallas_call(
        kernel,
        out_shape=shapes,
        compiler_params=pltpu.CompilerParams(vmem_limit_bytes=VMEM_LIMIT),
        name=name,
    )(*arrays)


def window_sums(read, rows, first, begin, span):
    lines = begin.shape[0]
    sub = lax.broadcasted_iota(jnp.int32, (SUB, LANES), 0)
    spans = [jnp.broadcast_to(span[j : j + 1], (SUB, LANES)).astype(F32) for j in range(lines)]
    offsets = [
        (2 * (first + sub - jnp.broadcast_to(begin[j : j + 1], (SUB, LANES))) + 1).astype(F32) - spans[j]
        for j in range(lines)
    ]

    def add(block, shift, sums):
        size = block.shape[0]
        out = []
        for j in range(lines):
            m = offsets[j][:size] + shift
            masked = jnp.where(jnp.abs(m) < spans[j][:size], block, 0.0)
            weighted = masked * m
            out += [sums[3 * j] + masked, sums[3 * j + 1] + weighted, sums[3 * j + 2] + weighted * m]
        return out

    full = rows // SUB
    out = [jnp.zeros((1, LANES), F32)] * (3 * lines)
    if full:
        sums = [jnp.zeros((SUB, LANES), F32)] * (3 * lines)
        for i in range(full):
            sums = add(read(i * SUB, SUB), 2.0 * i * SUB, sums)
        out = [jnp.sum(x, axis=0, keepdims=True) for x in sums]
    if rows % SUB:
        sums = [jnp.zeros((rows % SUB, LANES), F32)] * (3 * lines)
        sums = add(read(full * SUB, rows % SUB), 2.0 * full * SUB, sums)
        out = [x + jnp.sum(y, axis=0, keepdims=True) for x, y in zip(out, sums)]
    return [out[3 * j + k] for k in range(3) for j in range(lines)]


def cube_kernel(
    device_ref, begin_ref, span_ref, cube_ref, out_ref, begins_ref, spans_ref, held_ref, lines_sem, cube_sem,
):
    width = cube_ref.shape[0]
    owners = out_ref.shape[0]
    device = device_ref[0]

    def tile_copy(i):
        lanes = pl.ds(pl.multiple_of(i * LANES, LANES), LANES)
        return pltpu.make_async_copy(cube_ref.at[:, lanes], held_ref.at[i], cube_sem.at[i])

    line_copies = [
        pltpu.make_async_copy(begin_ref, begins_ref, lines_sem.at[0]),
        pltpu.make_async_copy(span_ref, spans_ref, lines_sem.at[1]),
    ]
    for copy in line_copies:
        copy.start()
    for i in range(owners):
        tile_copy(i).start()
    for copy in line_copies:
        copy.wait()

    def owner(i, carry):
        tile_copy(i).wait()
        lanes = pl.ds(pl.multiple_of(i * LANES, LANES), LANES)
        sums = window_sums(
            lambda row, size: held_ref[i, row : row + size, :],
            width,
            device * width,
            begins_ref[:, lanes],
            spans_ref[:, lanes],
        )
        for r, value in enumerate(sums):
            out_ref[i, r : r + 1, :] = value
        return carry

    lax.fori_loop(0, owners, owner, 0)


def cube_windows(device, begin, span, cube, devices):
    hbm = pl.BlockSpec(memory_space=pltpu.HBM)
    return pl.pallas_call(
        cube_kernel,
        in_specs=[pl.BlockSpec(memory_space=pltpu.SMEM), hbm, hbm, hbm],
        out_shape=jax.ShapeDtypeStruct((devices, 3 * begin.shape[0], LANES), F32),
        scratch_shapes=[
            pltpu.VMEM(begin.shape, jnp.int32),
            pltpu.VMEM(span.shape, jnp.int32),
            pltpu.VMEM((devices, cube.shape[0], LANES), F32),
            pltpu.SemaphoreType.DMA((2,)),
            pltpu.SemaphoreType.DMA((devices,)),
        ],
        compiler_params=pltpu.CompilerParams(vmem_limit_bytes=VMEM_LIMIT),
        name="cube_windows",
    )(device, begin, span, cube)


def add_kernel(x_ref, y_ref, out_ref):
    out_ref[...] = x_ref[...] + y_ref[...]


def pack_kernel(received_ref, sums_ref, out_ref):
    slots = received_ref.shape[1]
    for half in range(2):
        total = received_ref[half]
        for i in range(half + 2, received_ref.shape[0], 2):
            total = total + received_ref[i]
        for i in range(half, out_ref.shape[0], 2):
            out_ref[i, :slots, :] = total
    out_ref[:, slots:, :] = sums_ref[...]


def owner_kernel(
    device_ref, bins_ref, owner_ref, begin_ref, span_ref, near_ref, far_ref, inverse_ref, hi_ref, mid_ref, low_ref,
    weights_ref, out_ref,
    continuum_ref, bins_held_ref, owner_held_ref, begins_ref, spans_ref, starts_ref, small_sem,
    *, chunk,
):
    devices = near_ref.shape[0]
    slots = weights_ref.shape[0]
    own = bins_held_ref.shape[1]
    lines = begin_ref.shape[0]
    full_width = hi_ref.shape[1]
    device = device_ref[0]
    own_lanes = pl.ds(pl.multiple_of(device * own, LANES), own)

    small_copies = [
        pltpu.make_async_copy(bins_ref.at[:, own_lanes], bins_held_ref, small_sem.at[0]),
        pltpu.make_async_copy(owner_ref, owner_held_ref, small_sem.at[1]),
        pltpu.make_async_copy(begin_ref.at[:, own_lanes], begins_ref, small_sem.at[2]),
        pltpu.make_async_copy(span_ref.at[:, own_lanes], spans_ref, small_sem.at[3]),
        pltpu.make_async_copy(begin_ref.at[:, own_lanes], starts_ref, small_sem.at[4]),
    ]
    for small in small_copies:
        small.start()

    low_first = device % 2 == 0

    def halves(near, far):
        return jnp.where(low_first, near, far), jnp.where(low_first, far, near)

    mine = jnp.concatenate(halves(near_ref[device, :slots, :], far_ref[device, :slots, :]), axis=1)
    weights_ref[...] = dot_f32(mine, inverse_ref[...], NN)

    for small in small_copies:
        small.wait()
    bins = jnp.broadcast_to(bins_held_ref[...], (SUB, own)).T[:, :1]
    member = jnp.where(bins == owner_held_ref[...], 1.0, 0.0).astype(BF16)
    picked = []
    for half in (near_ref, far_ref):
        hi, mid, low = split3(half[:, :slots, :].reshape(devices * slots, LANES))
        picked.append(dot(member, hi, NN) + (dot(member, mid, NN) + dot(member, low, NN)))
    hi, mid, low = split3(jnp.concatenate(halves(*picked), axis=1))

    for i in range(full_width // chunk):
        lanes = slice(i * chunk, (i + 1) * chunk)
        first, second, third = hi_ref[:, lanes], mid_ref[:, lanes], low_ref[:, lanes]
        value = dot(hi, first, NN) + (
            (dot(mid, first, NN) + dot(hi, second, NN))
            + (dot(low, first, NN) + dot(mid, second, NN) + dot(hi, third, NN))
        )
        for t in range(chunk // LANES):
            continuum_ref[i * (chunk // LANES) + t] = value[:, t * LANES : (t + 1) * LANES]
    continuum_ref[full_width // LANES] = jnp.zeros((own, LANES), F32)

    begin = begins_ref[...]
    span = spans_ref[...].astype(F32)
    centre = 2.0 * (begin & (LANES - 1)).astype(F32) + span - 1.0
    rows_at = lax.broadcasted_iota(jnp.int32, (SUB, LANES), 0)
    at_row = [rows_at == r for r in range(SUB)]
    twice = 2.0 * lax.broadcasted_iota(jnp.int32, (LANES, own), 0).astype(F32)
    sums = [None] * (3 * lines)
    for j in range(lines):
        picks = ([], [])
        for g in range(own // SUB):
            rows = slice(g * SUB, (g + 1) * SUB)
            left = right = None
            for r in range(SUB):
                tile = lax.shift_right_logical(starts_ref[j, g * SUB + r], 7)
                a = continuum_ref[tile, rows, :]
                b = continuum_ref[tile + 1, rows, :]
                left = a if left is None else jnp.where(at_row[r], a, left)
                right = b if right is None else jnp.where(at_row[r], b, right)
            picks[0].append(left)
            picks[1].append(right)
        terms = None
        for side in range(2):
            block = jnp.concatenate(picks[side], axis=0).T
            m = twice + (2.0 * LANES * side - centre[j : j + 1])
            masked = jnp.where(jnp.abs(m) < span[j : j + 1], block, 0.0)
            weighted = masked * m
            new = [masked, weighted, weighted * m]
            terms = new if terms is None else [x + y for x, y in zip(terms, new)]
        for k in range(3):
            sums[k * lines + j] = jnp.sum(terms[k], axis=0, keepdims=True)
    continuum_sums = jnp.concatenate(sums, axis=0)

    cube_sums = near_ref[0, slots:, :]
    for i in range(1, devices):
        cube_sums = cube_sums + near_ref[i, slots:, :]
    scale = jnp.concatenate([span, span * span, span * span * span], axis=0)
    out_ref[...] = (cube_sums - continuum_sums) / scale


def owned(device, bins, owner, begin, span, near, far, inverse, parts, own_slots, own, chunk):
    vmem = pl.BlockSpec(memory_space=pltpu.VMEM)
    hbm = pl.BlockSpec(memory_space=pltpu.HBM)
    count, full_width = parts[0].shape
    lines = begin.shape[0]
    return pl.pallas_call(
        functools.partial(owner_kernel, chunk=chunk),
        in_specs=[pl.BlockSpec(memory_space=pltpu.SMEM)] + [hbm] * 4 + [vmem] * 6,
        out_shape=(
            jax.ShapeDtypeStruct((own_slots, count), F32),
            jax.ShapeDtypeStruct((3 * lines, own), F32),
        ),
        scratch_shapes=[
            pltpu.VMEM((full_width // LANES + 1, own, LANES), F32),
            pltpu.VMEM((1, own), jnp.int32),
            pltpu.VMEM(owner.shape, jnp.int32),
            pltpu.VMEM((lines, own), jnp.int32),
            pltpu.VMEM((lines, own), jnp.int32),
            pltpu.SMEM((lines, own), jnp.int32),
            pltpu.SemaphoreType.DMA((5,)),
        ],
        compiler_params=pltpu.CompilerParams(vmem_limit_bytes=VMEM_LIMIT),
        name="owned",
    )(device, bins, owner, begin, span, near, far, inverse, *parts)


def shards(cube, templates, bin_id, owner_bins, line_start, line_width):
    devices = lax.axis_size("spax")
    device = lax.axis_index("spax")
    spaxels = cube.shape[0]
    total_bins = owner_bins.shape[0]
    count = templates.shape[0]
    own_spaxels = spaxels // devices
    own_slots = total_bins // devices
    here = device.reshape(1).astype(jnp.int32)
    pin = lambda x: pltpu.with_memory_space_constraint(x, pltpu.HBM)
    raw_templates = templates
    templates, columns = pin(templates), pin(cube.T)
    begin, span = pin(line_start), pin(line_width)
    bins, owner = pin(bin_id[None, :]), pin(owner_bins[None, :])

    swap = [(d, d ^ 1) for d in range(devices)]
    keep, send = project(here, bins, owner, columns, templates)
    swapped = lax.ppermute(send, "spax", swap)
    partial = in_vmem(add_kernel, jax.ShapeDtypeStruct(keep.shape, F32), "add", keep, swapped)
    partial, here_after, later = lax.optimization_barrier((partial, here, raw_templates))
    later = pin(later)
    received = lax.all_to_all(partial.reshape(devices, own_slots, LANES), "spax", 0, 0)

    sums = cube_windows(here_after, begin, span, columns, devices)
    gram, scale = scaled_gram(later, 512)
    received, sums, gram, scale = lax.optimization_barrier((received, sums, gram, scale))
    parcel = in_vmem(
        pack_kernel,
        jax.ShapeDtypeStruct((devices, own_slots + sums.shape[1], LANES), F32),
        "pack",
        received,
        sums,
    )
    parcel, gram, scale = lax.optimization_barrier((parcel, gram, scale))
    near = lax.all_to_all(parcel, "spax", 0, 0)
    inverse, *parts = invert(gram, scale, later, 512)
    near, inverse = lax.optimization_barrier((near, inverse))
    far = lax.ppermute(near, "spax", swap)
    return owned(
        here, bins, owner, begin, span, near, far, inverse, parts, own_slots, own_spaxels, 512
    )


def solution(mesh):
    placed = (
        P("strips", "spax"),
        P(),
        P("strips"),
        P("strips"),
        P(None, "strips"),
        P(None, "strips"),
    )
    return jax.shard_map(
        shards,
        mesh=mesh,
        in_specs=placed,
        out_specs=(P(("strips", "spax"), None), P(None, ("strips", "spax"))),
        check_vma=False,
    )
```

```python
import functools

import jax
import jax.numpy as jnp
from jax import lax
from jax.experimental import pallas as pl
from jax.experimental.pallas import tpu as pltpu
from jax.sharding import PartitionSpec as P

HIGHEST = lax.Precision.HIGHEST
F32 = jnp.float32
BF16 = jnp.bfloat16
LANES = 128
SUB = 8
VMEM_LIMIT = 20 * 1024 * 1024

NT = (((1,), (1,)), ((), ()))
NN = (((1,), (0,)), ((), ()))


def split3(x):
    hi = x.astype(BF16)
    rest = x - hi.astype(F32)
    mid = rest.astype(BF16)
    low = (rest - mid.astype(F32)).astype(BF16)
    return hi, mid, low


def dot(a, b, dims):
    return lax.dot_general(a, b, dims, preferred_element_type=F32)


def dot_f32(a, b, dims):
    return lax.dot_general(a, b, dims, precision=HIGHEST, preferred_element_type=F32)


def template_window(width, full_width):
    return min(full_width, -(-(width + LANES - 1) // LANES) * LANES)


def project_kernel(
    device_ref, bins_ref, owner_ref, cube_ref, templates_ref, keep_ref, send_ref,
    held_ref, window_ref, member_ref, bins_held_ref, owner_held_ref, cube_sem, window_sem, small_sem, *, chunk,
):
    width, spaxels = cube_ref.shape
    slots = keep_ref.shape[0]
    full_width = templates_ref.shape[1]
    first = device_ref[0] * width
    window = window_ref.shape[1]
    base = pl.multiple_of(jnp.minimum(first // LANES * LANES, full_width - window), LANES)
    chunks = spaxels // chunk

    def cube_copy(i):
        lanes = pl.ds(i * chunk, chunk)
        return pltpu.make_async_copy(cube_ref.at[:, lanes], held_ref.at[:, lanes], cube_sem.at[i])

    window_copy = pltpu.make_async_copy(templates_ref.at[:, pl.ds(base, window)], window_ref, window_sem)

    small_copies = [
        pltpu.make_async_copy(bins_ref, bins_held_ref, small_sem.at[0]),
        pltpu.make_async_copy(owner_ref, owner_held_ref, small_sem.at[1]),
    ]

    def at_first(action):
        pl.when(pl.program_id(0) == 0)(action)

    @at_first
    def _():
        for copy in small_copies:
            copy.start()
        window_copy.start()
        for i in range(chunks):
            cube_copy(i).start()
        for copy in small_copies:
            copy.wait()

    owner = owner_held_ref[:, pl.ds(pl.multiple_of(pl.program_id(0) * slots, LANES), slots)]
    owner = jnp.broadcast_to(owner, (SUB, slots)).T[:, :1]
    counts = jnp.zeros((slots, LANES), F32)
    for i in range(chunks):
        lanes = slice(i * chunk, (i + 1) * chunk)
        ones = jnp.where(owner == bins_held_ref[:, lanes], 1.0, 0.0)
        for lane in range(0, chunk, LANES):
            counts = counts + ones[:, lane : lane + LANES]
        member_ref[:, lanes] = ones.astype(BF16)
    counts = jnp.sum(counts, axis=1, keepdims=True)

    @at_first
    def _():
        window_copy.wait()

    mine = pltpu.roll(window_ref[...], window - (first - base), 1)[:, :width]

    sums = jnp.zeros((slots, width), F32)
    for i in range(chunks):

        @at_first
        def _(i=i):
            cube_copy(i).wait()

        lanes = slice(i * chunk, (i + 1) * chunk)
        member = member_ref[:, lanes]
        for part in split3(held_ref[:, lanes]):
            sums = sums + dot(member, part, NT)
    means = sums / counts
    projections = dot_f32(means, mine, NT) * (1.0 / full_width)
    low, high = projections[:, :LANES], projections[:, LANES:]
    low_kept = device_ref[0] % 2 == 0
    keep_ref[...] = jnp.where(low_kept, low, high)
    send_ref[...] = jnp.where(low_kept, high, low)


def project(device, bins, owner, cube, templates):
    width, spaxels = cube.shape
    slots = owner.shape[1]
    block = min(slots, 512, max(LANES, 2**20 // spaxels))
    chunk = min(spaxels, 512)
    count, full_width = templates.shape
    return pl.pallas_call(
        functools.partial(project_kernel, chunk=chunk),
        grid=(slots // block,),
        in_specs=[
            pl.BlockSpec(memory_space=pltpu.SMEM),
            pl.BlockSpec(memory_space=pltpu.HBM),
            pl.BlockSpec(memory_space=pltpu.HBM),
            pl.BlockSpec(memory_space=pltpu.HBM),
            pl.BlockSpec(memory_space=pltpu.HBM),
        ],
        out_specs=[pl.BlockSpec((block, LANES), lambda i: (i, 0))] * 2,
        out_shape=[jax.ShapeDtypeStruct((slots, LANES), F32)] * 2,
        scratch_shapes=[
            pltpu.VMEM((width, spaxels), F32),
            pltpu.VMEM((count, template_window(width, full_width)), F32),
            pltpu.VMEM((block, spaxels), BF16),
            pltpu.VMEM(bins.shape, jnp.int32),
            pltpu.VMEM(owner.shape, jnp.int32),
            pltpu.SemaphoreType.DMA((spaxels // chunk,)),
            pltpu.SemaphoreType.DMA,
            pltpu.SemaphoreType.DMA((2,)),
        ],
        compiler_params=pltpu.CompilerParams(vmem_limit_bytes=VMEM_LIMIT),
        name="project",
    )(device, bins, owner, cube, templates)


def reciprocal(x):
    r = pl.reciprocal(x, approx=True)
    r = r * (2.0 - x * r)
    return r * (2.0 - x * r)


def invert_tile(tile):
    size = tile.shape[0]
    count = size // SUB
    lanes = lax.broadcasted_iota(jnp.int32, (SUB, size), 1)
    rows_at = lax.broadcasted_iota(jnp.int32, (SUB, size), 0)
    rows = [tile[i * SUB : (i + 1) * SUB, :] for i in range(count)]
    for k in range(count):
        block = rows[k]
        first = k * SUB
        a = {}
        for i in range(SUB):
            for j in range(i, SUB):
                a[i, j] = jnp.broadcast_to(block[i : i + 1, first + j : first + j + 1], (SUB, size))

        def at(i, j):
            return (i, j) if i <= j else (j, i)

        for p in range(0, SUB, 2):
            q = p + 1
            pp, pq, qq = a[p, p], a[p, q], a[q, q]
            inverse = reciprocal(pp * qq - pq * pq)
            others = [i for i in range(SUB) if i not in (p, q)]
            old = {i: (a[at(i, p)], a[at(i, q)]) for i in others}
            new = {
                i: ((u * qq - v * pq) * inverse, (v * pp - u * pq) * inverse) for i, (u, v) in old.items()
            }
            for i in others:
                for j in others:
                    if i <= j:
                        a[i, j] = a[i, j] - new[i][0] * old[j][0] - new[i][1] * old[j][1]
            for i in others:
                a[at(i, p)], a[at(i, q)] = new[i]
            a[p, p], a[p, q], a[q, q] = -(qq * inverse), pq * inverse, -(pp * inverse)
        columns = []
        for j in range(SUB):
            column = a[at(0, j)]
            for i in range(1, SUB):
                column = jnp.where(rows_at == i, a[at(i, j)], column)
            columns.append(column)
        terms = [columns[j] * jnp.broadcast_to(block[j : j + 1, :], (SUB, size)) for j in range(SUB)]
        while len(terms) > 1:
            terms = [x + y for x, y in zip(terms[::2], terms[1::2])]
        swept = -terms[0]
        for j in range(SUB):
            swept = jnp.where(lanes == first + j, columns[j], swept)
        inside = (lanes >= first) & (lanes < first + SUB)
        spread_rows = [jnp.broadcast_to(swept[j : j + 1, :], (SUB, size)) for j in range(SUB)]
        order = list(range(k + 1, count)) + list(range(k))
        for i in order:
            terms = [
                jnp.broadcast_to(rows[i][:, first + j : first + j + 1], (SUB, size)) * spread_rows[j]
                for j in range(SUB)
            ]
            while len(terms) > 1:
                terms = [x + y for x, y in zip(terms[::2], terms[1::2])]
            rows[i] = jnp.where(inside, 0.0, rows[i]) - terms[0]
        rows[k] = swept
    return -jnp.concatenate(rows, axis=0)


def gram_kernel(templates_ref, gram_ref, scale_ref, hi_ref, mid_ref, low_ref, held_ref, sem, *, chunk):
    count, full_width = templates_ref.shape

    def copy(i):
        lanes = pl.ds(i * chunk, chunk)
        return pltpu.make_async_copy(templates_ref.at[:, lanes], held_ref.at[:, lanes], sem.at[i])

    for i in range(full_width // chunk):
        copy(i).start()
    even = jnp.zeros((count, count), F32)
    mixed = jnp.zeros((count, count), F32)
    for i in range(full_width // chunk):
        copy(i).wait()
        lanes = slice(i * chunk, (i + 1) * chunk)
        hi, mid, low = split3(held_ref[:, lanes])
        hi_ref[:, lanes], mid_ref[:, lanes], low_ref[:, lanes] = hi, mid, low
        even = even + (dot(hi, hi, NT) + dot(mid, mid, NT))
        mixed = mixed + (dot(hi, mid, NT) + dot(hi, low, NT))
    gram = (even + (mixed + mixed.T)) * (1.0 / full_width)
    same = lax.broadcasted_iota(jnp.int32, gram.shape, 0) == lax.broadcasted_iota(jnp.int32, gram.shape, 1)
    diagonal = jnp.where(same, gram, 0.0)
    row = lax.rsqrt(jnp.sum(diagonal, axis=0, keepdims=True))
    column = lax.rsqrt(jnp.sum(diagonal, axis=1, keepdims=True))
    gram = gram * row * column
    scale_ref[...] = row
    gram_ref[...] = gram


def scaled_gram(templates, chunk):
    count, full_width = templates.shape
    part = pltpu.VMEM((count, full_width), BF16)
    return pl.pallas_call(
        functools.partial(gram_kernel, chunk=chunk),
        in_specs=[pl.BlockSpec(memory_space=pltpu.HBM)],
        out_shape=(
            jax.ShapeDtypeStruct((count, count), F32),
            jax.ShapeDtypeStruct((1, count), F32),
            part,
            part,
            part,
        ),
        scratch_shapes=[
            pltpu.VMEM((count, full_width), F32),
            pltpu.SemaphoreType.DMA((full_width // chunk,)),
        ],
        compiler_params=pltpu.CompilerParams(vmem_limit_bytes=VMEM_LIMIT),
        name="gram",
    )(templates)


def invert_kernel(gram_ref, scale_ref, out_ref):
    first = invert_tile(gram_ref[:LANES, :LANES])
    side = gram_ref[:LANES, LANES:]
    half = dot_f32(first, side, NN)
    schur = gram_ref[LANES:, LANES:] - dot_f32(side.T, half, NN)
    last = invert_tile(schur)
    cross = dot_f32(half, last, NN)
    row = scale_ref[...]
    column = jnp.broadcast_to(row, (SUB, row.shape[1])).T[:, :1]
    near, far = row[:, :LANES], row[:, LANES:]
    out_ref[:LANES, :LANES] = (first + dot_f32(cross, half, NT)) * near * column[:LANES]
    out_ref[:LANES, LANES:] = -cross * far * column[:LANES]
    out_ref[LANES:, :LANES] = -cross.T * near * column[LANES:]
    out_ref[LANES:, LANES:] = last * far * column[LANES:]


def in_vmem(kernel, shapes, name, *arrays):
    return pl.pallas_call(
        kernel,
        out_shape=shapes,
        compiler_params=pltpu.CompilerParams(vmem_limit_bytes=VMEM_LIMIT),
        name=name,
    )(*arrays)


def window_sums(read, rows, first, begin, span):
    lines = begin.shape[0]
    sub = lax.broadcasted_iota(jnp.int32, (SUB, LANES), 0)
    spans = [jnp.broadcast_to(span[j : j + 1], (SUB, LANES)).astype(F32) for j in range(lines)]
    offsets = [
        (2 * (first + sub - jnp.broadcast_to(begin[j : j + 1], (SUB, LANES))) + 1).astype(F32) - spans[j]
        for j in range(lines)
    ]

    def add(block, shift, sums):
        size = block.shape[0]
        out = []
        for j in range(lines):
            m = offsets[j][:size] + shift
            masked = jnp.where(jnp.abs(m) < spans[j][:size], block, 0.0)
            weighted = masked * m
            out += [sums[3 * j] + masked, sums[3 * j + 1] + weighted, sums[3 * j + 2] + weighted * m]
        return out

    full = rows // SUB
    out = [jnp.zeros((1, LANES), F32)] * (3 * lines)
    if full:
        sums = [jnp.zeros((SUB, LANES), F32)] * (3 * lines)
        for i in range(full):
            sums = add(read(i * SUB, SUB), 2.0 * i * SUB, sums)
        out = [jnp.sum(x, axis=0, keepdims=True) for x in sums]
    if rows % SUB:
        sums = [jnp.zeros((rows % SUB, LANES), F32)] * (3 * lines)
        sums = add(read(full * SUB, rows % SUB), 2.0 * full * SUB, sums)
        out = [x + jnp.sum(y, axis=0, keepdims=True) for x, y in zip(out, sums)]
    return [out[3 * j + k] for k in range(3) for j in range(lines)]


def cube_kernel(
    device_ref, begin_ref, span_ref, cube_ref, out_ref, begins_ref, spans_ref, held_ref, lines_sem, cube_sem,
):
    width = cube_ref.shape[0]
    owners = out_ref.shape[0]
    device = device_ref[0]

    def tile_copy(i):
        lanes = pl.ds(pl.multiple_of(i * LANES, LANES), LANES)
        return pltpu.make_async_copy(cube_ref.at[:, lanes], held_ref.at[i], cube_sem.at[i])

    line_copies = [
        pltpu.make_async_copy(begin_ref, begins_ref, lines_sem.at[0]),
        pltpu.make_async_copy(span_ref, spans_ref, lines_sem.at[1]),
    ]
    for copy in line_copies:
        copy.start()
    for i in range(owners):
        tile_copy(i).start()
    for copy in line_copies:
        copy.wait()

    def owner(i, carry):
        tile_copy(i).wait()
        lanes = pl.ds(pl.multiple_of(i * LANES, LANES), LANES)
        sums = window_sums(
            lambda row, size: held_ref[i, row : row + size, :],
            width,
            device * width,
            begins_ref[:, lanes],
            spans_ref[:, lanes],
        )
        for r, value in enumerate(sums):
            out_ref[i, r : r + 1, :] = value
        return carry

    lax.fori_loop(0, owners, owner, 0)


def cube_windows(device, begin, span, cube, devices):
    hbm = pl.BlockSpec(memory_space=pltpu.HBM)
    return pl.pallas_call(
        cube_kernel,
        in_specs=[pl.BlockSpec(memory_space=pltpu.SMEM), hbm, hbm, hbm],
        out_shape=jax.ShapeDtypeStruct((devices, 3 * begin.shape[0], LANES), F32),
        scratch_shapes=[
            pltpu.VMEM(begin.shape, jnp.int32),
            pltpu.VMEM(span.shape, jnp.int32),
            pltpu.VMEM((devices, cube.shape[0], LANES), F32),
            pltpu.SemaphoreType.DMA((2,)),
            pltpu.SemaphoreType.DMA((devices,)),
        ],
        compiler_params=pltpu.CompilerParams(vmem_limit_bytes=VMEM_LIMIT),
        name="cube_windows",
    )(device, begin, span, cube)


def add_kernel(x_ref, y_ref, out_ref):
    out_ref[...] = x_ref[...] + y_ref[...]


def pack_kernel(received_ref, sums_ref, out_ref):
    slots = received_ref.shape[1]
    for half in range(2):
        total = received_ref[half]
        for i in range(half + 2, received_ref.shape[0], 2):
            total = total + received_ref[i]
        for i in range(half, out_ref.shape[0], 2):
            out_ref[i, :slots, :] = total
    out_ref[:, slots:, :] = sums_ref[...]


def owner_kernel(
    device_ref, bins_ref, owner_ref, begin_ref, span_ref, near_ref, far_ref, inverse_ref, hi_ref, mid_ref, low_ref,
    weights_ref, out_ref,
    continuum_ref, bins_held_ref, owner_held_ref, begins_ref, spans_ref, starts_ref, small_sem,
    *, chunk,
):
    devices = near_ref.shape[0]
    slots = weights_ref.shape[0]
    own = bins_held_ref.shape[1]
    lines = begin_ref.shape[0]
    full_width = hi_ref.shape[1]
    device = device_ref[0]
    own_lanes = pl.ds(pl.multiple_of(device * own, LANES), own)

    small_copies = [
        pltpu.make_async_copy(bins_ref.at[:, own_lanes], bins_held_ref, small_sem.at[0]),
        pltpu.make_async_copy(owner_ref, owner_held_ref, small_sem.at[1]),
        pltpu.make_async_copy(begin_ref.at[:, own_lanes], begins_ref, small_sem.at[2]),
        pltpu.make_async_copy(span_ref.at[:, own_lanes], spans_ref, small_sem.at[3]),
        pltpu.make_async_copy(begin_ref.at[:, own_lanes], starts_ref, small_sem.at[4]),
    ]
    for small in small_copies:
        small.start()

    low_first = device % 2 == 0

    def halves(near, far):
        return jnp.where(low_first, near, far), jnp.where(low_first, far, near)

    mine = jnp.concatenate(halves(near_ref[device, :slots, :], far_ref[device, :slots, :]), axis=1)
    inverse = inverse_ref[...]
    weights_ref[...] = dot_f32(mine, inverse, NN)

    for small in small_copies:
        small.wait()
    bins = jnp.broadcast_to(bins_held_ref[...], (SUB, own)).T[:, :1]
    member = jnp.where(bins == owner_held_ref[...], 1.0, 0.0).astype(BF16)
    picked = []
    for half in (near_ref, far_ref):
        hi, mid, low = split3(half[:, :slots, :].reshape(devices * slots, LANES))
        picked.append(dot(member, hi, NN) + (dot(member, mid, NN) + dot(member, low, NN)))
    spaxel_weights = dot_f32(jnp.concatenate(halves(*picked), axis=1), inverse, NN)
    hi, mid, low = split3(spaxel_weights)

    for i in range(full_width // chunk):
        lanes = slice(i * chunk, (i + 1) * chunk)
        first, second, third = hi_ref[:, lanes], mid_ref[:, lanes], low_ref[:, lanes]
        value = dot(hi, first, NN) + (
            (dot(mid, first, NN) + dot(hi, second, NN))
            + (dot(low, first, NN) + dot(mid, second, NN) + dot(hi, third, NN))
        )
        for t in range(chunk // LANES):
            continuum_ref[i * (chunk // LANES) + t] = value[:, t * LANES : (t + 1) * LANES]
    continuum_ref[full_width // LANES] = jnp.zeros((own, LANES), F32)

    begin = begins_ref[...]
    span = spans_ref[...].astype(F32)
    centre = 2.0 * (begin & (LANES - 1)).astype(F32) + span - 1.0
    rows_at = lax.broadcasted_iota(jnp.int32, (SUB, LANES), 0)
    at_row = [rows_at == r for r in range(SUB)]
    twice = 2.0 * lax.broadcasted_iota(jnp.int32, (LANES, own), 0).astype(F32)
    sums = [None] * (3 * lines)
    for j in range(lines):
        picks = ([], [])
        for g in range(own // SUB):
            rows = slice(g * SUB, (g + 1) * SUB)
            left = right = None
            for r in range(SUB):
                tile = lax.shift_right_logical(starts_ref[j, g * SUB + r], 7)
                a = continuum_ref[tile, rows, :]
                b = continuum_ref[tile + 1, rows, :]
                left = a if left is None else jnp.where(at_row[r], a, left)
                right = b if right is None else jnp.where(at_row[r], b, right)
            picks[0].append(left)
            picks[1].append(right)
        terms = None
        for side in range(2):
            block = jnp.concatenate(picks[side], axis=0).T
            m = twice + (2.0 * LANES * side - centre[j : j + 1])
            masked = jnp.where(jnp.abs(m) < span[j : j + 1], block, 0.0)
            weighted = masked * m
            new = [masked, weighted, weighted * m]
            terms = new if terms is None else [x + y for x, y in zip(terms, new)]
        for k in range(3):
            sums[k * lines + j] = jnp.sum(terms[k], axis=0, keepdims=True)
    continuum_sums = jnp.concatenate(sums, axis=0)

    cube_sums = near_ref[0, slots:, :]
    for i in range(1, devices):
        cube_sums = cube_sums + near_ref[i, slots:, :]
    scale = jnp.concatenate([span, span * span, span * span * span], axis=0)
    out_ref[...] = (cube_sums - continuum_sums) / scale


def owned(device, bins, owner, begin, span, near, far, inverse, parts, own_slots, own, chunk):
    vmem = pl.BlockSpec(memory_space=pltpu.VMEM)
    hbm = pl.BlockSpec(memory_space=pltpu.HBM)
    count, full_width = parts[0].shape
    lines = begin.shape[0]
    return pl.pallas_call(
        functools.partial(owner_kernel, chunk=chunk),
        in_specs=[pl.BlockSpec(memory_space=pltpu.SMEM)] + [hbm] * 4 + [vmem] * 6,
        out_shape=(
            jax.ShapeDtypeStruct((own_slots, count), F32),
            jax.ShapeDtypeStruct((3 * lines, own), F32),
        ),
        scratch_shapes=[
            pltpu.VMEM((full_width // LANES + 1, own, LANES), F32),
            pltpu.VMEM((1, own), jnp.int32),
            pltpu.VMEM(owner.shape, jnp.int32),
            pltpu.VMEM((lines, own), jnp.int32),
            pltpu.VMEM((lines, own), jnp.int32),
            pltpu.SMEM((lines, own), jnp.int32),
            pltpu.SemaphoreType.DMA((5,)),
        ],
        compiler_params=pltpu.CompilerParams(vmem_limit_bytes=VMEM_LIMIT),
        name="owned",
    )(device, bins, owner, begin, span, near, far, inverse, *parts)


def shards(cube, templates, bin_id, owner_bins, line_start, line_width):
    devices = lax.axis_size("spax")
    device = lax.axis_index("spax")
    spaxels = cube.shape[0]
    total_bins = owner_bins.shape[0]
    count = templates.shape[0]
    own_spaxels = spaxels // devices
    own_slots = total_bins // devices
    here = device.reshape(1).astype(jnp.int32)
    pin = lambda x: pltpu.with_memory_space_constraint(x, pltpu.HBM)
    raw_templates = templates
    templates, columns = pin(templates), pin(cube.T)
    begin, span = pin(line_start), pin(line_width)
    bins, owner = pin(bin_id[None, :]), pin(owner_bins[None, :])

    swap = [(d, d ^ 1) for d in range(devices)]
    keep, send = project(here, bins, owner, columns, templates)
    swapped = lax.ppermute(send, "spax", swap)
    partial = in_vmem(add_kernel, jax.ShapeDtypeStruct(keep.shape, F32), "add", keep, swapped)
    partial, here_after, later = lax.optimization_barrier((partial, here, raw_templates))
    later = pin(later)
    received = lax.all_to_all(partial.reshape(devices, own_slots, LANES), "spax", 0, 0)

    sums = cube_windows(here_after, begin, span, columns, devices)
    gram, scale, *parts = scaled_gram(later, 512)
    received, sums, gram, scale = lax.optimization_barrier((received, sums, gram, scale))
    parcel = in_vmem(
        pack_kernel,
        jax.ShapeDtypeStruct((devices, own_slots + sums.shape[1], LANES), F32),
        "pack",
        received,
        sums,
    )
    parcel, gram, scale = lax.optimization_barrier((parcel, gram, scale))
    near = lax.all_to_all(parcel, "spax", 0, 0)
    inverse = in_vmem(invert_kernel, jax.ShapeDtypeStruct((count, count), F32), "invert", gram, scale)
    near, inverse = lax.optimization_barrier((near, inverse))
    far = lax.ppermute(near, "spax", swap)
    return owned(
        here, bins, owner, begin, span, near, far, inverse, parts, own_slots, own_spaxels, 512
    )


def solution(mesh):
    placed = (
        P("strips", "spax"),
        P(),
        P("strips"),
        P("strips"),
        P(None, "strips"),
        P(None, "strips"),
    )
    return jax.shard_map(
        shards,
        mesh=mesh,
        in_specs=placed,
        out_specs=(P(("strips", "spax"), None), P(None, ("strips", "spax"))),
        check_vma=False,
    )
```

```python
import functools

import jax
import jax.numpy as jnp
from jax import lax
from jax.experimental import pallas as pl
from jax.experimental.pallas import tpu as pltpu
from jax.sharding import PartitionSpec as P

HIGHEST = lax.Precision.HIGHEST
F32 = jnp.float32
BF16 = jnp.bfloat16
LANES = 128
SUB = 8
VMEM_LIMIT = 20 * 1024 * 1024

NT = (((1,), (1,)), ((), ()))
NN = (((1,), (0,)), ((), ()))


def split3(x):
    hi = x.astype(BF16)
    rest = x - hi.astype(F32)
    mid = rest.astype(BF16)
    low = (rest - mid.astype(F32)).astype(BF16)
    return hi, mid, low


def dot(a, b, dims):
    return lax.dot_general(a, b, dims, preferred_element_type=F32)


def dot_f32(a, b, dims):
    return lax.dot_general(a, b, dims, precision=HIGHEST, preferred_element_type=F32)


def template_window(width, full_width):
    return min(full_width, -(-(width + LANES - 1) // LANES) * LANES)


def project_kernel(
    device_ref, bins_ref, owner_ref, cube_ref, templates_ref, keep_ref, send_ref,
    held_ref, window_ref, member_ref, bins_held_ref, owner_held_ref, cube_sem, window_sem, small_sem, *, chunk,
):
    width, spaxels = cube_ref.shape
    slots = keep_ref.shape[0]
    full_width = templates_ref.shape[1]
    first = device_ref[0] * width
    window = window_ref.shape[1]
    base = pl.multiple_of(jnp.minimum(first // LANES * LANES, full_width - window), LANES)
    chunks = spaxels // chunk

    def cube_copy(i):
        lanes = pl.ds(i * chunk, chunk)
        return pltpu.make_async_copy(cube_ref.at[:, lanes], held_ref.at[:, lanes], cube_sem.at[i])

    window_copy = pltpu.make_async_copy(templates_ref.at[:, pl.ds(base, window)], window_ref, window_sem)

    small_copies = [
        pltpu.make_async_copy(bins_ref, bins_held_ref, small_sem.at[0]),
        pltpu.make_async_copy(owner_ref, owner_held_ref, small_sem.at[1]),
    ]

    def at_first(action):
        pl.when(pl.program_id(0) == 0)(action)

    @at_first
    def _():
        for copy in small_copies:
            copy.start()
        window_copy.start()
        for i in range(chunks):
            cube_copy(i).start()
        for copy in small_copies:
            copy.wait()

    owner = owner_held_ref[:, pl.ds(pl.multiple_of(pl.program_id(0) * slots, LANES), slots)]
    owner = jnp.broadcast_to(owner, (SUB, slots)).T[:, :1]
    counts = jnp.zeros((slots, LANES), F32)
    for i in range(chunks):
        lanes = slice(i * chunk, (i + 1) * chunk)
        ones = jnp.where(owner == bins_held_ref[:, lanes], 1.0, 0.0)
        for lane in range(0, chunk, LANES):
            counts = counts + ones[:, lane : lane + LANES]
        member_ref[:, lanes] = ones.astype(BF16)
    counts = jnp.sum(counts, axis=1, keepdims=True)

    @at_first
    def _():
        window_copy.wait()

    mine = pltpu.roll(window_ref[...], window - (first - base), 1)[:, :width]

    sums = jnp.zeros((slots, width), F32)
    for i in range(chunks):

        @at_first
        def _(i=i):
            cube_copy(i).wait()

        lanes = slice(i * chunk, (i + 1) * chunk)
        member = member_ref[:, lanes]
        for part in split3(held_ref[:, lanes]):
            sums = sums + dot(member, part, NT)
    means = sums / counts
    projections = dot_f32(means, mine, NT) * (1.0 / full_width)
    low, high = projections[:, :LANES], projections[:, LANES:]
    low_kept = device_ref[0] % 2 == 0
    keep_ref[...] = jnp.where(low_kept, low, high)
    send_ref[...] = jnp.where(low_kept, high, low)


def project(device, bins, owner, cube, templates):
    width, spaxels = cube.shape
    slots = owner.shape[1]
    block = min(slots, 512, max(LANES, 2**20 // spaxels))
    chunk = min(spaxels, 512)
    count, full_width = templates.shape
    return pl.pallas_call(
        functools.partial(project_kernel, chunk=chunk),
        grid=(slots // block,),
        in_specs=[
            pl.BlockSpec(memory_space=pltpu.SMEM),
            pl.BlockSpec(memory_space=pltpu.HBM),
            pl.BlockSpec(memory_space=pltpu.HBM),
            pl.BlockSpec(memory_space=pltpu.HBM),
            pl.BlockSpec(memory_space=pltpu.HBM),
        ],
        out_specs=[pl.BlockSpec((block, LANES), lambda i: (i, 0))] * 2,
        out_shape=[jax.ShapeDtypeStruct((slots, LANES), F32)] * 2,
        scratch_shapes=[
            pltpu.VMEM((width, spaxels), F32),
            pltpu.VMEM((count, template_window(width, full_width)), F32),
            pltpu.VMEM((block, spaxels), BF16),
            pltpu.VMEM(bins.shape, jnp.int32),
            pltpu.VMEM(owner.shape, jnp.int32),
            pltpu.SemaphoreType.DMA((spaxels // chunk,)),
            pltpu.SemaphoreType.DMA,
            pltpu.SemaphoreType.DMA((2,)),
        ],
        compiler_params=pltpu.CompilerParams(vmem_limit_bytes=VMEM_LIMIT),
        name="project",
    )(device, bins, owner, cube, templates)


def reciprocal(x):
    r = pl.reciprocal(x, approx=True)
    r = r * (2.0 - x * r)
    return r * (2.0 - x * r)


def invert_tile(tile):
    size = tile.shape[0]
    count = size // SUB
    lanes = lax.broadcasted_iota(jnp.int32, (SUB, size), 1)
    rows_at = lax.broadcasted_iota(jnp.int32, (SUB, size), 0)
    rows = [tile[i * SUB : (i + 1) * SUB, :] for i in range(count)]
    for k in range(count):
        block = rows[k]
        first = k * SUB
        a = {}
        for i in range(SUB):
            for j in range(i, SUB):
                a[i, j] = jnp.broadcast_to(block[i : i + 1, first + j : first + j + 1], (SUB, size))

        def at(i, j):
            return (i, j) if i <= j else (j, i)

        for p in range(0, SUB, 2):
            q = p + 1
            pp, pq, qq = a[p, p], a[p, q], a[q, q]
            inverse = reciprocal(pp * qq - pq * pq)
            others = [i for i in range(SUB) if i not in (p, q)]
            old = {i: (a[at(i, p)], a[at(i, q)]) for i in others}
            new = {
                i: ((u * qq - v * pq) * inverse, (v * pp - u * pq) * inverse) for i, (u, v) in old.items()
            }
            for i in others:
                for j in others:
                    if i <= j:
                        a[i, j] = a[i, j] - new[i][0] * old[j][0] - new[i][1] * old[j][1]
            for i in others:
                a[at(i, p)], a[at(i, q)] = new[i]
            a[p, p], a[p, q], a[q, q] = -(qq * inverse), pq * inverse, -(pp * inverse)
        columns = []
        for j in range(SUB):
            column = a[at(0, j)]
            for i in range(1, SUB):
                column = jnp.where(rows_at == i, a[at(i, j)], column)
            columns.append(column)
        terms = [columns[j] * jnp.broadcast_to(block[j : j + 1, :], (SUB, size)) for j in range(SUB)]
        while len(terms) > 1:
            terms = [x + y for x, y in zip(terms[::2], terms[1::2])]
        swept = -terms[0]
        for j in range(SUB):
            swept = jnp.where(lanes == first + j, columns[j], swept)
        inside = (lanes >= first) & (lanes < first + SUB)
        spread_rows = [jnp.broadcast_to(swept[j : j + 1, :], (SUB, size)) for j in range(SUB)]
        order = list(range(k + 1, count)) + list(range(k))
        for i in order:
            terms = [
                jnp.broadcast_to(rows[i][:, first + j : first + j + 1], (SUB, size)) * spread_rows[j]
                for j in range(SUB)
            ]
            while len(terms) > 1:
                terms = [x + y for x, y in zip(terms[::2], terms[1::2])]
            rows[i] = jnp.where(inside, 0.0, rows[i]) - terms[0]
        rows[k] = swept
    return -jnp.concatenate(rows, axis=0)


def gram_kernel(
    templates_ref, gram_ref, scale_ref, hi_ref, mid_ref, low_ref, held_ref, mid_held_ref, low_held_ref, sem, out_sem,
    *, chunk,
):
    count, full_width = templates_ref.shape

    def copy(i):
        lanes = pl.ds(i * chunk, chunk)
        return pltpu.make_async_copy(templates_ref.at[:, lanes], held_ref.at[:, lanes], sem.at[i])

    def out_copies(i):
        lanes = pl.ds(i * chunk, chunk)
        return [
            pltpu.make_async_copy(mid_held_ref.at[:, lanes], mid_ref.at[:, lanes], out_sem.at[0, i]),
            pltpu.make_async_copy(low_held_ref.at[:, lanes], low_ref.at[:, lanes], out_sem.at[1, i]),
        ]

    for i in range(full_width // chunk):
        copy(i).start()
    even = jnp.zeros((count, count), F32)
    mixed = jnp.zeros((count, count), F32)
    for i in range(full_width // chunk):
        copy(i).wait()
        lanes = slice(i * chunk, (i + 1) * chunk)
        hi, mid, low = split3(held_ref[:, lanes])
        hi_ref[:, lanes], mid_held_ref[:, lanes], low_held_ref[:, lanes] = hi, mid, low
        for out in out_copies(i):
            out.start()
        even = even + (dot(hi, hi, NT) + dot(mid, mid, NT))
        mixed = mixed + (dot(hi, mid, NT) + dot(hi, low, NT))
    gram = (even + (mixed + mixed.T)) * (1.0 / full_width)
    same = lax.broadcasted_iota(jnp.int32, gram.shape, 0) == lax.broadcasted_iota(jnp.int32, gram.shape, 1)
    diagonal = jnp.where(same, gram, 0.0)
    row = lax.rsqrt(jnp.sum(diagonal, axis=0, keepdims=True))
    column = lax.rsqrt(jnp.sum(diagonal, axis=1, keepdims=True))
    gram = gram * row * column
    scale_ref[...] = row
    gram_ref[...] = gram
    for i in range(full_width // chunk):
        for out in out_copies(i):
            out.wait()


def scaled_gram(templates, chunk):
    count, full_width = templates.shape
    vmem, hbm = (pl.BlockSpec(memory_space=space) for space in (pltpu.VMEM, pltpu.HBM))
    return pl.pallas_call(
        functools.partial(gram_kernel, chunk=chunk),
        in_specs=[hbm],
        out_specs=(vmem, vmem, vmem, hbm, hbm),
        out_shape=(
            jax.ShapeDtypeStruct((count, count), F32),
            jax.ShapeDtypeStruct((1, count), F32),
            pltpu.VMEM((count, full_width), BF16),
            pltpu.HBM((count, full_width), BF16),
            pltpu.HBM((count, full_width), BF16),
        ),
        scratch_shapes=[
            pltpu.VMEM((count, full_width), F32),
            pltpu.VMEM((count, full_width), BF16),
            pltpu.VMEM((count, full_width), BF16),
            pltpu.SemaphoreType.DMA((full_width // chunk,)),
            pltpu.SemaphoreType.DMA((2, full_width // chunk)),
        ],
        compiler_params=pltpu.CompilerParams(vmem_limit_bytes=VMEM_LIMIT),
        name="gram",
    )(templates)


def first_kernel(gram_ref, out_ref):
    out_ref[...] = invert_tile(gram_ref[:LANES, :LANES])


def finish_kernel(gram_ref, first_ref, scale_ref, out_ref):
    first = first_ref[...]
    side = gram_ref[:LANES, LANES:]
    half = dot_f32(first, side, NN)
    schur = gram_ref[LANES:, LANES:] - dot_f32(side.T, half, NN)
    last = invert_tile(schur)
    cross = dot_f32(half, last, NN)
    row = scale_ref[...]
    column = jnp.broadcast_to(row, (SUB, row.shape[1])).T[:, :1]
    near, far = row[:, :LANES], row[:, LANES:]
    out_ref[:LANES, :LANES] = (first + dot_f32(cross, half, NT)) * near * column[:LANES]
    out_ref[:LANES, LANES:] = -cross * far * column[:LANES]
    out_ref[LANES:, :LANES] = -cross.T * near * column[LANES:]
    out_ref[LANES:, LANES:] = last * far * column[LANES:]


def in_vmem(kernel, shapes, name, *arrays):
    return pl.pallas_call(
        kernel,
        out_shape=shapes,
        compiler_params=pltpu.CompilerParams(vmem_limit_bytes=VMEM_LIMIT),
        name=name,
    )(*arrays)


def window_sums(read, rows, first, begin, span):
    lines = begin.shape[0]
    sub = lax.broadcasted_iota(jnp.int32, (SUB, LANES), 0)
    spans = [jnp.broadcast_to(span[j : j + 1], (SUB, LANES)).astype(F32) for j in range(lines)]
    offsets = [
        (2 * (first + sub - jnp.broadcast_to(begin[j : j + 1], (SUB, LANES))) + 1).astype(F32) - spans[j]
        for j in range(lines)
    ]

    def add(block, shift, sums):
        size = block.shape[0]
        out = []
        for j in range(lines):
            m = offsets[j][:size] + shift
            masked = jnp.where(jnp.abs(m) < spans[j][:size], block, 0.0)
            weighted = masked * m
            out += [sums[3 * j] + masked, sums[3 * j + 1] + weighted, sums[3 * j + 2] + weighted * m]
        return out

    full = rows // SUB
    out = [jnp.zeros((1, LANES), F32)] * (3 * lines)
    if full:
        sums = [jnp.zeros((SUB, LANES), F32)] * (3 * lines)
        for i in range(full):
            sums = add(read(i * SUB, SUB), 2.0 * i * SUB, sums)
        out = [jnp.sum(x, axis=0, keepdims=True) for x in sums]
    if rows % SUB:
        sums = [jnp.zeros((rows % SUB, LANES), F32)] * (3 * lines)
        sums = add(read(full * SUB, rows % SUB), 2.0 * full * SUB, sums)
        out = [x + jnp.sum(y, axis=0, keepdims=True) for x, y in zip(out, sums)]
    return [out[3 * j + k] for k in range(3) for j in range(lines)]


def halving_order(devices):
    bits = devices.bit_length() - 1
    return list(range(2, bits)) + [1, 0]


def flips(position, devices):
    order = halving_order(devices)
    return sum(((position >> (len(order) - 1 - t)) & 1) << bit for t, bit in enumerate(order))


def cube_kernel(
    device_ref, begin_ref, span_ref, cube_ref, out_ref, begins_ref, spans_ref, held_ref, lines_sem, cube_sem,
):
    width = cube_ref.shape[0]
    owners = out_ref.shape[0]
    device = device_ref[0]

    def owner_lanes(i):
        return pl.ds(pl.multiple_of((device ^ flips(i, owners)) * LANES, LANES), LANES)

    def tile_copy(i):
        return pltpu.make_async_copy(cube_ref.at[:, owner_lanes(i)], held_ref.at[i], cube_sem.at[i])

    line_copies = [
        pltpu.make_async_copy(begin_ref, begins_ref, lines_sem.at[0]),
        pltpu.make_async_copy(span_ref, spans_ref, lines_sem.at[1]),
    ]
    for copy in line_copies:
        copy.start()
    for i in range(owners):
        tile_copy(i).start()
    for copy in line_copies:
        copy.wait()

    def owner(i, carry):
        tile_copy(i).wait()
        lanes = owner_lanes(i)
        sums = window_sums(
            lambda row, size: held_ref[i, row : row + size, :],
            width,
            device * width,
            begins_ref[:, lanes],
            spans_ref[:, lanes],
        )
        for r, value in enumerate(sums):
            out_ref[i, r : r + 1, :] = value
        return carry

    lax.fori_loop(0, owners, owner, 0)


def cube_windows(device, begin, span, cube, devices):
    hbm = pl.BlockSpec(memory_space=pltpu.HBM)
    return pl.pallas_call(
        cube_kernel,
        in_specs=[pl.BlockSpec(memory_space=pltpu.SMEM), hbm, hbm, hbm],
        out_shape=jax.ShapeDtypeStruct((devices, 3 * begin.shape[0], LANES), F32),
        scratch_shapes=[
            pltpu.VMEM(begin.shape, jnp.int32),
            pltpu.VMEM(span.shape, jnp.int32),
            pltpu.VMEM((devices, cube.shape[0], LANES), F32),
            pltpu.SemaphoreType.DMA((2,)),
            pltpu.SemaphoreType.DMA((devices,)),
        ],
        compiler_params=pltpu.CompilerParams(vmem_limit_bytes=VMEM_LIMIT),
        name="cube_windows",
    )(device, begin, span, cube)


def split_kernel(device_ref, x_ref, y_ref, keep_ref, send_ref):
    half = keep_ref.shape[0]
    total = x_ref[...] + y_ref[...]
    low_kept = (device_ref[0] >> 1) % 2 == 0
    keep_ref[...] = jnp.where(low_kept, total[:half], total[half:])
    send_ref[...] = jnp.where(low_kept, total[half:], total[:half])


def join_kernel(x_ref, y_ref, sums_ref, keep_ref, send_ref):
    slots = x_ref.shape[0]
    half = sums_ref.shape[0] // 2
    total = x_ref[...] + y_ref[...]
    for out_ref, first in ((keep_ref, 0), (send_ref, half)):
        out_ref[:slots, :] = total
        out_ref[slots:, :] = sums_ref[first : first + half, :]


def step_kernel(x_ref, y_ref, keep_ref, send_ref):
    rows = x_ref.shape[0]
    half = rows - keep_ref.shape[0]
    slots = rows - 2 * half
    total = x_ref[:slots, :] + y_ref[:slots, :]
    for out_ref, first in ((keep_ref, slots), (send_ref, slots + half)):
        out_ref[:slots, :] = total
        out_ref[slots:, :] = x_ref[first : first + half, :] + y_ref[first : first + half, :]


def rows_of(count):
    return jax.ShapeDtypeStruct((count, LANES), F32)


def split_slots(device, x, y):
    vmem = pl.BlockSpec(memory_space=pltpu.VMEM)
    half = rows_of(x.shape[0] // 2)
    return pl.pallas_call(
        split_kernel,
        in_specs=[pl.BlockSpec(memory_space=pltpu.SMEM), vmem, vmem],
        out_shape=(half, half),
        compiler_params=pltpu.CompilerParams(vmem_limit_bytes=VMEM_LIMIT),
        name="split_slots",
    )(device, x, y)


def owner_kernel(
    device_ref, bins_ref, owner_ref, begin_ref, span_ref,
    kept_ref, by_x_ref, by_core_ref, by_both_ref, inverse_ref, hi_ref, mid_ref, low_ref,
    weights_ref, out_ref,
    continuum_ref, mid_held_ref, low_held_ref, bins_held_ref, owner_held_ref, begins_ref, spans_ref, starts_ref,
    parts_sem, small_sem, *, chunk,
):
    own_slots = weights_ref.shape[0]
    own = bins_held_ref.shape[1]
    lines = begin_ref.shape[0]
    full_width = hi_ref.shape[1]
    half = owner_held_ref.shape[1] // 2
    device = device_ref[0]
    own_lanes = pl.ds(pl.multiple_of(device * own, LANES), own)

    small_copies = [
        pltpu.make_async_copy(bins_ref.at[:, own_lanes], bins_held_ref, small_sem.at[0]),
        pltpu.make_async_copy(owner_ref, owner_held_ref, small_sem.at[1]),
        pltpu.make_async_copy(begin_ref.at[:, own_lanes], begins_ref, small_sem.at[2]),
        pltpu.make_async_copy(span_ref.at[:, own_lanes], spans_ref, small_sem.at[3]),
        pltpu.make_async_copy(begin_ref.at[:, own_lanes], starts_ref, small_sem.at[4]),
    ]
    part_copies = [
        pltpu.make_async_copy(mid_ref, mid_held_ref, parts_sem.at[0]),
        pltpu.make_async_copy(low_ref, low_held_ref, parts_sem.at[1]),
    ]
    for copy in small_copies + part_copies:
        copy.start()

    inverse = inverse_ref[...]
    core_low = device % 2 == 0
    low_kept = (device >> 1) % 2 == 0

    def by_lanes(near, far):
        return jnp.concatenate([jnp.where(core_low, near, far), jnp.where(core_low, far, near)], axis=1)

    slot = device * own_slots
    in_kept = (slot // half) == ((device >> 1) % 2)
    rows = pl.ds(pl.multiple_of(slot % half, own_slots), own_slots)
    mine = by_lanes(
        jnp.where(in_kept, kept_ref[rows, :], by_x_ref[rows, :]),
        jnp.where(in_kept, by_core_ref[rows, :], by_both_ref[rows, :]),
    )
    weights_ref[...] = dot_f32(mine, inverse, NN)

    for copy in small_copies:
        copy.wait()
    bins = jnp.broadcast_to(bins_held_ref[...], (SUB, own)).T[:, :1]
    low_slots, high_slots = owner_held_ref[:, :half], owner_held_ref[:, half:]
    members = [
        jnp.where(bins == jnp.where(low_kept, a, b), 1.0, 0.0).astype(BF16)
        for a, b in ((low_slots, high_slots), (high_slots, low_slots))
    ]
    picked = []
    for kept_half, other_half in ((kept_ref, by_x_ref), (by_core_ref, by_both_ref)):
        value = None
        for member, block in zip(members, (kept_half, other_half)):
            hi, mid, low = split3(block[:half, :])
            new = dot(member, hi, NN) + (dot(member, mid, NN) + dot(member, low, NN))
            value = new if value is None else value + new
        picked.append(value)
    spaxel_weights = dot_f32(by_lanes(*picked), inverse, NN)

    hi, mid, low = split3(spaxel_weights)
    tiles = chunk // LANES
    for i in range(full_width // chunk):
        first = hi_ref[:, i * chunk : (i + 1) * chunk]
        value = dot(hi, first, NN) + (dot(mid, first, NN) + dot(low, first, NN))
        for t in range(tiles):
            continuum_ref[i * tiles + t] = value[:, t * LANES : (t + 1) * LANES]
    for copy in part_copies:
        copy.wait()
    for i in range(full_width // chunk):
        lanes = slice(i * chunk, (i + 1) * chunk)
        second, third = mid_held_ref[:, lanes], low_held_ref[:, lanes]
        value = dot(hi, second, NN) + (dot(mid, second, NN) + dot(hi, third, NN))
        for t in range(tiles):
            continuum_ref[i * tiles + t] += value[:, t * LANES : (t + 1) * LANES]
    continuum_ref[full_width // LANES] = jnp.zeros((own, LANES), F32)

    begin = begins_ref[...]
    span = spans_ref[...].astype(F32)
    centre = 2.0 * (begin & (LANES - 1)).astype(F32) + span - 1.0
    rows_at = lax.broadcasted_iota(jnp.int32, (SUB, LANES), 0)
    at_row = [rows_at == r for r in range(SUB)]
    twice = 2.0 * lax.broadcasted_iota(jnp.int32, (LANES, own), 0).astype(F32)
    sums = [None] * (3 * lines)
    for j in range(lines):
        picks = ([], [])
        for g in range(own // SUB):
            rows = slice(g * SUB, (g + 1) * SUB)
            left = right = None
            for r in range(SUB):
                tile = lax.shift_right_logical(starts_ref[j, g * SUB + r], 7)
                a = continuum_ref[tile, rows, :]
                b = continuum_ref[tile + 1, rows, :]
                left = a if left is None else jnp.where(at_row[r], a, left)
                right = b if right is None else jnp.where(at_row[r], b, right)
            picks[0].append(left)
            picks[1].append(right)
        terms = None
        for side in range(2):
            block = jnp.concatenate(picks[side], axis=0).T
            m = twice + (2.0 * LANES * side - centre[j : j + 1])
            masked = jnp.where(jnp.abs(m) < span[j : j + 1], block, 0.0)
            weighted = masked * m
            new = [masked, weighted, weighted * m]
            terms = new if terms is None else [x + y for x, y in zip(terms, new)]
        for k in range(3):
            sums[k * lines + j] = jnp.sum(terms[k], axis=0, keepdims=True)
    continuum_sums = jnp.concatenate(sums, axis=0)

    own_rows = slice(half, half + 3 * lines)
    other_rows = slice(half + 3 * lines, half + 6 * lines)
    cube_sums = (kept_ref[own_rows, :] + by_x_ref[own_rows, :]) + (
        by_core_ref[other_rows, :] + by_both_ref[other_rows, :]
    )
    scale = jnp.concatenate([span, span * span, span * span * span], axis=0)
    out_ref[...] = (cube_sums - continuum_sums) / scale


def owned(device, bins, owner, begin, span, messages, inverse, parts, own_slots, own, chunk):
    vmem = pl.BlockSpec(memory_space=pltpu.VMEM)
    hbm = pl.BlockSpec(memory_space=pltpu.HBM)
    count, full_width = parts[0].shape
    lines = begin.shape[0]
    return pl.pallas_call(
        functools.partial(owner_kernel, chunk=chunk),
        in_specs=[pl.BlockSpec(memory_space=pltpu.SMEM)] + [hbm] * 4 + [vmem] * 6 + [hbm] * 2,
        out_shape=(
            jax.ShapeDtypeStruct((own_slots, count), F32),
            jax.ShapeDtypeStruct((3 * lines, own), F32),
        ),
        scratch_shapes=[
            pltpu.VMEM((full_width // LANES + 1, own, LANES), F32),
            pltpu.VMEM((count, full_width), BF16),
            pltpu.VMEM((count, full_width), BF16),
            pltpu.VMEM((1, own), jnp.int32),
            pltpu.VMEM(owner.shape, jnp.int32),
            pltpu.VMEM((lines, own), jnp.int32),
            pltpu.VMEM((lines, own), jnp.int32),
            pltpu.SMEM((lines, own), jnp.int32),
            pltpu.SemaphoreType.DMA((2,)),
            pltpu.SemaphoreType.DMA((5,)),
        ],
        compiler_params=pltpu.CompilerParams(vmem_limit_bytes=VMEM_LIMIT),
        name="owned",
    )(device, bins, owner, begin, span, *messages, inverse, *parts)


def shards(cube, templates, bin_id, owner_bins, line_start, line_width):
    devices = lax.axis_size("spax")
    device = lax.axis_index("spax")
    spaxels = cube.shape[0]
    total_bins = owner_bins.shape[0]
    count = templates.shape[0]
    lines = line_start.shape[0]
    own_spaxels = spaxels // devices
    own_slots = total_bins // devices
    here = device.reshape(1).astype(jnp.int32)
    pin = lambda x: pltpu.with_memory_space_constraint(x, pltpu.HBM)
    columns = pin(cube.T)
    begin, span = pin(line_start), pin(line_width)
    bins, owner = pin(bin_id[None, :]), pin(owner_bins[None, :])
    after = lax.optimization_barrier

    def swap(x, bit):
        return lax.ppermute(x, "spax", [(d, d ^ (1 << bit)) for d in range(devices)])

    keep, send = project(here, bins, owner, columns, pin(templates))
    keep, send = split_slots(here, keep, swap(send, 0))
    keep, send, now = after((keep, send, here))
    arrived = swap(send, 1)
    sums = cube_windows(now, begin, span, columns, devices)
    sums = sums.reshape(devices * 3 * lines, LANES)
    keep, arrived, sums, templates = after((keep, arrived, sums, templates))
    slots, extra = total_bins // 2, devices * 3 * lines // 2
    message = rows_of(slots + extra)
    keep, send = in_vmem(join_kernel, (message, message), "join", keep, arrived, sums)

    keep, send, templates = after((keep, send, templates))
    gram = scale = first = None
    for bit in range(2, devices.bit_length() - 1):
        arrived = swap(send, bit)
        if gram is None:
            gram, scale, *parts = scaled_gram(pin(templates), 512)
            arrived, gram = after((arrived, gram))
        elif first is None:
            first = in_vmem(first_kernel, jax.ShapeDtypeStruct((LANES, LANES), F32), "first", gram)
            arrived, first = after((arrived, first))
        extra //= 2
        message = rows_of(slots + extra)
        keep, send = in_vmem(step_kernel, (message, message), "step", keep, arrived)
        if first is None:
            keep, send, gram = after((keep, send, gram))
        else:
            keep, send, first = after((keep, send, first))

    by_x = swap(send, 1)
    by_core = swap(keep, 0)
    inverse = in_vmem(finish_kernel, jax.ShapeDtypeStruct((count, count), F32), "finish", gram, first, scale)
    by_x, by_core, inverse = after((by_x, by_core, inverse))
    by_both = swap(by_x, 0)
    messages = (keep, by_x, by_core, by_both)
    parts = [parts[0], pin(parts[1]), pin(parts[2])]
    return owned(here, bins, owner, begin, span, messages, inverse, parts, own_slots, own_spaxels, 512)


def solution(mesh):
    placed = (
        P("strips", "spax"),
        P(),
        P("strips"),
        P("strips"),
        P(None, "strips"),
        P(None, "strips"),
    )
    return jax.shard_map(
        shards,
        mesh=mesh,
        in_specs=placed,
        out_specs=(P(("strips", "spax"), None), P(None, ("strips", "spax"))),
        check_vma=False,
    )
```

```python
import functools

import jax
import jax.numpy as jnp
from jax import lax
from jax.experimental import pallas as pl
from jax.experimental.pallas import tpu as pltpu
from jax.sharding import PartitionSpec as P

HIGHEST = lax.Precision.HIGHEST
F32 = jnp.float32
BF16 = jnp.bfloat16
LANES = 128
SUB = 8
VMEM_LIMIT = 20 * 1024 * 1024

NT = (((1,), (1,)), ((), ()))
NN = (((1,), (0,)), ((), ()))


def split3(x):
    hi = x.astype(BF16)
    rest = x - hi.astype(F32)
    mid = rest.astype(BF16)
    low = (rest - mid.astype(F32)).astype(BF16)
    return hi, mid, low


def dot(a, b, dims):
    return lax.dot_general(a, b, dims, preferred_element_type=F32)


def dot_f32(a, b, dims):
    return lax.dot_general(a, b, dims, precision=HIGHEST, preferred_element_type=F32)


def template_window(width, full_width):
    return min(full_width, -(-(width + LANES - 1) // LANES) * LANES)


def project_kernel(
    device_ref, bins_ref, owner_ref, begin_ref, span_ref, cube_ref, templates_ref,
    keep_ref, send_ref, begins_ref, spans_ref, held_ref,
    window_ref, member_ref, bins_held_ref, owner_held_ref, cube_sem, window_sem, small_sem, *, chunk,
):
    width, spaxels = cube_ref.shape
    slots = keep_ref.shape[0]
    full_width = templates_ref.shape[1]
    first = device_ref[0] * width
    window = window_ref.shape[1]
    base = pl.multiple_of(jnp.minimum(first // LANES * LANES, full_width - window), LANES)
    chunks = spaxels // chunk

    def cube_copy(i):
        lanes = pl.ds(i * chunk, chunk)
        return pltpu.make_async_copy(cube_ref.at[:, lanes], held_ref.at[:, lanes], cube_sem.at[i])

    window_copy = pltpu.make_async_copy(templates_ref.at[:, pl.ds(base, window)], window_ref, window_sem)

    small_copies = [
        pltpu.make_async_copy(bins_ref, bins_held_ref, small_sem.at[0]),
        pltpu.make_async_copy(owner_ref, owner_held_ref, small_sem.at[1]),
    ]

    line_copies = [
        pltpu.make_async_copy(begin_ref, begins_ref, small_sem.at[2]),
        pltpu.make_async_copy(span_ref, spans_ref, small_sem.at[3]),
    ]

    def at_first(action):
        pl.when(pl.program_id(0) == 0)(action)

    @at_first
    def _():
        for copy in small_copies:
            copy.start()
        window_copy.start()
        for i in range(chunks):
            cube_copy(i).start()
        for copy in line_copies:
            copy.start()
        for copy in small_copies:
            copy.wait()

    owner = owner_held_ref[:, pl.ds(pl.multiple_of(pl.program_id(0) * slots, LANES), slots)]
    owner = jnp.broadcast_to(owner, (SUB, slots)).T[:, :1]
    counts = jnp.zeros((slots, LANES), F32)
    for i in range(chunks):
        lanes = slice(i * chunk, (i + 1) * chunk)
        ones = jnp.where(owner == bins_held_ref[:, lanes], 1.0, 0.0)
        for lane in range(0, chunk, LANES):
            counts = counts + ones[:, lane : lane + LANES]
        member_ref[:, lanes] = ones.astype(BF16)
    counts = jnp.sum(counts, axis=1, keepdims=True)

    @at_first
    def _():
        window_copy.wait()

    mine = pltpu.roll(window_ref[...], window - (first - base), 1)[:, :width]

    sums = jnp.zeros((slots, width), F32)
    for i in range(chunks):

        @at_first
        def _(i=i):
            cube_copy(i).wait()

        lanes = slice(i * chunk, (i + 1) * chunk)
        member = member_ref[:, lanes]
        for part in split3(held_ref[:, lanes]):
            sums = sums + dot(member, part, NT)
    means = sums / counts

    @at_first
    def _():
        for copy in line_copies:
            copy.wait()

    projections = dot_f32(means, mine, NT) * (1.0 / full_width)
    low, high = projections[:, :LANES], projections[:, LANES:]
    low_kept = device_ref[0] % 2 == 0
    keep_ref[...] = jnp.where(low_kept, low, high)
    send_ref[...] = jnp.where(low_kept, high, low)


def project(device, bins, owner, begin, span, cube, templates):
    width, spaxels = cube.shape
    slots = owner.shape[1]
    block = min(slots, 512, max(LANES, 2**20 // spaxels))
    chunk = min(spaxels, 512)
    count, full_width = templates.shape
    return pl.pallas_call(
        functools.partial(project_kernel, chunk=chunk),
        grid=(slots // block,),
        in_specs=[
            pl.BlockSpec(memory_space=pltpu.SMEM),
        ]
        + [pl.BlockSpec(memory_space=pltpu.HBM)] * 6,
        out_specs=[pl.BlockSpec((block, LANES), lambda i: (i, 0))] * 2 + [pl.BlockSpec(memory_space=pltpu.VMEM)] * 3,
        out_shape=[
            jax.ShapeDtypeStruct((slots, LANES), F32),
            jax.ShapeDtypeStruct((slots, LANES), F32),
            pltpu.VMEM(begin.shape, jnp.int32),
            pltpu.VMEM(span.shape, jnp.int32),
            pltpu.VMEM((width, spaxels), F32),
        ],
        scratch_shapes=[
            pltpu.VMEM((count, template_window(width, full_width)), F32),
            pltpu.VMEM((block, spaxels), BF16),
            pltpu.VMEM(bins.shape, jnp.int32),
            pltpu.VMEM(owner.shape, jnp.int32),
            pltpu.SemaphoreType.DMA((spaxels // chunk,)),
            pltpu.SemaphoreType.DMA,
            pltpu.SemaphoreType.DMA((4,)),
        ],
        compiler_params=pltpu.CompilerParams(vmem_limit_bytes=VMEM_LIMIT),
        name="project",
    )(device, bins, owner, begin, span, cube, templates)


def reciprocal(x):
    r = pl.reciprocal(x, approx=True)
    r = r * (2.0 - x * r)
    return r * (2.0 - x * r)


def eliminate(tile, start, stop):
    size = tile.shape[0]
    count = size // SUB
    lanes = lax.broadcasted_iota(jnp.int32, (SUB, size), 1)
    rows_at = lax.broadcasted_iota(jnp.int32, (SUB, size), 0)
    rows = [tile[i * SUB : (i + 1) * SUB, :] for i in range(count)]
    for k in range(start, stop):
        block = rows[k]
        first = k * SUB
        a = {}
        for i in range(SUB):
            for j in range(i, SUB):
                a[i, j] = jnp.broadcast_to(block[i : i + 1, first + j : first + j + 1], (SUB, size))

        def at(i, j):
            return (i, j) if i <= j else (j, i)

        for p in range(0, SUB, 2):
            q = p + 1
            pp, pq, qq = a[p, p], a[p, q], a[q, q]
            inverse = reciprocal(pp * qq - pq * pq)
            others = [i for i in range(SUB) if i not in (p, q)]
            old = {i: (a[at(i, p)], a[at(i, q)]) for i in others}
            new = {
                i: ((u * qq - v * pq) * inverse, (v * pp - u * pq) * inverse) for i, (u, v) in old.items()
            }
            for i in others:
                for j in others:
                    if i <= j:
                        a[i, j] = a[i, j] - new[i][0] * old[j][0] - new[i][1] * old[j][1]
            for i in others:
                a[at(i, p)], a[at(i, q)] = new[i]
            a[p, p], a[p, q], a[q, q] = -(qq * inverse), pq * inverse, -(pp * inverse)
        columns = []
        for j in range(SUB):
            column = a[at(0, j)]
            for i in range(1, SUB):
                column = jnp.where(rows_at == i, a[at(i, j)], column)
            columns.append(column)
        terms = [columns[j] * jnp.broadcast_to(block[j : j + 1, :], (SUB, size)) for j in range(SUB)]
        while len(terms) > 1:
            terms = [x + y for x, y in zip(terms[::2], terms[1::2])]
        swept = -terms[0]
        for j in range(SUB):
            swept = jnp.where(lanes == first + j, columns[j], swept)
        inside = (lanes >= first) & (lanes < first + SUB)
        spread_rows = [jnp.broadcast_to(swept[j : j + 1, :], (SUB, size)) for j in range(SUB)]
        order = list(range(k + 1, count)) + list(range(k))
        for i in order:
            terms = [
                jnp.broadcast_to(rows[i][:, first + j : first + j + 1], (SUB, size)) * spread_rows[j]
                for j in range(SUB)
            ]
            while len(terms) > 1:
                terms = [x + y for x, y in zip(terms[::2], terms[1::2])]
            rows[i] = jnp.where(inside, 0.0, rows[i]) - terms[0]
        rows[k] = swept
    return jnp.concatenate(rows, axis=0)


def gram_kernel(
    templates_ref, gram_ref, scale_ref, hi_ref, mid_ref, low_ref, held_ref, mid_held_ref, low_held_ref, sem, out_sem,
    *, chunk,
):
    count, full_width = templates_ref.shape

    def copy(i):
        lanes = pl.ds(i * chunk, chunk)
        return pltpu.make_async_copy(templates_ref.at[:, lanes], held_ref.at[:, lanes], sem.at[i])

    def out_copies(i):
        lanes = pl.ds(i * chunk, chunk)
        return [
            pltpu.make_async_copy(mid_held_ref.at[:, lanes], mid_ref.at[:, lanes], out_sem.at[0, i]),
            pltpu.make_async_copy(low_held_ref.at[:, lanes], low_ref.at[:, lanes], out_sem.at[1, i]),
        ]

    for i in range(full_width // chunk):
        copy(i).start()
    even = jnp.zeros((count, count), F32)
    mixed = jnp.zeros((count, count), F32)
    for i in range(full_width // chunk):
        copy(i).wait()
        lanes = slice(i * chunk, (i + 1) * chunk)
        hi, mid, low = split3(held_ref[:, lanes])
        hi_ref[:, lanes], mid_held_ref[:, lanes], low_held_ref[:, lanes] = hi, mid, low
        for out in out_copies(i):
            out.start()
        even = even + (dot(hi, hi, NT) + dot(mid, mid, NT))
        mixed = mixed + (dot(hi, mid, NT) + dot(hi, low, NT))
    gram = (even + (mixed + mixed.T)) * (1.0 / full_width)
    same = lax.broadcasted_iota(jnp.int32, gram.shape, 0) == lax.broadcasted_iota(jnp.int32, gram.shape, 1)
    diagonal = jnp.where(same, gram, 0.0)
    row = lax.rsqrt(jnp.sum(diagonal, axis=0, keepdims=True))
    column = lax.rsqrt(jnp.sum(diagonal, axis=1, keepdims=True))
    gram = gram * row * column
    scale_ref[...] = row
    gram_ref[...] = gram
    for i in range(full_width // chunk):
        for out in out_copies(i):
            out.wait()


def scaled_gram(templates, chunk):
    count, full_width = templates.shape
    vmem, hbm = (pl.BlockSpec(memory_space=space) for space in (pltpu.VMEM, pltpu.HBM))
    return pl.pallas_call(
        functools.partial(gram_kernel, chunk=chunk),
        in_specs=[hbm],
        out_specs=(vmem, vmem, vmem, hbm, hbm),
        out_shape=(
            jax.ShapeDtypeStruct((count, count), F32),
            jax.ShapeDtypeStruct((1, count), F32),
            pltpu.VMEM((count, full_width), BF16),
            pltpu.HBM((count, full_width), BF16),
            pltpu.HBM((count, full_width), BF16),
        ),
        scratch_shapes=[
            pltpu.VMEM((count, full_width), F32),
            pltpu.VMEM((count, full_width), BF16),
            pltpu.VMEM((count, full_width), BF16),
            pltpu.SemaphoreType.DMA((full_width // chunk,)),
            pltpu.SemaphoreType.DMA((2, full_width // chunk)),
        ],
        compiler_params=pltpu.CompilerParams(vmem_limit_bytes=VMEM_LIMIT),
        name="gram",
    )(templates)


STEPS = LANES // SUB
EARLY = 10


def first_kernel(gram_ref, first_ref, half_ref, second_ref):
    first = -eliminate(gram_ref[:LANES, :LANES], 0, STEPS)
    side = gram_ref[:LANES, LANES:]
    half = dot_f32(first, side, NN)
    first_ref[...] = first
    half_ref[...] = half
    second_ref[...] = eliminate(gram_ref[LANES:, LANES:] - dot_f32(side.T, half, NN), 0, EARLY)


def finish_kernel(first_ref, half_ref, second_ref, scale_ref, out_ref):
    first, half = first_ref[...], half_ref[...]
    last = -eliminate(second_ref[...], EARLY, STEPS)
    cross = dot_f32(half, last, NN)
    row = scale_ref[...]
    column = jnp.broadcast_to(row, (SUB, row.shape[1])).T[:, :1]
    near, far = row[:, :LANES], row[:, LANES:]
    out_ref[:LANES, :LANES] = (first + dot_f32(cross, half, NT)) * near * column[:LANES]
    out_ref[:LANES, LANES:] = -cross * far * column[:LANES]
    out_ref[LANES:, :LANES] = -cross.T * near * column[LANES:]
    out_ref[LANES:, LANES:] = last * far * column[LANES:]


def in_vmem(kernel, shapes, name, *arrays):
    return pl.pallas_call(
        kernel,
        out_shape=shapes,
        compiler_params=pltpu.CompilerParams(vmem_limit_bytes=VMEM_LIMIT),
        name=name,
    )(*arrays)


def window_sums(read, rows, first, begin, span):
    lines = begin.shape[0]
    sub = lax.broadcasted_iota(jnp.int32, (SUB, LANES), 0)
    spans = [jnp.broadcast_to(span[j : j + 1], (SUB, LANES)).astype(F32) for j in range(lines)]
    offsets = [
        (2 * (first + sub - jnp.broadcast_to(begin[j : j + 1], (SUB, LANES))) + 1).astype(F32) - spans[j]
        for j in range(lines)
    ]

    def add(block, shift, sums):
        size = block.shape[0]
        out = []
        for j in range(lines):
            m = offsets[j][:size] + shift
            masked = jnp.where(jnp.abs(m) < spans[j][:size], block, 0.0)
            weighted = masked * m
            out += [sums[3 * j] + masked, sums[3 * j + 1] + weighted, sums[3 * j + 2] + weighted * m]
        return out

    full = rows // SUB
    out = [jnp.zeros((1, LANES), F32)] * (3 * lines)
    if full:
        sums = [jnp.zeros((SUB, LANES), F32)] * (3 * lines)
        for i in range(full):
            sums = add(read(i * SUB, SUB), 2.0 * i * SUB, sums)
        out = [jnp.sum(x, axis=0, keepdims=True) for x in sums]
    if rows % SUB:
        sums = [jnp.zeros((rows % SUB, LANES), F32)] * (3 * lines)
        sums = add(read(full * SUB, rows % SUB), 2.0 * full * SUB, sums)
        out = [x + jnp.sum(y, axis=0, keepdims=True) for x, y in zip(out, sums)]
    return [out[3 * j + k] for k in range(3) for j in range(lines)]


def halving_order(devices):
    bits = devices.bit_length() - 1
    return list(range(2, bits)) + [1, 0]


def flips(position, devices):
    order = halving_order(devices)
    return sum(((position >> (len(order) - 1 - t)) & 1) << bit for t, bit in enumerate(order))


def cube_kernel(device_ref, begin_ref, span_ref, cube_ref, out_ref, *, devices, start):
    width = cube_ref.shape[0]
    device = device_ref[0]
    rows = 3 * begin_ref.shape[0]

    def owner(i, carry):
        lanes = pl.ds(pl.multiple_of((device ^ flips(start + i, devices)) * LANES, LANES), LANES)
        sums = window_sums(
            lambda row, size: cube_ref[row : row + size, lanes],
            width,
            device * width,
            begin_ref[:, lanes],
            span_ref[:, lanes],
        )
        out_ref[pl.ds(pl.multiple_of(i * rows, SUB), rows), :] = jnp.concatenate(sums, axis=0)
        return carry

    lax.fori_loop(0, out_ref.shape[0] // rows, owner, 0)


def cube_windows(device, begin, span, cube, devices, start, stop):
    vmem = pl.BlockSpec(memory_space=pltpu.VMEM)
    return pl.pallas_call(
        functools.partial(cube_kernel, devices=devices, start=start),
        in_specs=[pl.BlockSpec(memory_space=pltpu.SMEM), vmem, vmem, vmem],
        out_shape=rows_of((stop - start) * 3 * begin.shape[0]),
        compiler_params=pltpu.CompilerParams(vmem_limit_bytes=VMEM_LIMIT),
        name="cube_windows",
    )(device, begin, span, cube)


def split_kernel(device_ref, x_ref, y_ref, keep_ref, send_ref):
    half = keep_ref.shape[0]
    total = x_ref[...] + y_ref[...]
    low_kept = (device_ref[0] >> 1) % 2 == 0
    keep_ref[...] = jnp.where(low_kept, total[:half], total[half:])
    send_ref[...] = jnp.where(low_kept, total[half:], total[:half])


def join_kernel(x_ref, y_ref, early_ref, late_ref, keep_ref, send_ref):
    slots = x_ref.shape[0]
    early = early_ref.shape[0]
    rest = keep_ref.shape[0] - slots - early
    total = x_ref[...] + y_ref[...]
    keep_ref[:slots, :] = total
    keep_ref[slots : slots + early, :] = early_ref[...]
    keep_ref[slots + early :, :] = late_ref[:rest, :]
    send_ref[:slots, :] = total
    send_ref[slots:, :] = late_ref[rest:, :]


def step_kernel(x_ref, y_ref, keep_ref, send_ref):
    rows = x_ref.shape[0]
    half = rows - keep_ref.shape[0]
    slots = rows - 2 * half
    total = x_ref[:slots, :] + y_ref[:slots, :]
    for out_ref, first in ((keep_ref, slots), (send_ref, slots + half)):
        out_ref[:slots, :] = total
        out_ref[slots:, :] = x_ref[first : first + half, :] + y_ref[first : first + half, :]


def rows_of(count):
    return jax.ShapeDtypeStruct((count, LANES), F32)


def split_slots(device, x, y):
    vmem = pl.BlockSpec(memory_space=pltpu.VMEM)
    half = rows_of(x.shape[0] // 2)
    return pl.pallas_call(
        split_kernel,
        in_specs=[pl.BlockSpec(memory_space=pltpu.SMEM), vmem, vmem],
        out_shape=(half, half),
        compiler_params=pltpu.CompilerParams(vmem_limit_bytes=VMEM_LIMIT),
        name="split_slots",
    )(device, x, y)


def owner_kernel(
    device_ref, bins_ref, owner_ref, begin_ref, span_ref,
    kept_ref, by_x_ref, by_core_ref, by_both_ref, inverse_ref, hi_ref, mid_ref, low_ref,
    weights_ref, out_ref,
    continuum_ref, mid_held_ref, low_held_ref, bins_held_ref, owner_held_ref, begins_ref, spans_ref, starts_ref,
    parts_sem, small_sem, *, chunk,
):
    own_slots = weights_ref.shape[0]
    own = bins_held_ref.shape[1]
    lines = begin_ref.shape[0]
    full_width = hi_ref.shape[1]
    half = owner_held_ref.shape[1] // 2
    device = device_ref[0]
    own_lanes = pl.ds(pl.multiple_of(device * own, LANES), own)

    small_copies = [
        pltpu.make_async_copy(bins_ref.at[:, own_lanes], bins_held_ref, small_sem.at[0]),
        pltpu.make_async_copy(owner_ref, owner_held_ref, small_sem.at[1]),
        pltpu.make_async_copy(begin_ref.at[:, own_lanes], begins_ref, small_sem.at[2]),
        pltpu.make_async_copy(span_ref.at[:, own_lanes], spans_ref, small_sem.at[3]),
        pltpu.make_async_copy(begin_ref.at[:, own_lanes], starts_ref, small_sem.at[4]),
    ]
    part_copies = [
        pltpu.make_async_copy(mid_ref, mid_held_ref, parts_sem.at[0]),
        pltpu.make_async_copy(low_ref, low_held_ref, parts_sem.at[1]),
    ]
    for copy in small_copies + part_copies:
        copy.start()

    inverse = inverse_ref[...]
    core_low = device % 2 == 0
    low_kept = (device >> 1) % 2 == 0

    def by_lanes(near, far):
        return jnp.concatenate([jnp.where(core_low, near, far), jnp.where(core_low, far, near)], axis=1)

    slot = device * own_slots
    in_kept = (slot // half) == ((device >> 1) % 2)
    rows = pl.ds(pl.multiple_of(slot % half, own_slots), own_slots)
    mine = by_lanes(
        jnp.where(in_kept, kept_ref[rows, :], by_x_ref[rows, :]),
        jnp.where(in_kept, by_core_ref[rows, :], by_both_ref[rows, :]),
    )
    weights_ref[...] = dot_f32(mine, inverse, NN)

    for copy in small_copies:
        copy.wait()
    bins = jnp.broadcast_to(bins_held_ref[...], (SUB, own)).T[:, :1]
    low_slots, high_slots = owner_held_ref[:, :half], owner_held_ref[:, half:]
    members = [
        jnp.where(bins == jnp.where(low_kept, a, b), 1.0, 0.0).astype(BF16)
        for a, b in ((low_slots, high_slots), (high_slots, low_slots))
    ]
    picked = []
    for kept_half, other_half in ((kept_ref, by_x_ref), (by_core_ref, by_both_ref)):
        value = None
        for member, block in zip(members, (kept_half, other_half)):
            hi, mid, low = split3(block[:half, :])
            new = dot(member, hi, NN) + (dot(member, mid, NN) + dot(member, low, NN))
            value = new if value is None else value + new
        picked.append(value)
    spaxel_weights = dot_f32(by_lanes(*picked), inverse, NN)

    hi, mid, low = split3(spaxel_weights)
    tiles = chunk // LANES
    for i in range(full_width // chunk):
        first = hi_ref[:, i * chunk : (i + 1) * chunk]
        value = dot(hi, first, NN) + (dot(mid, first, NN) + dot(low, first, NN))
        for t in range(tiles):
            continuum_ref[i * tiles + t] = value[:, t * LANES : (t + 1) * LANES]
    for copy in part_copies:
        copy.wait()
    for i in range(full_width // chunk):
        lanes = slice(i * chunk, (i + 1) * chunk)
        second, third = mid_held_ref[:, lanes], low_held_ref[:, lanes]
        value = dot(hi, second, NN) + (dot(mid, second, NN) + dot(hi, third, NN))
        for t in range(tiles):
            continuum_ref[i * tiles + t] += value[:, t * LANES : (t + 1) * LANES]
    continuum_ref[full_width // LANES] = jnp.zeros((own, LANES), F32)

    begin = begins_ref[...]
    span = spans_ref[...].astype(F32)
    centre = 2.0 * (begin & (LANES - 1)).astype(F32) + span - 1.0
    rows_at = lax.broadcasted_iota(jnp.int32, (SUB, LANES), 0)
    at_row = [rows_at == r for r in range(SUB)]
    twice = 2.0 * lax.broadcasted_iota(jnp.int32, (LANES, own), 0).astype(F32)
    sums = [None] * (3 * lines)
    for j in range(lines):
        picks = ([], [])
        for g in range(own // SUB):
            rows = slice(g * SUB, (g + 1) * SUB)
            left = right = None
            for r in range(SUB):
                tile = lax.shift_right_logical(starts_ref[j, g * SUB + r], 7)
                a = continuum_ref[tile, rows, :]
                b = continuum_ref[tile + 1, rows, :]
                left = a if left is None else jnp.where(at_row[r], a, left)
                right = b if right is None else jnp.where(at_row[r], b, right)
            picks[0].append(left)
            picks[1].append(right)
        terms = None
        for side in range(2):
            block = jnp.concatenate(picks[side], axis=0).T
            m = twice + (2.0 * LANES * side - centre[j : j + 1])
            masked = jnp.where(jnp.abs(m) < span[j : j + 1], block, 0.0)
            weighted = masked * m
            new = [masked, weighted, weighted * m]
            terms = new if terms is None else [x + y for x, y in zip(terms, new)]
        for k in range(3):
            sums[k * lines + j] = jnp.sum(terms[k], axis=0, keepdims=True)
    continuum_sums = jnp.concatenate(sums, axis=0)

    own_rows = slice(half, half + 3 * lines)
    other_rows = slice(half + 3 * lines, half + 6 * lines)
    cube_sums = (kept_ref[own_rows, :] + by_x_ref[own_rows, :]) + (
        by_core_ref[other_rows, :] + by_both_ref[other_rows, :]
    )
    scale = jnp.concatenate([span, span * span, span * span * span], axis=0)
    out_ref[...] = (cube_sums - continuum_sums) / scale


def owned(device, bins, owner, begin, span, messages, inverse, parts, own_slots, own, chunk):
    vmem = pl.BlockSpec(memory_space=pltpu.VMEM)
    hbm = pl.BlockSpec(memory_space=pltpu.HBM)
    count, full_width = parts[0].shape
    lines = begin.shape[0]
    return pl.pallas_call(
        functools.partial(owner_kernel, chunk=chunk),
        in_specs=[pl.BlockSpec(memory_space=pltpu.SMEM)] + [hbm] * 4 + [vmem] * 6 + [hbm] * 2,
        out_shape=(
            jax.ShapeDtypeStruct((own_slots, count), F32),
            jax.ShapeDtypeStruct((3 * lines, own), F32),
        ),
        scratch_shapes=[
            pltpu.VMEM((full_width // LANES + 1, own, LANES), F32),
            pltpu.VMEM((count, full_width), BF16),
            pltpu.VMEM((count, full_width), BF16),
            pltpu.VMEM((1, own), jnp.int32),
            pltpu.VMEM(owner.shape, jnp.int32),
            pltpu.VMEM((lines, own), jnp.int32),
            pltpu.VMEM((lines, own), jnp.int32),
            pltpu.SMEM((lines, own), jnp.int32),
            pltpu.SemaphoreType.DMA((2,)),
            pltpu.SemaphoreType.DMA((5,)),
        ],
        compiler_params=pltpu.CompilerParams(vmem_limit_bytes=VMEM_LIMIT),
        name="owned",
    )(device, bins, owner, begin, span, *messages, inverse, *parts)


def shards(cube, templates, bin_id, owner_bins, line_start, line_width):
    devices = lax.axis_size("spax")
    device = lax.axis_index("spax")
    spaxels = cube.shape[0]
    total_bins = owner_bins.shape[0]
    count = templates.shape[0]
    lines = line_start.shape[0]
    own_spaxels = spaxels // devices
    own_slots = total_bins // devices
    here = device.reshape(1).astype(jnp.int32)
    pin = lambda x: pltpu.with_memory_space_constraint(x, pltpu.HBM)
    columns = pin(cube.T)
    begin, span = pin(line_start), pin(line_width)
    bins, owner = pin(bin_id[None, :]), pin(owner_bins[None, :])
    after = lax.optimization_barrier

    def swap(x, bit):
        return lax.ppermute(x, "spax", [(d, d ^ (1 << bit)) for d in range(devices)])

    keep, send, begins, spans, held = project(here, bins, owner, begin, span, columns, pin(templates))
    arrived = swap(send, 0)
    cut = devices * 3 // 16
    early = cube_windows(here, begins, spans, held, devices, 0, cut)
    keep, arrived, early = after((keep, arrived, early))
    keep, send = split_slots(here, keep, arrived)
    keep, send, now = after((keep, send, here))
    arrived = swap(send, 1)
    late = cube_windows(now, begins, spans, held, devices, cut, devices)
    keep, arrived, early, late, templates = after((keep, arrived, early, late, templates))
    slots, extra = total_bins // 2, devices * 3 * lines // 2
    message = rows_of(slots + extra)
    keep, send = in_vmem(join_kernel, (message, message), "join", keep, arrived, early, late)

    keep, send, templates = after((keep, send, templates))
    gram = scale = first = None
    for bit in range(2, devices.bit_length() - 1):
        arrived = swap(send, bit)
        if gram is None:
            gram, scale, *parts = scaled_gram(pin(templates), 512)
            arrived, gram = after((arrived, gram))
        elif first is None:
            first = in_vmem(first_kernel, [rows_of(LANES)] * 3, "first", gram)
            arrived, first = after((arrived, first))
        extra //= 2
        message = rows_of(slots + extra)
        keep, send = in_vmem(step_kernel, (message, message), "step", keep, arrived)
        if first is None:
            keep, send, gram = after((keep, send, gram))
        else:
            keep, send, first = after((keep, send, first))

    by_x = swap(send, 1)
    by_core = swap(keep, 0)
    inverse = in_vmem(finish_kernel, jax.ShapeDtypeStruct((count, count), F32), "finish", *first, scale)
    by_x, by_core, inverse = after((by_x, by_core, inverse))
    by_both = swap(by_x, 0)
    messages = (keep, by_x, by_core, by_both)
    parts = [parts[0], pin(parts[1]), pin(parts[2])]
    return owned(here, bins, owner, begin, span, messages, inverse, parts, own_slots, own_spaxels, 512)


def solution(mesh):
    placed = (
        P("strips", "spax"),
        P(),
        P("strips"),
        P("strips"),
        P(None, "strips"),
        P(None, "strips"),
    )
    return jax.shard_map(
        shards,
        mesh=mesh,
        in_specs=placed,
        out_specs=(P(("strips", "spax"), None), P(None, ("strips", "spax"))),
        check_vma=False,
    )
```

```python
import functools

import jax
import jax.numpy as jnp
from jax import lax
from jax.experimental import pallas as pl
from jax.experimental.pallas import tpu as pltpu
from jax.sharding import PartitionSpec as P

HIGHEST = lax.Precision.HIGHEST
F32 = jnp.float32
BF16 = jnp.bfloat16
LANES = 128
SUB = 8
VMEM_LIMIT = 20 * 1024 * 1024

NT = (((1,), (1,)), ((), ()))
NN = (((1,), (0,)), ((), ()))


def split3(x):
    hi = x.astype(BF16)
    rest = x - hi.astype(F32)
    mid = rest.astype(BF16)
    low = (rest - mid.astype(F32)).astype(BF16)
    return hi, mid, low


def dot(a, b, dims):
    return lax.dot_general(a, b, dims, preferred_element_type=F32)


def dot_f32(a, b, dims):
    return lax.dot_general(a, b, dims, precision=HIGHEST, preferred_element_type=F32)


def template_window(width, full_width):
    return min(full_width, -(-(width + LANES - 1) // LANES) * LANES)


def project_kernel(
    device_ref, bins_ref, begin_ref, span_ref, cube_ref, templates_ref,
    keep_ref, send_ref, begins_ref, spans_ref, held_ref,
    sums_ref, counts_ref, window_ref, bins_held_ref, firsts_ref, cube_sem, small_sem, *, chunk,
):
    width, spaxels = cube_ref.shape
    total_bins = keep_ref.shape[0]
    full_width = templates_ref.shape[1]
    first = device_ref[0] * width
    window = window_ref.shape[1]
    base = pl.multiple_of(jnp.minimum(first // LANES * LANES, full_width - window), LANES)
    chunks = spaxels // chunk
    reach = chunk + SUB

    def cube_copy(i):
        lanes = pl.ds(i * chunk, chunk)
        return pltpu.make_async_copy(cube_ref.at[:, lanes], held_ref.at[:, lanes], cube_sem.at[i])

    bins_copy = pltpu.make_async_copy(bins_ref, bins_held_ref, small_sem.at[0])
    firsts_copy = pltpu.make_async_copy(bins_ref, firsts_ref, small_sem.at[1])
    window_copy = pltpu.make_async_copy(templates_ref.at[:, pl.ds(base, window)], window_ref, small_sem.at[2])
    line_copies = [
        pltpu.make_async_copy(begin_ref, begins_ref, small_sem.at[3]),
        pltpu.make_async_copy(span_ref, spans_ref, small_sem.at[4]),
    ]
    for copy in [bins_copy, firsts_copy] + [cube_copy(i) for i in range(chunks)] + [window_copy] + line_copies:
        copy.start()
    sums_ref[...] = jnp.zeros(sums_ref.shape, F32)
    counts_ref[...] = jnp.zeros(counts_ref.shape, F32)
    rows_at = lax.broadcasted_iota(jnp.int32, (reach, chunk), 0)
    bins_copy.wait()
    firsts_copy.wait()

    for i in range(chunks):
        lanes = slice(i * chunk, (i + 1) * chunk)
        low_bin = pl.multiple_of(firsts_ref[0, i * chunk] // SUB * SUB, SUB)
        rows = pl.ds(low_bin, reach)
        ones = jnp.where(rows_at == bins_held_ref[:, lanes] - low_bin, 1.0, 0.0)
        counts = ones[:, :LANES]
        for lane in range(LANES, chunk, LANES):
            counts = counts + ones[:, lane : lane + LANES]
        counts_ref[rows, :] += counts
        member = ones.astype(BF16)
        cube_copy(i).wait()
        hi, mid, low = split3(held_ref[:, lanes])
        sums_ref[rows, :] += dot(member, hi, NT) + (dot(member, mid, NT) + dot(member, low, NT))

    window_copy.wait()
    mine = pltpu.roll(window_ref[...], window - (first - base), 1)[:, :width]
    low_kept = device_ref[0] % 2 == 0
    block = min(total_bins, 512)
    for at in range(0, total_bins, block):
        rows = slice(at, at + block)
        means = sums_ref[rows, :] / jnp.sum(counts_ref[rows, :], axis=1, keepdims=True)
        projections = dot_f32(means, mine, NT) * (1.0 / full_width)
        low, high = projections[:, :LANES], projections[:, LANES:]
        keep_ref[rows, :] = jnp.where(low_kept, low, high)
        send_ref[rows, :] = jnp.where(low_kept, high, low)
    for copy in line_copies:
        copy.wait()


def project(device, bins, begin, span, cube, templates, total_bins):
    width, spaxels = cube.shape
    chunk = min(spaxels, 256)
    count, full_width = templates.shape
    return pl.pallas_call(
        functools.partial(project_kernel, chunk=chunk),
        in_specs=[pl.BlockSpec(memory_space=pltpu.SMEM)] + [pl.BlockSpec(memory_space=pltpu.HBM)] * 5,
        out_specs=[pl.BlockSpec(memory_space=pltpu.VMEM)] * 5,
        out_shape=[
            rows_of(total_bins),
            rows_of(total_bins),
            pltpu.VMEM(begin.shape, jnp.int32),
            pltpu.VMEM(span.shape, jnp.int32),
            pltpu.VMEM((width, spaxels), F32),
        ],
        scratch_shapes=[
            pltpu.VMEM((total_bins + chunk + SUB, width), F32),
            pltpu.VMEM((total_bins + chunk + SUB, LANES), F32),
            pltpu.VMEM((count, template_window(width, full_width)), F32),
            pltpu.VMEM(bins.shape, jnp.int32),
            pltpu.SMEM(bins.shape, jnp.int32),
            pltpu.SemaphoreType.DMA((spaxels // chunk,)),
            pltpu.SemaphoreType.DMA((5,)),
        ],
        compiler_params=pltpu.CompilerParams(vmem_limit_bytes=VMEM_LIMIT),
        name="project",
    )(device, bins, begin, span, cube, templates)


def reciprocal(x):
    r = pl.reciprocal(x, approx=True)
    r = r * (2.0 - x * r)
    return r * (2.0 - x * r)


def eliminate(tile, start, stop):
    size = tile.shape[0]
    count = size // SUB
    lanes = lax.broadcasted_iota(jnp.int32, (SUB, size), 1)
    rows_at = lax.broadcasted_iota(jnp.int32, (SUB, size), 0)
    rows = [tile[i * SUB : (i + 1) * SUB, :] for i in range(count)]
    for k in range(start, stop):
        block = rows[k]
        first = k * SUB
        a = {}
        for i in range(SUB):
            for j in range(i, SUB):
                a[i, j] = jnp.broadcast_to(block[i : i + 1, first + j : first + j + 1], (SUB, size))

        def at(i, j):
            return (i, j) if i <= j else (j, i)

        for p in range(0, SUB, 2):
            q = p + 1
            pp, pq, qq = a[p, p], a[p, q], a[q, q]
            inverse = reciprocal(pp * qq - pq * pq)
            others = [i for i in range(SUB) if i not in (p, q)]
            old = {i: (a[at(i, p)], a[at(i, q)]) for i in others}
            new = {
                i: ((u * qq - v * pq) * inverse, (v * pp - u * pq) * inverse) for i, (u, v) in old.items()
            }
            for i in others:
                for j in others:
                    if i <= j:
                        a[i, j] = a[i, j] - new[i][0] * old[j][0] - new[i][1] * old[j][1]
            for i in others:
                a[at(i, p)], a[at(i, q)] = new[i]
            a[p, p], a[p, q], a[q, q] = -(qq * inverse), pq * inverse, -(pp * inverse)
        columns = []
        for j in range(SUB):
            column = a[at(0, j)]
            for i in range(1, SUB):
                column = jnp.where(rows_at == i, a[at(i, j)], column)
            columns.append(column)
        terms = [columns[j] * jnp.broadcast_to(block[j : j + 1, :], (SUB, size)) for j in range(SUB)]
        while len(terms) > 1:
            terms = [x + y for x, y in zip(terms[::2], terms[1::2])]
        swept = -terms[0]
        for j in range(SUB):
            swept = jnp.where(lanes == first + j, columns[j], swept)
        inside = (lanes >= first) & (lanes < first + SUB)
        spread_rows = [jnp.broadcast_to(swept[j : j + 1, :], (SUB, size)) for j in range(SUB)]
        order = list(range(k + 1, count)) + list(range(k))
        for i in order:
            terms = [
                jnp.broadcast_to(rows[i][:, first + j : first + j + 1], (SUB, size)) * spread_rows[j]
                for j in range(SUB)
            ]
            while len(terms) > 1:
                terms = [x + y for x, y in zip(terms[::2], terms[1::2])]
            rows[i] = jnp.where(inside, 0.0, rows[i]) - terms[0]
        rows[k] = swept
    return jnp.concatenate(rows, axis=0)


def gram_kernel(
    templates_ref, gram_ref, scale_ref, hi_ref, mid_ref, low_ref, held_ref, mid_held_ref, low_held_ref, sem, out_sem,
    *, chunk,
):
    count, full_width = templates_ref.shape

    def copy(i):
        lanes = pl.ds(i * chunk, chunk)
        return pltpu.make_async_copy(templates_ref.at[:, lanes], held_ref.at[:, lanes], sem.at[i])

    def out_copies(i):
        lanes = pl.ds(i * chunk, chunk)
        return [
            pltpu.make_async_copy(mid_held_ref.at[:, lanes], mid_ref.at[:, lanes], out_sem.at[0, i]),
            pltpu.make_async_copy(low_held_ref.at[:, lanes], low_ref.at[:, lanes], out_sem.at[1, i]),
        ]

    for i in range(full_width // chunk):
        copy(i).start()
    even = jnp.zeros((count, count), F32)
    mixed = jnp.zeros((count, count), F32)
    for i in range(full_width // chunk):
        copy(i).wait()
        lanes = slice(i * chunk, (i + 1) * chunk)
        hi, mid, low = split3(held_ref[:, lanes])
        hi_ref[:, lanes], mid_held_ref[:, lanes], low_held_ref[:, lanes] = hi, mid, low
        for out in out_copies(i):
            out.start()
        even = even + (dot(hi, hi, NT) + dot(mid, mid, NT))
        mixed = mixed + (dot(hi, mid, NT) + dot(hi, low, NT))
    gram = (even + (mixed + mixed.T)) * (1.0 / full_width)
    same = lax.broadcasted_iota(jnp.int32, gram.shape, 0) == lax.broadcasted_iota(jnp.int32, gram.shape, 1)
    diagonal = jnp.where(same, gram, 0.0)
    row = lax.rsqrt(jnp.sum(diagonal, axis=0, keepdims=True))
    column = lax.rsqrt(jnp.sum(diagonal, axis=1, keepdims=True))
    gram = gram * row * column
    scale_ref[...] = row
    gram_ref[...] = gram
    for i in range(full_width // chunk):
        for out in out_copies(i):
            out.wait()


def scaled_gram(templates, chunk):
    count, full_width = templates.shape
    vmem, hbm = (pl.BlockSpec(memory_space=space) for space in (pltpu.VMEM, pltpu.HBM))
    return pl.pallas_call(
        functools.partial(gram_kernel, chunk=chunk),
        in_specs=[hbm],
        out_specs=(vmem, vmem, vmem, hbm, hbm),
        out_shape=(
            jax.ShapeDtypeStruct((count, count), F32),
            jax.ShapeDtypeStruct((1, count), F32),
            pltpu.VMEM((count, full_width), BF16),
            pltpu.HBM((count, full_width), BF16),
            pltpu.HBM((count, full_width), BF16),
        ),
        scratch_shapes=[
            pltpu.VMEM((count, full_width), F32),
            pltpu.VMEM((count, full_width), BF16),
            pltpu.VMEM((count, full_width), BF16),
            pltpu.SemaphoreType.DMA((full_width // chunk,)),
            pltpu.SemaphoreType.DMA((2, full_width // chunk)),
        ],
        compiler_params=pltpu.CompilerParams(vmem_limit_bytes=VMEM_LIMIT),
        name="gram",
    )(templates)


STEPS = LANES // SUB
EARLY = 5


def first_kernel(gram_ref, first_ref, half_ref, second_ref):
    first = -eliminate(gram_ref[:LANES, :LANES], 0, STEPS)
    side = gram_ref[:LANES, LANES:]
    half = dot_f32(first, side, NN)
    first_ref[...] = first
    half_ref[...] = half
    second_ref[...] = eliminate(gram_ref[LANES:, LANES:] - dot_f32(side.T, half, NN), 0, EARLY)


def finish_kernel(first_ref, half_ref, second_ref, scale_ref, out_ref):
    first, half = first_ref[...], half_ref[...]
    last = -eliminate(second_ref[...], EARLY, STEPS)
    cross = dot_f32(half, last, NN)
    row = scale_ref[...]
    column = jnp.broadcast_to(row, (SUB, row.shape[1])).T[:, :1]
    near, far = row[:, :LANES], row[:, LANES:]
    out_ref[:LANES, :LANES] = (first + dot_f32(cross, half, NT)) * near * column[:LANES]
    out_ref[:LANES, LANES:] = -cross * far * column[:LANES]
    out_ref[LANES:, :LANES] = -cross.T * near * column[LANES:]
    out_ref[LANES:, LANES:] = last * far * column[LANES:]


def in_vmem(kernel, shapes, name, *arrays):
    return pl.pallas_call(
        kernel,
        out_shape=shapes,
        compiler_params=pltpu.CompilerParams(vmem_limit_bytes=VMEM_LIMIT),
        name=name,
    )(*arrays)


def window_sums(read, rows, first, begin, span):
    lines = begin.shape[0]
    sub = lax.broadcasted_iota(jnp.int32, (SUB, LANES), 0)
    spans = [jnp.broadcast_to(span[j : j + 1], (SUB, LANES)).astype(F32) for j in range(lines)]
    offsets = [
        (2 * (first + sub - jnp.broadcast_to(begin[j : j + 1], (SUB, LANES))) + 1).astype(F32) - spans[j]
        for j in range(lines)
    ]

    def add(block, shift, sums):
        size = block.shape[0]
        out = []
        for j in range(lines):
            m = offsets[j][:size] + shift
            masked = jnp.where(jnp.abs(m) < spans[j][:size], block, 0.0)
            weighted = masked * m
            out += [sums[3 * j] + masked, sums[3 * j + 1] + weighted, sums[3 * j + 2] + weighted * m]
        return out

    full = rows // SUB
    out = [jnp.zeros((1, LANES), F32)] * (3 * lines)
    if full:
        sums = [jnp.zeros((SUB, LANES), F32)] * (3 * lines)
        for i in range(full):
            sums = add(read(i * SUB, SUB), 2.0 * i * SUB, sums)
        out = [jnp.sum(x, axis=0, keepdims=True) for x in sums]
    if rows % SUB:
        sums = [jnp.zeros((rows % SUB, LANES), F32)] * (3 * lines)
        sums = add(read(full * SUB, rows % SUB), 2.0 * full * SUB, sums)
        out = [x + jnp.sum(y, axis=0, keepdims=True) for x, y in zip(out, sums)]
    return [out[3 * j + k] for k in range(3) for j in range(lines)]


def halving_order(devices):
    bits = devices.bit_length() - 1
    return list(range(2, bits)) + [1, 0]


def flips(position, devices):
    order = halving_order(devices)
    return sum(((position >> (len(order) - 1 - t)) & 1) << bit for t, bit in enumerate(order))


def cube_kernel(device_ref, begin_ref, span_ref, cube_ref, out_ref, *, devices, start):
    width = cube_ref.shape[0]
    device = device_ref[0]
    rows = 3 * begin_ref.shape[0]

    def owner(i, carry):
        lanes = pl.ds(pl.multiple_of((device ^ flips(start + i, devices)) * LANES, LANES), LANES)
        sums = window_sums(
            lambda row, size: cube_ref[row : row + size, lanes],
            width,
            device * width,
            begin_ref[:, lanes],
            span_ref[:, lanes],
        )
        out_ref[pl.ds(pl.multiple_of(i * rows, SUB), rows), :] = jnp.concatenate(sums, axis=0)
        return carry

    lax.fori_loop(0, out_ref.shape[0] // rows, owner, 0)


def cube_windows(device, begin, span, cube, devices, start, stop):
    vmem = pl.BlockSpec(memory_space=pltpu.VMEM)
    return pl.pallas_call(
        functools.partial(cube_kernel, devices=devices, start=start),
        in_specs=[pl.BlockSpec(memory_space=pltpu.SMEM), vmem, vmem, vmem],
        out_shape=rows_of((stop - start) * 3 * begin.shape[0]),
        compiler_params=pltpu.CompilerParams(vmem_limit_bytes=VMEM_LIMIT),
        name="cube_windows",
    )(device, begin, span, cube)


def split_kernel(device_ref, x_ref, y_ref, keep_ref, send_ref):
    half = keep_ref.shape[0]
    total = x_ref[...] + y_ref[...]
    low_kept = (device_ref[0] >> 1) % 2 == 0
    keep_ref[...] = jnp.where(low_kept, total[:half], total[half:])
    send_ref[...] = jnp.where(low_kept, total[half:], total[:half])


def join_kernel(x_ref, y_ref, early_ref, late_ref, keep_ref, send_ref):
    slots, early = x_ref.shape[0], early_ref.shape[0]
    total = x_ref[...] + y_ref[...]
    keep_ref[...] = total
    send_ref[:slots, :] = total
    send_ref[slots : slots + early, :] = early_ref[...]
    send_ref[slots + early :, :] = late_ref[...]


def step_kernel(x_ref, y_ref, sums_ref, keep_ref, send_ref, *, slots):
    half = (y_ref.shape[0] - slots) // 2
    own = sums_ref.shape[0]
    total = x_ref[:slots, :] + y_ref[:slots, :]

    def gathered(first):
        value = y_ref[slots + first : slots + first + half, :]
        if x_ref.shape[0] > slots:
            value = value + x_ref[slots + first : slots + first + half, :]
        return value

    kept, sent = gathered(0), gathered(half) + sums_ref[own - half :, :]
    if own > half:
        kept = kept + sums_ref[:half, :]
    keep_ref[:slots, :] = total
    keep_ref[slots:, :] = kept
    send_ref[:slots, :] = total
    send_ref[slots:, :] = sent


def rows_of(count):
    return jax.ShapeDtypeStruct((count, LANES), F32)


def split_slots(device, x, y):
    vmem = pl.BlockSpec(memory_space=pltpu.VMEM)
    half = rows_of(x.shape[0] // 2)
    return pl.pallas_call(
        split_kernel,
        in_specs=[pl.BlockSpec(memory_space=pltpu.SMEM), vmem, vmem],
        out_shape=(half, half),
        compiler_params=pltpu.CompilerParams(vmem_limit_bytes=VMEM_LIMIT),
        name="split_slots",
    )(device, x, y)


def owner_kernel(
    device_ref, bins_ref, owner_ref, begin_ref, span_ref,
    kept_ref, by_x_ref, by_core_ref, by_both_ref, inverse_ref, hi_ref, mid_ref, low_ref,
    weights_ref, out_ref,
    continuum_ref, mine_ref, mid_held_ref, low_held_ref, bins_held_ref, owner_held_ref, begins_ref, spans_ref, starts_ref,
    parts_sem, small_sem, *, chunk,
):
    own_slots = weights_ref.shape[0]
    own = bins_held_ref.shape[1]
    lines = begin_ref.shape[0]
    full_width = hi_ref.shape[1]
    half = owner_held_ref.shape[1] // 2
    inverse = inverse_ref[...]
    device = device_ref[0]
    own_lanes = pl.ds(pl.multiple_of(device * own, LANES), own)

    small_copies = [
        pltpu.make_async_copy(bins_ref.at[:, own_lanes], bins_held_ref, small_sem.at[0]),
        pltpu.make_async_copy(owner_ref, owner_held_ref, small_sem.at[1]),
        pltpu.make_async_copy(begin_ref.at[:, own_lanes], begins_ref, small_sem.at[2]),
        pltpu.make_async_copy(span_ref.at[:, own_lanes], spans_ref, small_sem.at[3]),
        pltpu.make_async_copy(begin_ref.at[:, own_lanes], starts_ref, small_sem.at[4]),
    ]
    part_copies = [
        pltpu.make_async_copy(mid_ref, mid_held_ref, parts_sem.at[0]),
        pltpu.make_async_copy(low_ref, low_held_ref, parts_sem.at[1]),
    ]
    for copy in small_copies + part_copies:
        copy.start()

    core_low = device % 2 == 0
    low_kept = (device >> 1) % 2 == 0

    def lane_halves(near, far):
        return jnp.where(core_low, near, far), jnp.where(core_low, far, near)

    def by_lanes(near, far):
        return jnp.concatenate(lane_halves(near, far), axis=1)

    for copy in small_copies:
        copy.wait()

    kept_first = jnp.where(low_kept, 0, half)
    for i in range(own_slots):
        picked_bin = owner_held_ref[0, device * own_slots + i]
        in_kept = (picked_bin >= half) == (kept_first > 0)
        row = pl.ds(picked_bin - jnp.where(picked_bin >= half, half, 0), 1)
        low, high = lane_halves(
            jnp.where(in_kept, kept_ref[row, :], by_x_ref[row, :]),
            jnp.where(in_kept, by_core_ref[row, :], by_both_ref[row, :]),
        )
        mine_ref[i : i + 1, :LANES] = low
        mine_ref[i : i + 1, LANES:] = high
    weights_ref[...] = dot_f32(mine_ref[...], inverse, NN)

    bins = jnp.broadcast_to(bins_held_ref[...], (SUB, own)).T[:, :1]
    bins_at = lax.broadcasted_iota(jnp.int32, (own, half), 1)
    members = [
        jnp.where(bins_at == bins - low, 1.0, 0.0).astype(BF16) for low in (kept_first, half - kept_first)
    ]
    picked = []
    for kept_half, other_half in ((kept_ref, by_x_ref), (by_core_ref, by_both_ref)):
        value = None
        for member, block in zip(members, (kept_half, other_half)):
            hi, mid, low = split3(block[:half, :])
            new = dot(member, hi, NN) + (dot(member, mid, NN) + dot(member, low, NN))
            value = new if value is None else value + new
        picked.append(value)
    spaxel_weights = dot_f32(by_lanes(*picked), inverse, NN)

    hi, mid, low = split3(spaxel_weights)
    tiles = chunk // LANES
    for i in range(full_width // chunk):
        first = hi_ref[:, i * chunk : (i + 1) * chunk]
        value = dot(hi, first, NN) + (dot(mid, first, NN) + dot(low, first, NN))
        for t in range(tiles):
            continuum_ref[i * tiles + t] = value[:, t * LANES : (t + 1) * LANES]
    for copy in part_copies:
        copy.wait()
    for i in range(full_width // chunk):
        lanes = slice(i * chunk, (i + 1) * chunk)
        second, third = mid_held_ref[:, lanes], low_held_ref[:, lanes]
        value = dot(hi, second, NN) + (dot(mid, second, NN) + dot(hi, third, NN))
        for t in range(tiles):
            continuum_ref[i * tiles + t] += value[:, t * LANES : (t + 1) * LANES]
    continuum_ref[full_width // LANES] = jnp.zeros((own, LANES), F32)

    begin = begins_ref[...]
    span = spans_ref[...].astype(F32)
    centre = 2.0 * (begin & (LANES - 1)).astype(F32) + span - 1.0
    rows_at = lax.broadcasted_iota(jnp.int32, (SUB, LANES), 0)
    at_row = [rows_at == r for r in range(SUB)]
    twice = 2.0 * lax.broadcasted_iota(jnp.int32, (LANES, own), 0).astype(F32)
    sums = [None] * (3 * lines)
    for j in range(lines):
        picks = ([], [])
        for g in range(own // SUB):
            rows = slice(g * SUB, (g + 1) * SUB)
            left = right = None
            for r in range(SUB):
                tile = lax.shift_right_logical(starts_ref[j, g * SUB + r], 7)
                a = continuum_ref[tile, rows, :]
                b = continuum_ref[tile + 1, rows, :]
                left = a if left is None else jnp.where(at_row[r], a, left)
                right = b if right is None else jnp.where(at_row[r], b, right)
            picks[0].append(left)
            picks[1].append(right)
        terms = None
        for side in range(2):
            block = jnp.concatenate(picks[side], axis=0).T
            m = twice + (2.0 * LANES * side - centre[j : j + 1])
            masked = jnp.where(jnp.abs(m) < span[j : j + 1], block, 0.0)
            weighted = masked * m
            new = [masked, weighted, weighted * m]
            terms = new if terms is None else [x + y for x, y in zip(terms, new)]
        for k in range(3):
            sums[k * lines + j] = jnp.sum(terms[k], axis=0, keepdims=True)
    continuum_sums = jnp.concatenate(sums, axis=0)

    own_rows = slice(half, half + 3 * lines)
    other_rows = slice(half + 3 * lines, half + 6 * lines)
    cube_sums = (kept_ref[own_rows, :] + by_x_ref[own_rows, :]) + (
        by_core_ref[other_rows, :] + by_both_ref[other_rows, :]
    )
    scale = jnp.concatenate([span, span * span, span * span * span], axis=0)
    out_ref[...] = (cube_sums - continuum_sums) / scale


def owned(device, bins, owner, begin, span, messages, inverse, parts, own_slots, own, chunk):
    vmem = pl.BlockSpec(memory_space=pltpu.VMEM)
    hbm = pl.BlockSpec(memory_space=pltpu.HBM)
    count, full_width = parts[0].shape
    lines = begin.shape[0]
    return pl.pallas_call(
        functools.partial(owner_kernel, chunk=chunk),
        in_specs=[pl.BlockSpec(memory_space=pltpu.SMEM)] + [hbm] * 4 + [vmem] * 6 + [hbm] * 2,
        out_shape=(
            jax.ShapeDtypeStruct((own_slots, count), F32),
            jax.ShapeDtypeStruct((3 * lines, own), F32),
        ),
        scratch_shapes=[
            pltpu.VMEM((full_width // LANES + 1, own, LANES), F32),
            pltpu.VMEM((own_slots, count), F32),
            pltpu.VMEM((count, full_width), BF16),
            pltpu.VMEM((count, full_width), BF16),
            pltpu.VMEM((1, own), jnp.int32),
            pltpu.SMEM(owner.shape, jnp.int32),
            pltpu.VMEM((lines, own), jnp.int32),
            pltpu.VMEM((lines, own), jnp.int32),
            pltpu.SMEM((lines, own), jnp.int32),
            pltpu.SemaphoreType.DMA((2,)),
            pltpu.SemaphoreType.DMA((5,)),
        ],
        compiler_params=pltpu.CompilerParams(vmem_limit_bytes=VMEM_LIMIT),
        name="owned",
    )(device, bins, owner, begin, span, *messages, inverse, *parts)


def shards(cube, templates, bin_id, owner_bins, line_start, line_width):
    devices = lax.axis_size("spax")
    device = lax.axis_index("spax")
    spaxels = cube.shape[0]
    total_bins = owner_bins.shape[0]
    count = templates.shape[0]
    lines = line_start.shape[0]
    own_spaxels = spaxels // devices
    own_slots = total_bins // devices
    here = device.reshape(1).astype(jnp.int32)
    pin = lambda x: pltpu.with_memory_space_constraint(x, pltpu.HBM)
    columns = pin(cube.T)
    begin, span = pin(line_start), pin(line_width)
    bins, owner = pin(bin_id[None, :]), pin(owner_bins[None, :])
    after = lax.optimization_barrier

    def swap(x, bit):
        return lax.ppermute(x, "spax", [(d, d ^ (1 << bit)) for d in range(devices)])

    keep, send, begins, spans, held = project(here, bins, begin, span, columns, pin(templates), total_bins)
    windows = lambda start, stop, now: cube_windows(now, begins, spans, held, devices, start, stop)
    arrived = swap(send, 0)
    left = devices // 2
    cut = left + devices * 3 // 16
    early = windows(left, cut, here)
    keep, arrived, early = after((keep, arrived, early))
    keep, send = split_slots(here, keep, arrived)
    keep, send, now = after((keep, send, here))
    arrived = swap(send, 1)
    late = windows(cut, devices, now)
    keep, arrived, early, late, templates = after((keep, arrived, early, late, templates))
    slots = total_bins // 2
    message = rows_of(slots + left * 3 * lines)
    keep, send = in_vmem(join_kernel, (rows_of(slots), message), "join", keep, arrived, early, late)

    keep, send, now, templates = after((keep, send, here, templates))
    gram = first = None
    for bit in range(2, devices.bit_length() - 1):
        arrived = swap(send, bit)
        left //= 2
        last_step = bit == devices.bit_length() - 2
        sums = windows(0 if last_step else left, 2 * left, now)
        if gram is None:
            gram, scale, *parts = scaled_gram(pin(templates), 512)
            arrived, sums, gram = after((arrived, sums, gram))
        elif first is None:
            first = in_vmem(first_kernel, [rows_of(LANES)] * 3, "first", gram)
            arrived, sums, first = after((arrived, sums, first))
        message = rows_of(slots + left * 3 * lines)
        keep, send = in_vmem(
            functools.partial(step_kernel, slots=slots), (message, message), "step", keep, arrived, sums
        )
        if first is None:
            keep, send, now, gram = after((keep, send, here, gram))
        else:
            keep, send, now, first = after((keep, send, here, first))

    by_x = swap(send, 1)
    by_core = swap(keep, 0)
    inverse = in_vmem(finish_kernel, jax.ShapeDtypeStruct((count, count), F32), "finish", *first, scale)
    by_x, by_core, inverse = after((by_x, by_core, inverse))
    by_both = swap(by_x, 0)
    messages = (keep, by_x, by_core, by_both)
    parts = [parts[0], pin(parts[1]), pin(parts[2])]
    return owned(here, bins, owner, begin, span, messages, inverse, parts, own_slots, own_spaxels, 512)


def solution(mesh):
    placed = (
        P("strips", "spax"),
        P(),
        P("strips"),
        P("strips"),
        P(None, "strips"),
        P(None, "strips"),
    )
    return jax.shard_map(
        shards,
        mesh=mesh,
        in_specs=placed,
        out_specs=(P(("strips", "spax"), None), P(None, ("strips", "spax"))),
        check_vma=False,
    )
```

```python
import functools

import jax
import jax.numpy as jnp
from jax import lax
from jax.experimental import pallas as pl
from jax.experimental.pallas import tpu as pltpu
from jax.sharding import PartitionSpec as P

HIGHEST = lax.Precision.HIGHEST
F32 = jnp.float32
BF16 = jnp.bfloat16
LANES = 128
SUB = 8
VMEM_LIMIT = 20 * 1024 * 1024

NT = (((1,), (1,)), ((), ()))
NN = (((1,), (0,)), ((), ()))


def split3(x):
    hi = x.astype(BF16)
    rest = x - hi.astype(F32)
    mid = rest.astype(BF16)
    low = (rest - mid.astype(F32)).astype(BF16)
    return hi, mid, low


def dot(a, b, dims):
    return lax.dot_general(a, b, dims, preferred_element_type=F32)


def dot_f32(a, b, dims):
    return lax.dot_general(a, b, dims, precision=HIGHEST, preferred_element_type=F32)


def template_window(width, full_width):
    return min(full_width, -(-(width + LANES - 1) // LANES) * LANES)


def project_kernel(
    device_ref, bins_ref, begin_ref, span_ref, cube_ref, templates_ref,
    keep_ref, send_ref, begins_ref, spans_ref, held_ref,
    bins_held_ref, sums_ref, window_ref, firsts_ref, cube_sem, small_sem, *, chunk,
):
    width, spaxels = cube_ref.shape
    total_bins = keep_ref.shape[0]
    full_width = templates_ref.shape[1]
    first = device_ref[0] * width
    window = window_ref.shape[1]
    base = pl.multiple_of(jnp.minimum(first // LANES * LANES, full_width - window), LANES)
    chunks = spaxels // chunk
    reach = chunk + SUB

    def cube_copy(i):
        lanes = pl.ds(i * chunk, chunk)
        return pltpu.make_async_copy(cube_ref.at[:, lanes], held_ref.at[pl.ds(0, width), lanes], cube_sem.at[i])

    bins_copy = pltpu.make_async_copy(bins_ref, bins_held_ref, small_sem.at[0])
    firsts_copy = pltpu.make_async_copy(bins_ref, firsts_ref, small_sem.at[1])
    window_copy = pltpu.make_async_copy(templates_ref.at[:, pl.ds(base, window)], window_ref, small_sem.at[2])
    line_copies = [
        pltpu.make_async_copy(begin_ref, begins_ref, small_sem.at[3]),
        pltpu.make_async_copy(span_ref, spans_ref, small_sem.at[4]),
    ]
    for copy in [bins_copy, firsts_copy, window_copy] + [cube_copy(i) for i in range(chunks)] + line_copies:
        copy.start()
    sums_ref[...] = jnp.zeros(sums_ref.shape, F32)
    joined = held_ref.shape[0] > width
    counted = sums_ref.shape[1] - COUNT_ROWS
    if joined:
        held_ref[width:, :] = jnp.ones((COUNT_ROWS, spaxels), F32)
    rows_at = lax.broadcasted_iota(jnp.int32, (reach, chunk), 0)
    bins_copy.wait()
    firsts_copy.wait()
    window_copy.wait()
    mine = pltpu.roll(window_ref[...], window - (first - base), 1)[:, :width]

    for i in range(chunks):
        lanes = slice(i * chunk, (i + 1) * chunk)
        low_bin = pl.multiple_of(firsts_ref[0, i * chunk] // SUB * SUB, SUB)
        rows = pl.ds(low_bin, reach)
        member = jnp.where(rows_at == bins_held_ref[:, lanes] - low_bin, 1.0, 0.0).astype(BF16)
        cube_copy(i).wait()
        hi, mid, low = split3(held_ref[:, lanes])
        new = dot(member, hi, NT) + (dot(member, mid, NT) + dot(member, low, NT))
        if joined:
            sums_ref[rows, :] += new
        else:
            sums_ref[rows, :width] += new
            sums_ref[rows, counted:] += dot(member, jnp.ones((COUNT_ROWS, chunk), BF16), NT)

    low_kept = device_ref[0] % 2 == 0
    block = min(total_bins, 512)
    for at in range(0, total_bins, block):
        rows = slice(at, at + block)
        means = sums_ref[rows, :width] / sums_ref[rows, counted : counted + 1]
        projections = dot_f32(means, mine, NT) * (1.0 / full_width)
        low, high = projections[:, :LANES], projections[:, LANES:]
        keep_ref[rows, :] = jnp.where(low_kept, low, high)
        send_ref[rows, :] = jnp.where(low_kept, high, low)
    for copy in line_copies:
        copy.wait()


COUNT_ROWS = 16


def project(device, bins, begin, span, cube, templates, total_bins):
    width, spaxels = cube.shape
    chunk = min(spaxels, 256)
    wide = -(-width // COUNT_ROWS) * COUNT_ROWS + COUNT_ROWS
    held = width if width % COUNT_ROWS else wide
    count, full_width = templates.shape
    return pl.pallas_call(
        functools.partial(project_kernel, chunk=chunk),
        in_specs=[pl.BlockSpec(memory_space=pltpu.SMEM)] + [pl.BlockSpec(memory_space=pltpu.HBM)] * 5,
        out_specs=[pl.BlockSpec(memory_space=pltpu.VMEM)] * 6,
        out_shape=[
            rows_of(total_bins),
            rows_of(total_bins),
            pltpu.VMEM(begin.shape, jnp.int32),
            pltpu.VMEM(span.shape, jnp.int32),
            pltpu.VMEM((held, spaxels), F32),
            pltpu.VMEM(bins.shape, jnp.int32),
        ],
        scratch_shapes=[
            pltpu.VMEM((total_bins + chunk + SUB, wide), F32),
            pltpu.VMEM((count, template_window(width, full_width)), F32),
            pltpu.SMEM(bins.shape, jnp.int32),
            pltpu.SemaphoreType.DMA((spaxels // chunk,)),
            pltpu.SemaphoreType.DMA((5,)),
        ],
        compiler_params=pltpu.CompilerParams(vmem_limit_bytes=VMEM_LIMIT),
        name="project",
    )(device, bins, begin, span, cube, templates)


def reciprocal(x):
    r = pl.reciprocal(x, approx=True)
    r = r * (2.0 - x * r)
    return r * (2.0 - x * r)


def eliminate(tile, start, stop):
    size = tile.shape[0]
    count = size // SUB
    lanes = lax.broadcasted_iota(jnp.int32, (SUB, size), 1)
    rows_at = lax.broadcasted_iota(jnp.int32, (SUB, size), 0)
    rows = [tile[i * SUB : (i + 1) * SUB, :] for i in range(count)]
    for k in range(start, stop):
        block = rows[k]
        first = k * SUB
        a = {}
        for i in range(SUB):
            for j in range(i, SUB):
                a[i, j] = jnp.broadcast_to(block[i : i + 1, first + j : first + j + 1], (SUB, size))

        def at(i, j):
            return (i, j) if i <= j else (j, i)

        for p in range(0, SUB, 2):
            q = p + 1
            pp, pq, qq = a[p, p], a[p, q], a[q, q]
            inverse = reciprocal(pp * qq - pq * pq)
            others = [i for i in range(SUB) if i not in (p, q)]
            old = {i: (a[at(i, p)], a[at(i, q)]) for i in others}
            new = {
                i: ((u * qq - v * pq) * inverse, (v * pp - u * pq) * inverse) for i, (u, v) in old.items()
            }
            for i in others:
                for j in others:
                    if i <= j:
                        a[i, j] = a[i, j] - new[i][0] * old[j][0] - new[i][1] * old[j][1]
            for i in others:
                a[at(i, p)], a[at(i, q)] = new[i]
            a[p, p], a[p, q], a[q, q] = -(qq * inverse), pq * inverse, -(pp * inverse)
        columns = []
        for j in range(SUB):
            column = a[at(0, j)]
            for i in range(1, SUB):
                column = jnp.where(rows_at == i, a[at(i, j)], column)
            columns.append(column)
        terms = [columns[j] * jnp.broadcast_to(block[j : j + 1, :], (SUB, size)) for j in range(SUB)]
        while len(terms) > 1:
            terms = [x + y for x, y in zip(terms[::2], terms[1::2])]
        swept = -terms[0]
        for j in range(SUB):
            swept = jnp.where(lanes == first + j, columns[j], swept)
        inside = (lanes >= first) & (lanes < first + SUB)
        spread_rows = [jnp.broadcast_to(swept[j : j + 1, :], (SUB, size)) for j in range(SUB)]
        order = list(range(k + 1, count)) + list(range(k))
        for i in order:
            terms = [
                jnp.broadcast_to(rows[i][:, first + j : first + j + 1], (SUB, size)) * spread_rows[j]
                for j in range(SUB)
            ]
            while len(terms) > 1:
                terms = [x + y for x, y in zip(terms[::2], terms[1::2])]
            rows[i] = jnp.where(inside, 0.0, rows[i]) - terms[0]
        rows[k] = swept
    return jnp.concatenate(rows, axis=0)


def gram_kernel(
    templates_ref, gram_ref, scale_ref, hi_ref, mid_ref, low_ref, held_ref, mid_held_ref, low_held_ref, sem, out_sem,
    *, chunk,
):
    count, full_width = templates_ref.shape

    def copy(i):
        lanes = pl.ds(i * chunk, chunk)
        return pltpu.make_async_copy(templates_ref.at[:, lanes], held_ref.at[:, lanes], sem.at[i])

    def out_copies(i):
        lanes = pl.ds(i * chunk, chunk)
        return [
            pltpu.make_async_copy(mid_held_ref.at[:, lanes], mid_ref.at[:, lanes], out_sem.at[0, i]),
            pltpu.make_async_copy(low_held_ref.at[:, lanes], low_ref.at[:, lanes], out_sem.at[1, i]),
        ]

    for i in range(full_width // chunk):
        copy(i).start()
    even = jnp.zeros((count, count), F32)
    mixed = jnp.zeros((count, count), F32)
    for i in range(full_width // chunk):
        copy(i).wait()
        lanes = slice(i * chunk, (i + 1) * chunk)
        hi, mid, low = split3(held_ref[:, lanes])
        hi_ref[:, lanes], mid_held_ref[:, lanes], low_held_ref[:, lanes] = hi, mid, low
        for out in out_copies(i):
            out.start()
        even = even + (dot(hi, hi, NT) + dot(mid, mid, NT))
        mixed = mixed + (dot(hi, mid, NT) + dot(hi, low, NT))
    gram = (even + (mixed + mixed.T)) * (1.0 / full_width)
    same = lax.broadcasted_iota(jnp.int32, gram.shape, 0) == lax.broadcasted_iota(jnp.int32, gram.shape, 1)
    diagonal = jnp.where(same, gram, 0.0)
    row = lax.rsqrt(jnp.sum(diagonal, axis=0, keepdims=True))
    column = lax.rsqrt(jnp.sum(diagonal, axis=1, keepdims=True))
    gram = gram * row * column
    scale_ref[...] = row
    gram_ref[...] = gram
    for i in range(full_width // chunk):
        for out in out_copies(i):
            out.wait()


def scaled_gram(templates, chunk):
    count, full_width = templates.shape
    vmem, hbm = (pl.BlockSpec(memory_space=space) for space in (pltpu.VMEM, pltpu.HBM))
    return pl.pallas_call(
        functools.partial(gram_kernel, chunk=chunk),
        in_specs=[hbm],
        out_specs=(vmem, vmem, vmem, hbm, hbm),
        out_shape=(
            jax.ShapeDtypeStruct((count, count), F32),
            jax.ShapeDtypeStruct((1, count), F32),
            pltpu.VMEM((count, full_width), BF16),
            pltpu.HBM((count, full_width), BF16),
            pltpu.HBM((count, full_width), BF16),
        ),
        scratch_shapes=[
            pltpu.VMEM((count, full_width), F32),
            pltpu.VMEM((count, full_width), BF16),
            pltpu.VMEM((count, full_width), BF16),
            pltpu.SemaphoreType.DMA((full_width // chunk,)),
            pltpu.SemaphoreType.DMA((2, full_width // chunk)),
        ],
        compiler_params=pltpu.CompilerParams(vmem_limit_bytes=VMEM_LIMIT),
        name="gram",
    )(templates)


STEPS = LANES // SUB
EARLY = 4


def first_kernel(gram_ref, first_ref, half_ref, second_ref):
    first = -eliminate(gram_ref[:LANES, :LANES], 0, STEPS)
    side = gram_ref[:LANES, LANES:]
    half = dot_f32(first, side, NN)
    first_ref[...] = first
    half_ref[...] = half
    second_ref[...] = eliminate(gram_ref[LANES:, LANES:] - dot_f32(side.T, half, NN), 0, EARLY)


def finish_kernel(first_ref, half_ref, second_ref, scale_ref, out_ref):
    first, half = first_ref[...], half_ref[...]
    last = -eliminate(second_ref[...], EARLY, STEPS)
    cross = dot_f32(half, last, NN)
    row = scale_ref[...]
    column = jnp.broadcast_to(row, (SUB, row.shape[1])).T[:, :1]
    near, far = row[:, :LANES], row[:, LANES:]
    out_ref[:LANES, :LANES] = (first + dot_f32(cross, half, NT)) * near * column[:LANES]
    out_ref[:LANES, LANES:] = -cross * far * column[:LANES]
    out_ref[LANES:, :LANES] = -cross.T * near * column[LANES:]
    out_ref[LANES:, LANES:] = last * far * column[LANES:]


def in_vmem(kernel, shapes, name, *arrays):
    return pl.pallas_call(
        kernel,
        out_shape=shapes,
        compiler_params=pltpu.CompilerParams(vmem_limit_bytes=VMEM_LIMIT),
        name=name,
    )(*arrays)


def window_sums(read, rows, first, begin, span):
    lines = begin.shape[0]
    sub = lax.broadcasted_iota(jnp.int32, (SUB, LANES), 0)
    spans = [jnp.broadcast_to(span[j : j + 1], (SUB, LANES)).astype(F32) for j in range(lines)]
    offsets = [
        (2 * (first + sub - jnp.broadcast_to(begin[j : j + 1], (SUB, LANES))) + 1).astype(F32) - spans[j]
        for j in range(lines)
    ]

    def add(block, shift, sums):
        size = block.shape[0]
        out = []
        for j in range(lines):
            m = offsets[j][:size] + shift
            masked = jnp.where(jnp.abs(m) < spans[j][:size], block, 0.0)
            weighted = masked * m
            out += [sums[3 * j] + masked, sums[3 * j + 1] + weighted, sums[3 * j + 2] + weighted * m]
        return out

    full = rows // SUB
    out = [jnp.zeros((1, LANES), F32)] * (3 * lines)
    if full:
        sums = [jnp.zeros((SUB, LANES), F32)] * (3 * lines)
        for i in range(full):
            sums = add(read(i * SUB, SUB), 2.0 * i * SUB, sums)
        out = [jnp.sum(x, axis=0, keepdims=True) for x in sums]
    if rows % SUB:
        sums = [jnp.zeros((rows % SUB, LANES), F32)] * (3 * lines)
        sums = add(read(full * SUB, rows % SUB), 2.0 * full * SUB, sums)
        out = [x + jnp.sum(y, axis=0, keepdims=True) for x, y in zip(out, sums)]
    return [out[3 * j + k] for k in range(3) for j in range(lines)]


def halving_order(devices):
    bits = devices.bit_length() - 1
    return list(range(2, bits)) + [1, 0]


def flips(position, devices):
    order = halving_order(devices)
    return sum(((position >> (len(order) - 1 - t)) & 1) << bit for t, bit in enumerate(order))


def cube_kernel(device_ref, begin_ref, span_ref, cube_ref, out_ref, *, devices, start, width):
    device = device_ref[0]
    rows = 3 * begin_ref.shape[0]

    def owner(i, carry):
        lanes = pl.ds(pl.multiple_of((device ^ flips(start + i, devices)) * LANES, LANES), LANES)
        sums = window_sums(
            lambda row, size: cube_ref[row : row + size, lanes],
            width,
            device * width,
            begin_ref[:, lanes],
            span_ref[:, lanes],
        )
        out_ref[pl.ds(pl.multiple_of(i * rows, SUB), rows), :] = jnp.concatenate(sums, axis=0)
        return carry

    lax.fori_loop(0, out_ref.shape[0] // rows, owner, 0)


def cube_windows(device, begin, span, cube, devices, start, stop, width):
    vmem = pl.BlockSpec(memory_space=pltpu.VMEM)
    return pl.pallas_call(
        functools.partial(cube_kernel, devices=devices, start=start, width=width),
        in_specs=[pl.BlockSpec(memory_space=pltpu.SMEM), vmem, vmem, vmem],
        out_shape=rows_of((stop - start) * 3 * begin.shape[0]),
        compiler_params=pltpu.CompilerParams(vmem_limit_bytes=VMEM_LIMIT),
        name="cube_windows",
    )(device, begin, span, cube)


def split_kernel(device_ref, x_ref, y_ref, keep_ref, send_ref):
    half = keep_ref.shape[0]
    total = x_ref[...] + y_ref[...]
    low_kept = (device_ref[0] >> 1) % 2 == 0
    keep_ref[...] = jnp.where(low_kept, total[:half], total[half:])
    send_ref[...] = jnp.where(low_kept, total[half:], total[:half])


def join_kernel(x_ref, y_ref, early_ref, late_ref, keep_ref, send_ref):
    slots, early = x_ref.shape[0], early_ref.shape[0]
    total = x_ref[...] + y_ref[...]
    keep_ref[...] = total
    send_ref[:slots, :] = total
    send_ref[slots : slots + early, :] = early_ref[...]
    send_ref[slots + early :, :] = late_ref[...]


def step_kernel(x_ref, y_ref, sums_ref, keep_ref, send_ref, *, slots):
    half = (y_ref.shape[0] - slots) // 2
    own = sums_ref.shape[0]
    total = x_ref[:slots, :] + y_ref[:slots, :]

    def gathered(first):
        value = y_ref[slots + first : slots + first + half, :]
        if x_ref.shape[0] > slots:
            value = value + x_ref[slots + first : slots + first + half, :]
        return value

    kept, sent = gathered(0), gathered(half) + sums_ref[own - half :, :]
    if own > half:
        kept = kept + sums_ref[:half, :]
    keep_ref[:slots, :] = total
    keep_ref[slots:, :] = kept
    send_ref[:slots, :] = total
    send_ref[slots:, :] = sent


def rows_of(count):
    return jax.ShapeDtypeStruct((count, LANES), F32)


def split_slots(device, x, y):
    vmem = pl.BlockSpec(memory_space=pltpu.VMEM)
    half = rows_of(x.shape[0] // 2)
    return pl.pallas_call(
        split_kernel,
        in_specs=[pl.BlockSpec(memory_space=pltpu.SMEM), vmem, vmem],
        out_shape=(half, half),
        compiler_params=pltpu.CompilerParams(vmem_limit_bytes=VMEM_LIMIT),
        name="split_slots",
    )(device, x, y)


def pick(bins_ref, device, lows, blocks, own, half):
    bins = bins_ref[:, pl.ds(pl.multiple_of(device * own, LANES), own)]
    bins = jnp.broadcast_to(bins, (SUB, own)).T[:, :1]
    total = None
    for low_bin, block in zip(lows, blocks):
        at = lax.broadcasted_iota(jnp.int32, (own, half), 1)
        member = jnp.where(at == bins - low_bin, 1.0, 0.0).astype(BF16)
        hi, mid, low = split3(block[:half, :])
        value = dot(member, hi, NN) + (dot(member, mid, NN) + dot(member, low, NN))
        total = value if total is None else total + value
    return total


def pick_kernel(device_ref, bins_ref, kept_ref, by_x_ref, by_core_ref, near_ref, far_ref, *, half):
    device = device_ref[0]
    own = near_ref.shape[0]
    kept_first = jnp.where((device >> 1) % 2 == 0, 0, half)
    lows = (kept_first, half - kept_first)
    near_ref[...] = pick(bins_ref, device, lows, (kept_ref, by_x_ref), own, half)
    far_ref[...] = pick(bins_ref, device, lows[:1], (by_core_ref,), own, half)


def pick_early(device, bins, kept, by_x, by_core, own, half):
    vmem = pl.BlockSpec(memory_space=pltpu.VMEM)
    return pl.pallas_call(
        functools.partial(pick_kernel, half=half),
        in_specs=[pl.BlockSpec(memory_space=pltpu.SMEM)] + [vmem] * 4,
        out_shape=(rows_of(own), rows_of(own)),
        compiler_params=pltpu.CompilerParams(vmem_limit_bytes=VMEM_LIMIT),
        name="pick_early",
    )(device, bins, kept, by_x, by_core)


def owner_kernel(
    device_ref, bins_ref, owner_ref, begin_ref, span_ref,
    kept_ref, by_x_ref, by_core_ref, by_both_ref, near_ref, far_ref, inverse_ref, hi_ref, mid_ref, low_ref,
    weights_ref, out_ref,
    continuum_ref, mine_ref, mid_held_ref, low_held_ref, owner_held_ref, begins_ref, spans_ref, starts_ref,
    parts_sem, small_sem, *, chunk,
):
    own_slots = weights_ref.shape[0]
    own = begins_ref.shape[1]
    lines = begin_ref.shape[0]
    full_width = hi_ref.shape[1]
    half = owner_held_ref.shape[1] // 2
    inverse = inverse_ref[...]
    device = device_ref[0]
    own_lanes = pl.ds(pl.multiple_of(device * own, LANES), own)

    small_copies = [
        pltpu.make_async_copy(owner_ref, owner_held_ref, small_sem.at[1]),
        pltpu.make_async_copy(begin_ref.at[:, own_lanes], begins_ref, small_sem.at[2]),
        pltpu.make_async_copy(span_ref.at[:, own_lanes], spans_ref, small_sem.at[3]),
        pltpu.make_async_copy(begin_ref.at[:, own_lanes], starts_ref, small_sem.at[4]),
    ]
    part_copies = [
        pltpu.make_async_copy(mid_ref, mid_held_ref, parts_sem.at[0]),
        pltpu.make_async_copy(low_ref, low_held_ref, parts_sem.at[1]),
    ]
    for copy in small_copies + part_copies:
        copy.start()

    core_low = device % 2 == 0
    low_kept = (device >> 1) % 2 == 0

    def lane_halves(near, far):
        return jnp.where(core_low, near, far), jnp.where(core_low, far, near)

    def by_lanes(near, far):
        return jnp.concatenate(lane_halves(near, far), axis=1)

    for copy in small_copies:
        copy.wait()

    kept_first = jnp.where(low_kept, 0, half)
    for i in range(own_slots):
        picked_bin = owner_held_ref[0, device * own_slots + i]
        in_kept = (picked_bin >= half) == (kept_first > 0)
        row = pl.ds(picked_bin - jnp.where(picked_bin >= half, half, 0), 1)
        low, high = lane_halves(
            jnp.where(in_kept, kept_ref[row, :], by_x_ref[row, :]),
            jnp.where(in_kept, by_core_ref[row, :], by_both_ref[row, :]),
        )
        mine_ref[i : i + 1, :LANES] = low
        mine_ref[i : i + 1, LANES:] = high
    weights_ref[...] = dot_f32(mine_ref[...], inverse, NN)

    far = far_ref[...] + pick(bins_ref, device, (half - kept_first,), (by_both_ref,), own, half)
    spaxel_weights = dot_f32(by_lanes(near_ref[...], far), inverse, NN)

    hi, mid, low = split3(spaxel_weights)
    tiles = chunk // LANES
    for i in range(full_width // chunk):
        first = hi_ref[:, i * chunk : (i + 1) * chunk]
        value = dot(hi, first, NN) + (dot(mid, first, NN) + dot(low, first, NN))
        for t in range(tiles):
            continuum_ref[2 * (i * tiles + t)] = value[:, t * LANES : (t + 1) * LANES]
    for copy in part_copies:
        copy.wait()
    left_half = lax.broadcasted_iota(jnp.int32, (own, LANES), 1) < LANES // 2
    before = None
    for i in range(full_width // chunk):
        lanes = slice(i * chunk, (i + 1) * chunk)
        second, third = mid_held_ref[:, lanes], low_held_ref[:, lanes]
        value = dot(hi, second, NN) + (dot(mid, second, NN) + dot(hi, third, NN))
        for t in range(tiles):
            at = 2 * (i * tiles + t)
            tile = continuum_ref[at] + value[:, t * LANES : (t + 1) * LANES]
            continuum_ref[at] = tile
            turned = pltpu.roll(tile, LANES // 2, 1)
            if at:
                continuum_ref[at - 1] = jnp.where(left_half, before, turned)
            before = turned
    continuum_ref[2 * (full_width // LANES) - 1] = jnp.where(left_half, before, 0.0)

    begin = begins_ref[...]
    span = spans_ref[...].astype(F32)
    centre = 2.0 * (begin & (LANES // 2 - 1)).astype(F32) + span - 1.0
    rows_at = lax.broadcasted_iota(jnp.int32, (SUB, LANES), 0)
    at_row = [rows_at == r for r in range(SUB)]
    twice = 2.0 * lax.broadcasted_iota(jnp.int32, (LANES, own), 0).astype(F32)
    sums = [None] * (3 * lines)
    for j in range(lines):
        picks = []
        for g in range(own // SUB):
            rows = slice(g * SUB, (g + 1) * SUB)
            block = None
            for r in range(SUB):
                tile = continuum_ref[lax.shift_right_logical(starts_ref[j, g * SUB + r], 6), rows, :]
                block = tile if block is None else jnp.where(at_row[r], tile, block)
            picks.append(block)
        m = twice - centre[j : j + 1]
        masked = jnp.where(jnp.abs(m) < span[j : j + 1], jnp.concatenate(picks, axis=0).T, 0.0)
        weighted = masked * m
        for k, term in enumerate((masked, weighted, weighted * m)):
            sums[k * lines + j] = jnp.sum(term, axis=0, keepdims=True)
    continuum_sums = jnp.concatenate(sums, axis=0)

    own_rows = slice(half, half + 3 * lines)
    other_rows = slice(half + 3 * lines, half + 6 * lines)
    cube_sums = (kept_ref[own_rows, :] + by_x_ref[own_rows, :]) + (
        by_core_ref[other_rows, :] + by_both_ref[other_rows, :]
    )
    scale = jnp.concatenate([span, span * span, span * span * span], axis=0)
    out_ref[...] = (cube_sums - continuum_sums) / scale


def owned(device, bins, owner, begin, span, messages, inverse, parts, own_slots, own, chunk):
    vmem = pl.BlockSpec(memory_space=pltpu.VMEM)
    hbm = pl.BlockSpec(memory_space=pltpu.HBM)
    count, full_width = parts[0].shape
    lines = begin.shape[0]
    return pl.pallas_call(
        functools.partial(owner_kernel, chunk=chunk),
        in_specs=[pl.BlockSpec(memory_space=pltpu.SMEM)] + [vmem] + [hbm] * 3 + [vmem] * 8 + [hbm] * 2,
        out_shape=(
            jax.ShapeDtypeStruct((own_slots, count), F32),
            jax.ShapeDtypeStruct((3 * lines, own), F32),
        ),
        scratch_shapes=[
            pltpu.VMEM((2 * (full_width // LANES), own, LANES), F32),
            pltpu.VMEM((own_slots, count), F32),
            pltpu.VMEM((count, full_width), BF16),
            pltpu.VMEM((count, full_width), BF16),
            pltpu.SMEM(owner.shape, jnp.int32),
            pltpu.VMEM((lines, own), jnp.int32),
            pltpu.VMEM((lines, own), jnp.int32),
            pltpu.SMEM((lines, own), jnp.int32),
            pltpu.SemaphoreType.DMA((2,)),
            pltpu.SemaphoreType.DMA((5,)),
        ],
        compiler_params=pltpu.CompilerParams(vmem_limit_bytes=VMEM_LIMIT),
        name="owned",
    )(device, bins, owner, begin, span, *messages, inverse, *parts)


def shards(cube, templates, bin_id, owner_bins, line_start, line_width):
    devices = lax.axis_size("spax")
    device = lax.axis_index("spax")
    spaxels = cube.shape[0]
    total_bins = owner_bins.shape[0]
    count = templates.shape[0]
    lines = line_start.shape[0]
    own_spaxels = spaxels // devices
    own_slots = total_bins // devices
    here = device.reshape(1).astype(jnp.int32)
    pin = lambda x: pltpu.with_memory_space_constraint(x, pltpu.HBM)
    columns = pin(cube.T)
    begin, span = pin(line_start), pin(line_width)
    bins, owner = pin(bin_id[None, :]), pin(owner_bins[None, :])
    after = lax.optimization_barrier

    def swap(x, bit):
        return lax.ppermute(x, "spax", [(d, d ^ (1 << bit)) for d in range(devices)])

    keep, send, begins, spans, held, bins_held = project(here, bins, begin, span, columns, pin(templates), total_bins)
    windows = lambda start, stop, now: cube_windows(
        now, begins, spans, held, devices, start, stop, cube.shape[1]
    )
    arrived = swap(send, 0)
    left = devices // 2
    cut = left + devices * 3 // 16
    early = windows(left, cut, here)
    keep, arrived, early = after((keep, arrived, early))
    keep, send = split_slots(here, keep, arrived)
    keep, send, now = after((keep, send, here))
    arrived = swap(send, 1)
    late, next_sums = windows(cut, devices, now), windows(left // 2, left, now)
    keep, arrived, early, late, next_sums, templates = after((keep, arrived, early, late, next_sums, templates))
    slots = total_bins // 2
    message = rows_of(slots + left * 3 * lines)
    keep, send = in_vmem(join_kernel, (rows_of(slots), message), "join", keep, arrived, early, late)

    keep, send, now, templates = after((keep, send, here, templates))
    gram = first = None
    for bit in range(2, devices.bit_length() - 1):
        arrived = swap(send, bit)
        left //= 2
        last_step = bit == devices.bit_length() - 2
        sums = next_sums if gram is None else windows(0 if last_step else left, 2 * left, now)
        if gram is None:
            gram, scale, *parts = scaled_gram(pin(templates), 512)
            arrived, sums, gram = after((arrived, sums, gram))
        elif first is None:
            first = in_vmem(first_kernel, [rows_of(LANES)] * 3, "first", gram)
            arrived, sums, first = after((arrived, sums, first))
        message = rows_of(slots + left * 3 * lines)
        keep, send = in_vmem(
            functools.partial(step_kernel, slots=slots), (message, message), "step", keep, arrived, sums
        )
        if first is None:
            keep, send, now, gram = after((keep, send, here, gram))
        else:
            keep, send, now, first = after((keep, send, here, first))

    by_x = swap(send, 1)
    by_core = swap(keep, 0)
    inverse = in_vmem(finish_kernel, jax.ShapeDtypeStruct((count, count), F32), "finish", *first, scale)
    by_x, by_core, inverse = after((by_x, by_core, inverse))
    by_both = swap(by_x, 0)
    near, far = pick_early(here, bins_held, keep, by_x, by_core, own_spaxels, slots)
    by_both, near, far = after((by_both, near, far))
    messages = (keep, by_x, by_core, by_both, near, far)
    parts = [parts[0], pin(parts[1]), pin(parts[2])]
    return owned(here, bins_held, owner, begin, span, messages, inverse, parts, own_slots, own_spaxels, 512)


def solution(mesh):
    placed = (
        P("strips", "spax"),
        P(),
        P("strips"),
        P("strips"),
        P(None, "strips"),
        P(None, "strips"),
    )
    return jax.shard_map(
        shards,
        mesh=mesh,
        in_specs=placed,
        out_specs=(P(("strips", "spax"), None), P(None, ("strips", "spax"))),
        check_vma=False,
    )
```

```python
import functools

import jax
import jax.numpy as jnp
from jax import lax
from jax.experimental import pallas as pl
from jax.experimental.pallas import tpu as pltpu
from jax.sharding import PartitionSpec as P

HIGHEST = lax.Precision.HIGHEST
F32 = jnp.float32
BF16 = jnp.bfloat16
LANES = 128
SUB = 8
VMEM_LIMIT = 20 * 1024 * 1024

NT = (((1,), (1,)), ((), ()))
NN = (((1,), (0,)), ((), ()))


def split3(x):
    hi = x.astype(BF16)
    rest = x - hi.astype(F32)
    mid = rest.astype(BF16)
    low = (rest - mid.astype(F32)).astype(BF16)
    return hi, mid, low


def dot(a, b, dims):
    return lax.dot_general(a, b, dims, preferred_element_type=F32)


def dot_f32(a, b, dims):
    return lax.dot_general(a, b, dims, precision=HIGHEST, preferred_element_type=F32)


def template_window(width, full_width):
    return min(full_width, -(-(width + LANES - 1) // LANES) * LANES)


def project_kernel(
    device_ref, bins_ref, begin_ref, span_ref, cube_ref, templates_ref,
    keep_ref, send_ref, begins_ref, spans_ref, held_ref,
    bins_held_ref, sums_ref, parts_ref, window_ref, firsts_ref, cube_sem, small_sem, *, chunk,
):
    width, spaxels = cube_ref.shape
    total_bins = keep_ref.shape[0]
    full_width = templates_ref.shape[1]
    first = device_ref[0] * width
    window = window_ref.shape[1]
    base = pl.multiple_of(jnp.minimum(first // LANES * LANES, full_width - window), LANES)
    chunks = spaxels // chunk
    reach = chunk + SUB
    pieces = cube_sem.shape[0]

    def cube_copy(i):
        lanes = pl.ds(i * (spaxels // pieces), spaxels // pieces)
        return pltpu.make_async_copy(cube_ref.at[:, lanes], held_ref.at[pl.ds(0, width), lanes], cube_sem.at[i])

    bins_copy = pltpu.make_async_copy(bins_ref, bins_held_ref, small_sem.at[0])
    firsts_copy = pltpu.make_async_copy(bins_ref, firsts_ref, small_sem.at[1])
    window_copy = pltpu.make_async_copy(templates_ref.at[:, pl.ds(base, window)], window_ref, small_sem.at[2])
    line_copies = [
        pltpu.make_async_copy(begin_ref, begins_ref, small_sem.at[3]),
        pltpu.make_async_copy(span_ref, spans_ref, small_sem.at[4]),
    ]
    for copy in [bins_copy, firsts_copy] + [cube_copy(i) for i in range(pieces)] + [window_copy] + line_copies:
        copy.start()
    sums_ref[...] = jnp.zeros(sums_ref.shape, F32)
    joined = held_ref.shape[0] > width
    counted = sums_ref.shape[1] - COUNT_ROWS
    if joined:
        held_ref[width:, :] = jnp.ones((COUNT_ROWS, spaxels), F32)
    rows_at = lax.broadcasted_iota(jnp.int32, (reach, chunk), 0)
    bins_copy.wait()
    firsts_copy.wait()

    def low_bin(i):
        return pl.multiple_of(firsts_ref[0, i * chunk] // SUB * SUB, SUB)

    for i in range(chunks):
        if i % (chunks // pieces) == 0:
            cube_copy(i // (chunks // pieces)).wait()
        lanes = slice(i * chunk, (i + 1) * chunk)
        member = jnp.where(rows_at == bins_held_ref[:, lanes] - low_bin(i), 1.0, 0.0).astype(BF16)
        hi, mid, low = split3(held_ref[:, lanes])
        new = dot(member, hi, NT) + (dot(member, mid, NT) + dot(member, low, NT))
        if joined:
            parts_ref[i] = new
        else:
            parts_ref[i] = jnp.zeros(parts_ref.shape[1:], F32)
            parts_ref[i, :, :width] = new
            parts_ref[i, :, counted:] = dot(member, jnp.ones((COUNT_ROWS, chunk), BF16), NT)
    for i in range(chunks):
        sums_ref[pl.ds(low_bin(i), reach), :] += parts_ref[i]
    window_copy.wait()
    mine = pltpu.roll(window_ref[...], window - (first - base), 1)[:, :width]
    low_kept = device_ref[0] % 2 == 0
    block = min(total_bins, 512)
    for at in range(0, total_bins, block):
        rows = slice(at, at + block)
        means = sums_ref[rows, :width] / sums_ref[rows, counted : counted + 1]
        projections = dot_f32(means, mine, NT) * (1.0 / full_width)
        low, high = projections[:, :LANES], projections[:, LANES:]
        keep_ref[rows, :] = jnp.where(low_kept, low, high)
        send_ref[rows, :] = jnp.where(low_kept, high, low)
    for copy in line_copies:
        copy.wait()


COUNT_ROWS = 16


def project(device, bins, begin, span, cube, templates, total_bins):
    width, spaxels = cube.shape
    chunk = min(spaxels, 256)
    wide = -(-width // COUNT_ROWS) * COUNT_ROWS + COUNT_ROWS
    held = width if width % COUNT_ROWS else wide
    count, full_width = templates.shape
    return pl.pallas_call(
        functools.partial(project_kernel, chunk=chunk),
        in_specs=[pl.BlockSpec(memory_space=pltpu.SMEM)] + [pl.BlockSpec(memory_space=pltpu.HBM)] * 5,
        out_specs=[pl.BlockSpec(memory_space=pltpu.VMEM)] * 6,
        out_shape=[
            rows_of(total_bins),
            rows_of(total_bins),
            pltpu.VMEM(begin.shape, jnp.int32),
            pltpu.VMEM(span.shape, jnp.int32),
            pltpu.VMEM((held, spaxels), F32),
            pltpu.VMEM(bins.shape, jnp.int32),
        ],
        scratch_shapes=[
            pltpu.VMEM((total_bins + chunk + SUB, wide), F32),
            pltpu.VMEM((spaxels // chunk, chunk + SUB, wide), F32),
            pltpu.VMEM((count, template_window(width, full_width)), F32),
            pltpu.SMEM(bins.shape, jnp.int32),
            pltpu.SemaphoreType.DMA((min(spaxels // chunk, 2),)),
            pltpu.SemaphoreType.DMA((5,)),
        ],
        compiler_params=pltpu.CompilerParams(vmem_limit_bytes=VMEM_LIMIT),
        name="project",
    )(device, bins, begin, span, cube, templates)


def reciprocal(x):
    r = pl.reciprocal(x, approx=True)
    r = r * (2.0 - x * r)
    return r * (2.0 - x * r)


def eliminate(tile, start, stop):
    size = tile.shape[0]
    count = size // SUB
    lanes = lax.broadcasted_iota(jnp.int32, (SUB, size), 1)
    rows_at = lax.broadcasted_iota(jnp.int32, (SUB, size), 0)
    rows = [tile[i * SUB : (i + 1) * SUB, :] for i in range(count)]
    for k in range(start, stop):
        block = rows[k]
        first = k * SUB
        a = {}
        for i in range(SUB):
            for j in range(i, SUB):
                a[i, j] = jnp.broadcast_to(block[i : i + 1, first + j : first + j + 1], (SUB, size))

        def at(i, j):
            return (i, j) if i <= j else (j, i)

        for p in range(0, SUB, 2):
            q = p + 1
            pp, pq, qq = a[p, p], a[p, q], a[q, q]
            inverse = reciprocal(pp * qq - pq * pq)
            others = [i for i in range(SUB) if i not in (p, q)]
            old = {i: (a[at(i, p)], a[at(i, q)]) for i in others}
            new = {
                i: ((u * qq - v * pq) * inverse, (v * pp - u * pq) * inverse) for i, (u, v) in old.items()
            }
            for i in others:
                for j in others:
                    if i <= j:
                        a[i, j] = a[i, j] - new[i][0] * old[j][0] - new[i][1] * old[j][1]
            for i in others:
                a[at(i, p)], a[at(i, q)] = new[i]
            a[p, p], a[p, q], a[q, q] = -(qq * inverse), pq * inverse, -(pp * inverse)
        columns = []
        for j in range(SUB):
            column = a[at(0, j)]
            for i in range(1, SUB):
                column = jnp.where(rows_at == i, a[at(i, j)], column)
            columns.append(column)
        terms = [columns[j] * jnp.broadcast_to(block[j : j + 1, :], (SUB, size)) for j in range(SUB)]
        while len(terms) > 1:
            terms = [x + y for x, y in zip(terms[::2], terms[1::2])]
        swept = -terms[0]
        for j in range(SUB):
            swept = jnp.where(lanes == first + j, columns[j], swept)
        inside = (lanes >= first) & (lanes < first + SUB)
        spread_rows = [jnp.broadcast_to(swept[j : j + 1, :], (SUB, size)) for j in range(SUB)]
        order = list(range(k + 1, count)) + list(range(k))
        for i in order:
            terms = [
                jnp.broadcast_to(rows[i][:, first + j : first + j + 1], (SUB, size)) * spread_rows[j]
                for j in range(SUB)
            ]
            while len(terms) > 1:
                terms = [x + y for x, y in zip(terms[::2], terms[1::2])]
            rows[i] = jnp.where(inside, 0.0, rows[i]) - terms[0]
        rows[k] = swept
    return jnp.concatenate(rows, axis=0)


def gram_kernel(
    templates_ref, gram_ref, scale_ref, hi_ref, mid_ref, low_ref, held_ref, mid_held_ref, low_held_ref, sem, out_sem,
    *, chunk,
):
    count, full_width = templates_ref.shape

    def copy(i):
        lanes = pl.ds(i * chunk, chunk)
        return pltpu.make_async_copy(templates_ref.at[:, lanes], held_ref.at[:, lanes], sem.at[i])

    def out_copies(i):
        lanes = pl.ds(i * chunk, chunk)
        return [
            pltpu.make_async_copy(mid_held_ref.at[:, lanes], mid_ref.at[:, lanes], out_sem.at[0, i]),
            pltpu.make_async_copy(low_held_ref.at[:, lanes], low_ref.at[:, lanes], out_sem.at[1, i]),
        ]

    for i in range(full_width // chunk):
        copy(i).start()
    even = jnp.zeros((count, count), F32)
    mixed = jnp.zeros((count, count), F32)
    for i in range(full_width // chunk):
        copy(i).wait()
        lanes = slice(i * chunk, (i + 1) * chunk)
        hi, mid, low = split3(held_ref[:, lanes])
        hi_ref[:, lanes], mid_held_ref[:, lanes], low_held_ref[:, lanes] = hi, mid, low
        for out in out_copies(i):
            out.start()
        even = even + (dot(hi, hi, NT) + dot(mid, mid, NT))
        mixed = mixed + (dot(hi, mid, NT) + dot(hi, low, NT))
    gram = (even + (mixed + mixed.T)) * (1.0 / full_width)
    same = lax.broadcasted_iota(jnp.int32, gram.shape, 0) == lax.broadcasted_iota(jnp.int32, gram.shape, 1)
    diagonal = jnp.where(same, gram, 0.0)
    row = lax.rsqrt(jnp.sum(diagonal, axis=0, keepdims=True))
    column = lax.rsqrt(jnp.sum(diagonal, axis=1, keepdims=True))
    gram = gram * row * column
    scale_ref[...] = row
    gram_ref[...] = gram
    for i in range(full_width // chunk):
        for out in out_copies(i):
            out.wait()


def scaled_gram(templates, chunk):
    count, full_width = templates.shape
    vmem, hbm = (pl.BlockSpec(memory_space=space) for space in (pltpu.VMEM, pltpu.HBM))
    return pl.pallas_call(
        functools.partial(gram_kernel, chunk=chunk),
        in_specs=[hbm],
        out_specs=(vmem, vmem, vmem, hbm, hbm),
        out_shape=(
            jax.ShapeDtypeStruct((count, count), F32),
            jax.ShapeDtypeStruct((1, count), F32),
            pltpu.VMEM((count, full_width), BF16),
            pltpu.HBM((count, full_width), BF16),
            pltpu.HBM((count, full_width), BF16),
        ),
        scratch_shapes=[
            pltpu.VMEM((count, full_width), F32),
            pltpu.VMEM((count, full_width), BF16),
            pltpu.VMEM((count, full_width), BF16),
            pltpu.SemaphoreType.DMA((full_width // chunk,)),
            pltpu.SemaphoreType.DMA((2, full_width // chunk)),
        ],
        compiler_params=pltpu.CompilerParams(vmem_limit_bytes=VMEM_LIMIT),
        name="gram",
    )(templates)


STEPS = LANES // SUB
EARLY = 4


def first_kernel(gram_ref, first_ref, half_ref, second_ref):
    first = -eliminate(gram_ref[:LANES, :LANES], 0, STEPS)
    side = gram_ref[:LANES, LANES:]
    half = dot_f32(first, side, NN)
    first_ref[...] = first
    half_ref[...] = half
    second_ref[...] = eliminate(gram_ref[LANES:, LANES:] - dot_f32(side.T, half, NN), 0, EARLY)


def finish_kernel(first_ref, half_ref, second_ref, scale_ref, out_ref):
    first, half = first_ref[...], half_ref[...]
    last = -eliminate(second_ref[...], EARLY, STEPS)
    cross = dot_f32(half, last, NN)
    row = scale_ref[...]
    column = jnp.broadcast_to(row, (SUB, row.shape[1])).T[:, :1]
    near, far = row[:, :LANES], row[:, LANES:]
    out_ref[:LANES, :LANES] = (first + dot_f32(cross, half, NT)) * near * column[:LANES]
    out_ref[:LANES, LANES:] = -cross * far * column[:LANES]
    out_ref[LANES:, :LANES] = -cross.T * near * column[LANES:]
    out_ref[LANES:, LANES:] = last * far * column[LANES:]


def in_vmem(kernel, shapes, name, *arrays):
    return pl.pallas_call(
        kernel,
        out_shape=shapes,
        compiler_params=pltpu.CompilerParams(vmem_limit_bytes=VMEM_LIMIT),
        name=name,
    )(*arrays)


def window_sums(read, rows, first, begin, span):
    lines = begin.shape[0]
    sub = lax.broadcasted_iota(jnp.int32, (SUB, LANES), 0)
    spans = [jnp.broadcast_to(span[j : j + 1], (SUB, LANES)).astype(F32) for j in range(lines)]
    offsets = [
        (2 * (first + sub - jnp.broadcast_to(begin[j : j + 1], (SUB, LANES))) + 1).astype(F32) - spans[j]
        for j in range(lines)
    ]

    def add(block, shift, sums):
        size = block.shape[0]
        out = []
        for j in range(lines):
            m = offsets[j][:size] + shift
            masked = jnp.where(jnp.abs(m) < spans[j][:size], block, 0.0)
            weighted = masked * m
            out += [sums[3 * j] + masked, sums[3 * j + 1] + weighted, sums[3 * j + 2] + weighted * m]
        return out

    full = rows // SUB
    out = [jnp.zeros((1, LANES), F32)] * (3 * lines)
    if full:
        sums = [jnp.zeros((SUB, LANES), F32)] * (3 * lines)
        for i in range(full):
            sums = add(read(i * SUB, SUB), 2.0 * i * SUB, sums)
        out = [jnp.sum(x, axis=0, keepdims=True) for x in sums]
    if rows % SUB:
        sums = [jnp.zeros((rows % SUB, LANES), F32)] * (3 * lines)
        sums = add(read(full * SUB, rows % SUB), 2.0 * full * SUB, sums)
        out = [x + jnp.sum(y, axis=0, keepdims=True) for x, y in zip(out, sums)]
    return [out[3 * j + k] for k in range(3) for j in range(lines)]


def halving_order(devices):
    bits = devices.bit_length() - 1
    return list(range(2, bits)) + [1, 0]


def flips(position, devices):
    order = halving_order(devices)
    return sum(((position >> (len(order) - 1 - t)) & 1) << bit for t, bit in enumerate(order))


def cube_kernel(device_ref, begin_ref, span_ref, cube_ref, out_ref, *, devices, start, width):
    device = device_ref[0]
    rows = 3 * begin_ref.shape[0]

    def owner(i, carry):
        lanes = pl.ds(pl.multiple_of((device ^ flips(start + i, devices)) * LANES, LANES), LANES)
        sums = window_sums(
            lambda row, size: cube_ref[row : row + size, lanes],
            width,
            device * width,
            begin_ref[:, lanes],
            span_ref[:, lanes],
        )
        out_ref[pl.ds(pl.multiple_of(i * rows, SUB), rows), :] = jnp.concatenate(sums, axis=0)
        return carry

    lax.fori_loop(0, out_ref.shape[0] // rows, owner, 0)


def cube_windows(device, begin, span, cube, devices, start, stop, width):
    vmem = pl.BlockSpec(memory_space=pltpu.VMEM)
    return pl.pallas_call(
        functools.partial(cube_kernel, devices=devices, start=start, width=width),
        in_specs=[pl.BlockSpec(memory_space=pltpu.SMEM), vmem, vmem, vmem],
        out_shape=rows_of((stop - start) * 3 * begin.shape[0]),
        compiler_params=pltpu.CompilerParams(vmem_limit_bytes=VMEM_LIMIT),
        name="cube_windows",
    )(device, begin, span, cube)


def split_kernel(device_ref, x_ref, y_ref, keep_ref, send_ref):
    half = keep_ref.shape[0]
    total = x_ref[...] + y_ref[...]
    low_kept = (device_ref[0] >> 1) % 2 == 0
    keep_ref[...] = jnp.where(low_kept, total[:half], total[half:])
    send_ref[...] = jnp.where(low_kept, total[half:], total[:half])


def join_kernel(x_ref, y_ref, early_ref, late_ref, keep_ref, send_ref):
    slots, early = x_ref.shape[0], early_ref.shape[0]
    total = x_ref[...] + y_ref[...]
    keep_ref[...] = total
    send_ref[:slots, :] = total
    send_ref[slots : slots + early, :] = early_ref[...]
    send_ref[slots + early :, :] = late_ref[...]


def step_kernel(x_ref, y_ref, sums_ref, keep_ref, send_ref, *, slots):
    half = (y_ref.shape[0] - slots) // 2
    own = sums_ref.shape[0]
    total = x_ref[:slots, :] + y_ref[:slots, :]

    def gathered(first):
        value = y_ref[slots + first : slots + first + half, :]
        if x_ref.shape[0] > slots:
            value = value + x_ref[slots + first : slots + first + half, :]
        return value

    kept, sent = gathered(0), gathered(half) + sums_ref[own - half :, :]
    if own > half:
        kept = kept + sums_ref[:half, :]
    keep_ref[:slots, :] = total
    keep_ref[slots:, :] = kept
    send_ref[:slots, :] = total
    send_ref[slots:, :] = sent


def rows_of(count):
    return jax.ShapeDtypeStruct((count, LANES), F32)


def split_slots(device, x, y):
    vmem = pl.BlockSpec(memory_space=pltpu.VMEM)
    half = rows_of(x.shape[0] // 2)
    return pl.pallas_call(
        split_kernel,
        in_specs=[pl.BlockSpec(memory_space=pltpu.SMEM), vmem, vmem],
        out_shape=(half, half),
        compiler_params=pltpu.CompilerParams(vmem_limit_bytes=VMEM_LIMIT),
        name="split_slots",
    )(device, x, y)


def pick(bins_ref, device, lows, blocks, own, half):
    bins = bins_ref[:, pl.ds(pl.multiple_of(device * own, LANES), own)]
    bins = jnp.broadcast_to(bins, (SUB, own)).T[:, :1]
    total = None
    for low_bin, block in zip(lows, blocks):
        at = lax.broadcasted_iota(jnp.int32, (own, half), 1)
        member = jnp.where(at == bins - low_bin, 1.0, 0.0).astype(BF16)
        hi, mid, low = split3(block[:half, :])
        value = dot(member, hi, NN) + (dot(member, mid, NN) + dot(member, low, NN))
        total = value if total is None else total + value
    return total


def pick_kernel(device_ref, bins_ref, kept_ref, by_x_ref, by_core_ref, near_ref, far_ref, *, half):
    device = device_ref[0]
    own = near_ref.shape[0]
    kept_first = jnp.where((device >> 1) % 2 == 0, 0, half)
    lows = (kept_first, half - kept_first)
    near_ref[...] = pick(bins_ref, device, lows, (kept_ref, by_x_ref), own, half)
    far_ref[...] = pick(bins_ref, device, lows[:1], (by_core_ref,), own, half)


def pick_early(device, bins, kept, by_x, by_core, own, half):
    vmem = pl.BlockSpec(memory_space=pltpu.VMEM)
    return pl.pallas_call(
        functools.partial(pick_kernel, half=half),
        in_specs=[pl.BlockSpec(memory_space=pltpu.SMEM)] + [vmem] * 4,
        out_shape=(rows_of(own), rows_of(own)),
        compiler_params=pltpu.CompilerParams(vmem_limit_bytes=VMEM_LIMIT),
        name="pick_early",
    )(device, bins, kept, by_x, by_core)


def owner_kernel(
    device_ref, bins_ref, owner_ref, begin_ref, span_ref,
    kept_ref, by_x_ref, by_core_ref, by_both_ref, near_ref, far_ref, inverse_ref, hi_ref, mid_ref, low_ref,
    weights_ref, out_ref,
    continuum_ref, mine_ref, mid_held_ref, low_held_ref, owner_held_ref, begins_ref, spans_ref, starts_ref,
    parts_sem, small_sem, *, chunk,
):
    own_slots = weights_ref.shape[0]
    own = begins_ref.shape[1]
    lines = begin_ref.shape[0]
    full_width = hi_ref.shape[1]
    half = owner_held_ref.shape[1] // 2
    inverse = inverse_ref[...]
    device = device_ref[0]
    own_lanes = pl.ds(pl.multiple_of(device * own, LANES), own)

    small_copies = [
        pltpu.make_async_copy(owner_ref, owner_held_ref, small_sem.at[1]),
        pltpu.make_async_copy(begin_ref.at[:, own_lanes], begins_ref, small_sem.at[2]),
        pltpu.make_async_copy(span_ref.at[:, own_lanes], spans_ref, small_sem.at[3]),
        pltpu.make_async_copy(begin_ref.at[:, own_lanes], starts_ref, small_sem.at[4]),
    ]

    def part_copies(i):
        lanes = pl.ds(i * chunk, chunk)
        return [
            pltpu.make_async_copy(mid_ref.at[:, lanes], mid_held_ref.at[:, lanes], parts_sem.at[0, i]),
            pltpu.make_async_copy(low_ref.at[:, lanes], low_held_ref.at[:, lanes], parts_sem.at[1, i]),
        ]

    for copy in small_copies + [copy for i in range(full_width // chunk) for copy in part_copies(i)]:
        copy.start()

    core_low = device % 2 == 0
    low_kept = (device >> 1) % 2 == 0

    def lane_halves(near, far):
        return jnp.where(core_low, near, far), jnp.where(core_low, far, near)

    def by_lanes(near, far):
        return jnp.concatenate(lane_halves(near, far), axis=1)

    for copy in small_copies:
        copy.wait()

    kept_first = jnp.where(low_kept, 0, half)
    for i in range(own_slots):
        picked_bin = owner_held_ref[0, device * own_slots + i]
        in_kept = (picked_bin >= half) == (kept_first > 0)
        row = pl.ds(picked_bin - jnp.where(picked_bin >= half, half, 0), 1)
        low, high = lane_halves(
            jnp.where(in_kept, kept_ref[row, :], by_x_ref[row, :]),
            jnp.where(in_kept, by_core_ref[row, :], by_both_ref[row, :]),
        )
        mine_ref[i : i + 1, :LANES] = low
        mine_ref[i : i + 1, LANES:] = high
    weights_ref[...] = dot_f32(mine_ref[...], inverse, NN)

    far = far_ref[...] + pick(bins_ref, device, (half - kept_first,), (by_both_ref,), own, half)
    spaxel_weights = dot_f32(by_lanes(near_ref[...], far), inverse, NN)

    hi, mid, low = split3(spaxel_weights)
    tiles = chunk // LANES
    for i in range(full_width // chunk):
        first = hi_ref[:, i * chunk : (i + 1) * chunk]
        value = dot(hi, first, NN) + (dot(mid, first, NN) + dot(low, first, NN))
        for t in range(tiles):
            continuum_ref[2 * (i * tiles + t)] = value[:, t * LANES : (t + 1) * LANES]
    left_half = lax.broadcasted_iota(jnp.int32, (own, LANES), 1) < LANES // 2
    before = None
    for i in range(full_width // chunk):
        for copy in part_copies(i):
            copy.wait()
        lanes = slice(i * chunk, (i + 1) * chunk)
        second, third = mid_held_ref[:, lanes], low_held_ref[:, lanes]
        value = dot(hi, second, NN) + (dot(mid, second, NN) + dot(hi, third, NN))
        for t in range(tiles):
            at = 2 * (i * tiles + t)
            tile = continuum_ref[at] + value[:, t * LANES : (t + 1) * LANES]
            continuum_ref[at] = tile
            turned = pltpu.roll(tile, LANES // 2, 1)
            if at:
                continuum_ref[at - 1] = jnp.where(left_half, before, turned)
            before = turned
    continuum_ref[2 * (full_width // LANES) - 1] = jnp.where(left_half, before, 0.0)

    begin = begins_ref[...]
    span = spans_ref[...].astype(F32)
    centre = 2.0 * (begin & (LANES // 2 - 1)).astype(F32) + span - 1.0
    rows_at = lax.broadcasted_iota(jnp.int32, (SUB, LANES), 0)
    at_row = [rows_at == r for r in range(SUB)]
    twice = 2.0 * lax.broadcasted_iota(jnp.int32, (LANES, own), 0).astype(F32)
    sums = [None] * (3 * lines)
    for j in range(lines):
        picks = []
        for g in range(own // SUB):
            rows = slice(g * SUB, (g + 1) * SUB)
            block = None
            for r in range(SUB):
                tile = continuum_ref[lax.shift_right_logical(starts_ref[j, g * SUB + r], 6), rows, :]
                block = tile if block is None else jnp.where(at_row[r], tile, block)
            picks.append(block)
        m = twice - centre[j : j + 1]
        masked = jnp.where(jnp.abs(m) < span[j : j + 1], jnp.concatenate(picks, axis=0).T, 0.0)
        weighted = masked * m
        for k, term in enumerate((masked, weighted, weighted * m)):
            sums[k * lines + j] = jnp.sum(term, axis=0, keepdims=True)
    continuum_sums = jnp.concatenate(sums, axis=0)

    own_rows = slice(half, half + 3 * lines)
    other_rows = slice(half + 3 * lines, half + 6 * lines)
    cube_sums = (kept_ref[own_rows, :] + by_x_ref[own_rows, :]) + (
        by_core_ref[other_rows, :] + by_both_ref[other_rows, :]
    )
    scale = jnp.concatenate([span, span * span, span * span * span], axis=0)
    out_ref[...] = (cube_sums - continuum_sums) / scale


def owned(device, bins, owner, begin, span, messages, inverse, parts, own_slots, own, chunk):
    vmem = pl.BlockSpec(memory_space=pltpu.VMEM)
    hbm = pl.BlockSpec(memory_space=pltpu.HBM)
    count, full_width = parts[0].shape
    lines = begin.shape[0]
    return pl.pallas_call(
        functools.partial(owner_kernel, chunk=chunk),
        in_specs=[pl.BlockSpec(memory_space=pltpu.SMEM)] + [vmem] + [hbm] * 3 + [vmem] * 8 + [hbm] * 2,
        out_shape=(
            jax.ShapeDtypeStruct((own_slots, count), F32),
            jax.ShapeDtypeStruct((3 * lines, own), F32),
        ),
        scratch_shapes=[
            pltpu.VMEM((2 * (full_width // LANES), own, LANES), F32),
            pltpu.VMEM((own_slots, count), F32),
            pltpu.VMEM((count, full_width), BF16),
            pltpu.VMEM((count, full_width), BF16),
            pltpu.SMEM(owner.shape, jnp.int32),
            pltpu.VMEM((lines, own), jnp.int32),
            pltpu.VMEM((lines, own), jnp.int32),
            pltpu.SMEM((lines, own), jnp.int32),
            pltpu.SemaphoreType.DMA((2, full_width // chunk)),
            pltpu.SemaphoreType.DMA((5,)),
        ],
        compiler_params=pltpu.CompilerParams(vmem_limit_bytes=VMEM_LIMIT),
        name="owned",
    )(device, bins, owner, begin, span, *messages, inverse, *parts)


def shards(cube, templates, bin_id, owner_bins, line_start, line_width):
    devices = lax.axis_size("spax")
    device = lax.axis_index("spax")
    spaxels = cube.shape[0]
    total_bins = owner_bins.shape[0]
    count = templates.shape[0]
    lines = line_start.shape[0]
    own_spaxels = spaxels // devices
    own_slots = total_bins // devices
    here = device.reshape(1).astype(jnp.int32)
    pin = lambda x: pltpu.with_memory_space_constraint(x, pltpu.HBM)
    columns = pin(cube.T)
    begin, span = pin(line_start), pin(line_width)
    bins, owner = pin(bin_id[None, :]), pin(owner_bins[None, :])
    after = lax.optimization_barrier

    def swap(x, bit):
        return lax.ppermute(x, "spax", [(d, d ^ (1 << bit)) for d in range(devices)])

    keep, send, begins, spans, held, bins_held = project(here, bins, begin, span, columns, pin(templates), total_bins)
    windows = lambda start, stop, now: cube_windows(
        now, begins, spans, held, devices, start, stop, cube.shape[1]
    )
    arrived = swap(send, 0)
    left = devices // 2
    cut = left + devices * 3 // 16
    early = windows(left, cut, here)
    keep, arrived, early = after((keep, arrived, early))
    keep, send = split_slots(here, keep, arrived)
    keep, send, now = after((keep, send, here))
    arrived = swap(send, 1)
    late, next_sums = windows(cut, devices, now), windows(left // 2, left, now)
    keep, arrived, early, late, next_sums, templates = after((keep, arrived, early, late, next_sums, templates))
    slots = total_bins // 2
    message = rows_of(slots + left * 3 * lines)
    keep, send = in_vmem(join_kernel, (rows_of(slots), message), "join", keep, arrived, early, late)

    keep, send, now, templates = after((keep, send, here, templates))
    gram = first = None
    for bit in range(2, devices.bit_length() - 1):
        arrived = swap(send, bit)
        left //= 2
        last_step = bit == devices.bit_length() - 2
        sums = next_sums if gram is None else windows(0 if last_step else left, 2 * left, now)
        if gram is None:
            gram, scale, *parts = scaled_gram(pin(templates), 512)
            arrived, sums, gram = after((arrived, sums, gram))
        elif first is None:
            first = in_vmem(first_kernel, [rows_of(LANES)] * 3, "first", gram)
            arrived, sums, first = after((arrived, sums, first))
        message = rows_of(slots + left * 3 * lines)
        keep, send = in_vmem(
            functools.partial(step_kernel, slots=slots), (message, message), "step", keep, arrived, sums
        )
        if first is None:
            keep, send, now, gram = after((keep, send, here, gram))
        else:
            keep, send, now, first = after((keep, send, here, first))

    by_x = swap(send, 1)
    by_core = swap(keep, 0)
    inverse = in_vmem(finish_kernel, jax.ShapeDtypeStruct((count, count), F32), "finish", *first, scale)
    by_x, by_core, inverse = after((by_x, by_core, inverse))
    by_both = swap(by_x, 0)
    near, far = pick_early(here, bins_held, keep, by_x, by_core, own_spaxels, slots)
    by_both, near, far = after((by_both, near, far))
    messages = (keep, by_x, by_core, by_both, near, far)
    parts = [parts[0], pin(parts[1]), pin(parts[2])]
    return owned(here, bins_held, owner, begin, span, messages, inverse, parts, own_slots, own_spaxels, 512)


def solution(mesh):
    placed = (
        P("strips", "spax"),
        P(),
        P("strips"),
        P("strips"),
        P(None, "strips"),
        P(None, "strips"),
    )
    return jax.shard_map(
        shards,
        mesh=mesh,
        in_specs=placed,
        out_specs=(P(("strips", "spax"), None), P(None, ("strips", "spax"))),
        check_vma=False,
    )
```

```python
import functools

import jax
import jax.numpy as jnp
from jax import lax
from jax.experimental import pallas as pl
from jax.experimental.pallas import tpu as pltpu
from jax.sharding import PartitionSpec as P

HIGHEST = lax.Precision.HIGHEST
F32 = jnp.float32
BF16 = jnp.bfloat16
LANES = 128
SUB = 8
VMEM_LIMIT = 20 * 1024 * 1024

NT = (((1,), (1,)), ((), ()))
NN = (((1,), (0,)), ((), ()))


def split3(x):
    hi = x.astype(BF16)
    rest = x - hi.astype(F32)
    mid = rest.astype(BF16)
    low = (rest - mid.astype(F32)).astype(BF16)
    return hi, mid, low


def dot(a, b, dims):
    return lax.dot_general(a, b, dims, preferred_element_type=F32)


def dot_f32(a, b, dims):
    return lax.dot_general(a, b, dims, precision=HIGHEST, preferred_element_type=F32)


def template_window(width, full_width):
    return min(full_width, -(-(width + LANES - 1) // LANES) * LANES)


def project_kernel(
    device_ref, bins_ref, begin_ref, span_ref, cube_ref, templates_ref,
    keep_ref, send_ref, begins_ref, spans_ref, held_ref,
    bins_held_ref, sums_ref, parts_ref, window_ref, firsts_ref, cube_sem, small_sem, *, chunk,
):
    width, spaxels = cube_ref.shape
    total_bins = keep_ref.shape[0]
    full_width = templates_ref.shape[1]
    first = device_ref[0] * width
    window = window_ref.shape[1]
    base = pl.multiple_of(jnp.minimum(first // LANES * LANES, full_width - window), LANES)
    chunks = spaxels // chunk
    reach = chunk + SUB
    pieces = cube_sem.shape[0]

    def cube_copy(i):
        lanes = pl.ds(i * (spaxels // pieces), spaxels // pieces)
        return pltpu.make_async_copy(cube_ref.at[:, lanes], held_ref.at[pl.ds(0, width), lanes], cube_sem.at[i])

    bins_copy = pltpu.make_async_copy(bins_ref, bins_held_ref, small_sem.at[0])
    firsts_copy = pltpu.make_async_copy(bins_ref, firsts_ref, small_sem.at[1])
    window_copy = pltpu.make_async_copy(templates_ref.at[:, pl.ds(base, window)], window_ref, small_sem.at[2])
    line_copies = [
        pltpu.make_async_copy(begin_ref, begins_ref, small_sem.at[3]),
        pltpu.make_async_copy(span_ref, spans_ref, small_sem.at[4]),
    ]
    for copy in [bins_copy, firsts_copy] + [cube_copy(i) for i in range(pieces)] + [window_copy] + line_copies:
        copy.start()
    sums_ref[...] = jnp.zeros(sums_ref.shape, F32)
    joined = held_ref.shape[0] > width
    counted = sums_ref.shape[1] - COUNT_ROWS
    if joined:
        held_ref[width:, :] = jnp.ones((COUNT_ROWS, spaxels), F32)
    rows_at = lax.broadcasted_iota(jnp.int32, (reach, chunk), 0)
    bins_copy.wait()
    firsts_copy.wait()

    def low_bin(i):
        return pl.multiple_of(firsts_ref[0, i * chunk] // SUB * SUB, SUB)

    for i in range(chunks):
        if i % (chunks // pieces) == 0:
            cube_copy(i // (chunks // pieces)).wait()
        lanes = slice(i * chunk, (i + 1) * chunk)
        member = jnp.where(rows_at == bins_held_ref[:, lanes] - low_bin(i), 1.0, 0.0).astype(BF16)
        hi, mid, low = split3(held_ref[:, lanes])
        new = dot(member, hi, NT) + (dot(member, mid, NT) + dot(member, low, NT))
        if joined:
            parts_ref[i] = new
        else:
            parts_ref[i] = jnp.zeros(parts_ref.shape[1:], F32)
            parts_ref[i, :, :width] = new
            parts_ref[i, :, counted:] = dot(member, jnp.ones((COUNT_ROWS, chunk), BF16), NT)
    for i in range(chunks):
        sums_ref[pl.ds(low_bin(i), reach), :] += parts_ref[i]
    window_copy.wait()
    mine = pltpu.roll(window_ref[...], window - (first - base), 1)[:, :width]
    low_kept = device_ref[0] % 2 == 0
    block = min(total_bins, 512)
    for at in range(0, total_bins, block):
        rows = slice(at, at + block)
        means = sums_ref[rows, :width] / sums_ref[rows, counted : counted + 1]
        projections = dot_f32(means, mine, NT) * (1.0 / full_width)
        low, high = projections[:, :LANES], projections[:, LANES:]
        keep_ref[rows, :] = jnp.where(low_kept, low, high)
        send_ref[rows, :] = jnp.where(low_kept, high, low)
    for copy in line_copies:
        copy.wait()


COUNT_ROWS = 16


def project(device, bins, begin, span, cube, templates, total_bins):
    width, spaxels = cube.shape
    chunk = min(spaxels, 256)
    wide = -(-width // COUNT_ROWS) * COUNT_ROWS + COUNT_ROWS
    held = width if width % COUNT_ROWS else wide
    count, full_width = templates.shape
    return pl.pallas_call(
        functools.partial(project_kernel, chunk=chunk),
        in_specs=[pl.BlockSpec(memory_space=pltpu.SMEM)] + [pl.BlockSpec(memory_space=pltpu.HBM)] * 5,
        out_specs=[pl.BlockSpec(memory_space=pltpu.VMEM)] * 6,
        out_shape=[
            rows_of(total_bins),
            rows_of(total_bins),
            pltpu.VMEM(begin.shape, jnp.int32),
            pltpu.VMEM(span.shape, jnp.int32),
            pltpu.VMEM((held, spaxels), F32),
            pltpu.VMEM(bins.shape, jnp.int32),
        ],
        scratch_shapes=[
            pltpu.VMEM((total_bins + chunk + SUB, wide), F32),
            pltpu.VMEM((spaxels // chunk, chunk + SUB, wide), F32),
            pltpu.VMEM((count, template_window(width, full_width)), F32),
            pltpu.SMEM(bins.shape, jnp.int32),
            pltpu.SemaphoreType.DMA((min(spaxels // chunk, 2),)),
            pltpu.SemaphoreType.DMA((5,)),
        ],
        compiler_params=pltpu.CompilerParams(vmem_limit_bytes=VMEM_LIMIT),
        name="project",
    )(device, bins, begin, span, cube, templates)


def reciprocal(x):
    r = pl.reciprocal(x, approx=True)
    r = r * (2.0 - x * r)
    return r * (2.0 - x * r)


def eliminate(tile, start, stop):
    size = tile.shape[0]
    count = size // SUB
    lanes = lax.broadcasted_iota(jnp.int32, (SUB, size), 1)
    rows_at = lax.broadcasted_iota(jnp.int32, (SUB, size), 0)
    rows = [tile[i * SUB : (i + 1) * SUB, :] for i in range(count)]
    for k in range(start, stop):
        block = rows[k]
        first = k * SUB
        a = {}
        for i in range(SUB):
            for j in range(i, SUB):
                a[i, j] = jnp.broadcast_to(block[i : i + 1, first + j : first + j + 1], (SUB, size))

        def at(i, j):
            return (i, j) if i <= j else (j, i)

        for p in range(0, SUB, 2):
            q = p + 1
            pp, pq, qq = a[p, p], a[p, q], a[q, q]
            inverse = reciprocal(pp * qq - pq * pq)
            others = [i for i in range(SUB) if i not in (p, q)]
            old = {i: (a[at(i, p)], a[at(i, q)]) for i in others}
            new = {
                i: ((u * qq - v * pq) * inverse, (v * pp - u * pq) * inverse) for i, (u, v) in old.items()
            }
            for i in others:
                for j in others:
                    if i <= j:
                        a[i, j] = a[i, j] - new[i][0] * old[j][0] - new[i][1] * old[j][1]
            for i in others:
                a[at(i, p)], a[at(i, q)] = new[i]
            a[p, p], a[p, q], a[q, q] = -(qq * inverse), pq * inverse, -(pp * inverse)
        columns = []
        for j in range(SUB):
            column = a[at(0, j)]
            for i in range(1, SUB):
                column = jnp.where(rows_at == i, a[at(i, j)], column)
            columns.append(column)
        terms = [columns[j] * jnp.broadcast_to(block[j : j + 1, :], (SUB, size)) for j in range(SUB)]
        while len(terms) > 1:
            terms = [x + y for x, y in zip(terms[::2], terms[1::2])]
        swept = -terms[0]
        for j in range(SUB):
            swept = jnp.where(lanes == first + j, columns[j], swept)
        inside = (lanes >= first) & (lanes < first + SUB)
        spread_rows = [jnp.broadcast_to(swept[j : j + 1, :], (SUB, size)) for j in range(SUB)]
        order = list(range(k + 1, count)) + list(range(k))
        for i in order:
            terms = [
                jnp.broadcast_to(rows[i][:, first + j : first + j + 1], (SUB, size)) * spread_rows[j]
                for j in range(SUB)
            ]
            while len(terms) > 1:
                terms = [x + y for x, y in zip(terms[::2], terms[1::2])]
            rows[i] = jnp.where(inside, 0.0, rows[i]) - terms[0]
        rows[k] = swept
    return jnp.concatenate(rows, axis=0)


def gram_kernel(
    templates_ref, gram_ref, scale_ref, hi_ref, mid_ref, low_ref, held_ref, mid_held_ref, low_held_ref, sem, out_sem,
    *, chunk,
):
    count, full_width = templates_ref.shape

    def copy(i):
        lanes = pl.ds(i * chunk, chunk)
        return pltpu.make_async_copy(templates_ref.at[:, lanes], held_ref.at[:, lanes], sem.at[i])

    def out_copies(i):
        lanes = pl.ds(i * chunk, chunk)
        return [
            pltpu.make_async_copy(mid_held_ref.at[:, lanes], mid_ref.at[:, lanes], out_sem.at[0, i]),
            pltpu.make_async_copy(low_held_ref.at[:, lanes], low_ref.at[:, lanes], out_sem.at[1, i]),
        ]

    for i in range(full_width // chunk):
        copy(i).start()
    even = jnp.zeros((count, count), F32)
    mixed = jnp.zeros((count, count), F32)
    for i in range(full_width // chunk):
        copy(i).wait()
        lanes = slice(i * chunk, (i + 1) * chunk)
        hi, mid, low = split3(held_ref[:, lanes])
        hi_ref[:, lanes], mid_held_ref[:, lanes], low_held_ref[:, lanes] = hi, mid, low
        for out in out_copies(i):
            out.start()
        even = even + (dot(hi, hi, NT) + dot(mid, mid, NT))
        mixed = mixed + (dot(hi, mid, NT) + dot(hi, low, NT))
    gram = (even + (mixed + mixed.T)) * (1.0 / full_width)
    same = lax.broadcasted_iota(jnp.int32, gram.shape, 0) == lax.broadcasted_iota(jnp.int32, gram.shape, 1)
    diagonal = jnp.where(same, gram, 0.0)
    row = lax.rsqrt(jnp.sum(diagonal, axis=0, keepdims=True))
    column = lax.rsqrt(jnp.sum(diagonal, axis=1, keepdims=True))
    gram = gram * row * column
    scale_ref[...] = row
    gram_ref[...] = gram
    for i in range(full_width // chunk):
        for out in out_copies(i):
            out.wait()


def scaled_gram(templates, chunk):
    count, full_width = templates.shape
    vmem, hbm = (pl.BlockSpec(memory_space=space) for space in (pltpu.VMEM, pltpu.HBM))
    return pl.pallas_call(
        functools.partial(gram_kernel, chunk=chunk),
        in_specs=[hbm],
        out_specs=(vmem, vmem, vmem, hbm, hbm),
        out_shape=(
            jax.ShapeDtypeStruct((count, count), F32),
            jax.ShapeDtypeStruct((1, count), F32),
            pltpu.VMEM((count, full_width), BF16),
            pltpu.HBM((count, full_width), BF16),
            pltpu.HBM((count, full_width), BF16),
        ),
        scratch_shapes=[
            pltpu.VMEM((count, full_width), F32),
            pltpu.VMEM((count, full_width), BF16),
            pltpu.VMEM((count, full_width), BF16),
            pltpu.SemaphoreType.DMA((full_width // chunk,)),
            pltpu.SemaphoreType.DMA((2, full_width // chunk)),
        ],
        compiler_params=pltpu.CompilerParams(vmem_limit_bytes=VMEM_LIMIT),
        name="gram",
    )(templates)


STEPS = LANES // SUB
EARLY = 4


def first_kernel(gram_ref, first_ref, half_ref, second_ref):
    first = -eliminate(gram_ref[:LANES, :LANES], 0, STEPS)
    side = gram_ref[:LANES, LANES:]
    half = dot_f32(first, side, NN)
    first_ref[...] = first
    half_ref[...] = half
    second_ref[...] = eliminate(gram_ref[LANES:, LANES:] - dot_f32(side.T, half, NN), 0, EARLY)


def finish_kernel(first_ref, half_ref, second_ref, scale_ref, out_ref):
    first, half = first_ref[...], half_ref[...]
    last = -eliminate(second_ref[...], EARLY, STEPS)
    cross = dot_f32(half, last, NN)
    row = scale_ref[...]
    column = jnp.broadcast_to(row, (SUB, row.shape[1])).T[:, :1]
    near, far = row[:, :LANES], row[:, LANES:]
    out_ref[:LANES, :LANES] = (first + dot_f32(cross, half, NT)) * near * column[:LANES]
    out_ref[:LANES, LANES:] = -cross * far * column[:LANES]
    out_ref[LANES:, :LANES] = -cross.T * near * column[LANES:]
    out_ref[LANES:, LANES:] = last * far * column[LANES:]


def in_vmem(kernel, shapes, name, *arrays):
    return pl.pallas_call(
        kernel,
        out_shape=shapes,
        compiler_params=pltpu.CompilerParams(vmem_limit_bytes=VMEM_LIMIT),
        name=name,
    )(*arrays)


def window_sums(read, rows, first, begin, span):
    lines = begin.shape[0]
    sub = lax.broadcasted_iota(jnp.int32, (SUB, LANES), 0)
    spans = [jnp.broadcast_to(span[j : j + 1], (SUB, LANES)).astype(F32) for j in range(lines)]
    offsets = [
        (2 * (first + sub - jnp.broadcast_to(begin[j : j + 1], (SUB, LANES))) + 1).astype(F32) - spans[j]
        for j in range(lines)
    ]

    def add(block, shift, sums):
        size = block.shape[0]
        out = []
        for j in range(lines):
            m = offsets[j][:size] + shift
            masked = jnp.where(jnp.abs(m) < spans[j][:size], block, 0.0)
            weighted = masked * m
            out += [sums[3 * j] + masked, sums[3 * j + 1] + weighted, sums[3 * j + 2] + weighted * m]
        return out

    full = rows // SUB
    out = [jnp.zeros((1, LANES), F32)] * (3 * lines)
    if full:
        sums = [jnp.zeros((SUB, LANES), F32)] * (3 * lines)
        for i in range(full):
            sums = add(read(i * SUB, SUB), 2.0 * i * SUB, sums)
        out = [jnp.sum(x, axis=0, keepdims=True) for x in sums]
    if rows % SUB:
        sums = [jnp.zeros((rows % SUB, LANES), F32)] * (3 * lines)
        sums = add(read(full * SUB, rows % SUB), 2.0 * full * SUB, sums)
        out = [x + jnp.sum(y, axis=0, keepdims=True) for x, y in zip(out, sums)]
    return [out[3 * j + k] for k in range(3) for j in range(lines)]


def halving_order(devices):
    bits = devices.bit_length() - 1
    return list(range(2, bits)) + [1, 0]


def flips(position, devices):
    order = halving_order(devices)
    return sum(((position >> (len(order) - 1 - t)) & 1) << bit for t, bit in enumerate(order))


def cube_kernel(device_ref, begin_ref, span_ref, cube_ref, out_ref, *, devices, start, width):
    device = device_ref[0]
    rows = 3 * begin_ref.shape[0]

    def owner(i, carry):
        lanes = pl.ds(pl.multiple_of((device ^ flips(start + i, devices)) * LANES, LANES), LANES)
        sums = window_sums(
            lambda row, size: cube_ref[row : row + size, lanes],
            width,
            device * width,
            begin_ref[:, lanes],
            span_ref[:, lanes],
        )
        out_ref[pl.ds(pl.multiple_of(i * rows, SUB), rows), :] = jnp.concatenate(sums, axis=0)
        return carry

    lax.fori_loop(0, out_ref.shape[0] // rows, owner, 0)


def cube_windows(device, begin, span, cube, devices, start, stop, width):
    vmem = pl.BlockSpec(memory_space=pltpu.VMEM)
    return pl.pallas_call(
        functools.partial(cube_kernel, devices=devices, start=start, width=width),
        in_specs=[pl.BlockSpec(memory_space=pltpu.SMEM), vmem, vmem, vmem],
        out_shape=rows_of((stop - start) * 3 * begin.shape[0]),
        compiler_params=pltpu.CompilerParams(vmem_limit_bytes=VMEM_LIMIT),
        name="cube_windows",
    )(device, begin, span, cube)


def split_kernel(device_ref, x_ref, y_ref, keep_ref, send_ref):
    half = keep_ref.shape[0]
    total = x_ref[...] + y_ref[...]
    low_kept = (device_ref[0] >> 1) % 2 == 0
    keep_ref[...] = jnp.where(low_kept, total[:half], total[half:])
    send_ref[...] = jnp.where(low_kept, total[half:], total[:half])


def join_kernel(x_ref, y_ref, early_ref, late_ref, keep_ref, send_ref):
    slots, early = x_ref.shape[0], early_ref.shape[0]
    total = x_ref[...] + y_ref[...]
    keep_ref[...] = total
    send_ref[:slots, :] = total
    send_ref[slots : slots + early, :] = early_ref[...]
    send_ref[slots + early :, :] = late_ref[...]


def step_kernel(x_ref, y_ref, sums_ref, keep_ref, send_ref, *, slots):
    half = (y_ref.shape[0] - slots) // 2
    own = sums_ref.shape[0]
    total = x_ref[:slots, :] + y_ref[:slots, :]

    def gathered(first):
        value = y_ref[slots + first : slots + first + half, :]
        if x_ref.shape[0] > slots:
            value = value + x_ref[slots + first : slots + first + half, :]
        return value

    kept, sent = gathered(0), gathered(half) + sums_ref[own - half :, :]
    if own > half:
        kept = kept + sums_ref[:half, :]
    keep_ref[:slots, :] = total
    keep_ref[slots:, :] = kept
    send_ref[:slots, :] = total
    send_ref[slots:, :] = sent


def rows_of(count):
    return jax.ShapeDtypeStruct((count, LANES), F32)


def split_slots(device, x, y):
    vmem = pl.BlockSpec(memory_space=pltpu.VMEM)
    half = rows_of(x.shape[0] // 2)
    return pl.pallas_call(
        split_kernel,
        in_specs=[pl.BlockSpec(memory_space=pltpu.SMEM), vmem, vmem],
        out_shape=(half, half),
        compiler_params=pltpu.CompilerParams(vmem_limit_bytes=VMEM_LIMIT),
        name="split_slots",
    )(device, x, y)


def pick(bins_ref, device, lows, blocks, own, half):
    bins = bins_ref[:, pl.ds(pl.multiple_of(device * own, LANES), own)]
    bins = jnp.broadcast_to(bins, (SUB, own)).T[:, :1]
    total = None
    for low_bin, block in zip(lows, blocks):
        at = lax.broadcasted_iota(jnp.int32, (own, half), 1)
        member = jnp.where(at == bins - low_bin, 1.0, 0.0).astype(BF16)
        hi, mid, low = split3(block[:half, :])
        value = dot(member, hi, NN) + (dot(member, mid, NN) + dot(member, low, NN))
        total = value if total is None else total + value
    return total


def pick_kernel(device_ref, bins_ref, kept_ref, by_x_ref, by_core_ref, near_ref, far_ref, *, half):
    device = device_ref[0]
    own = near_ref.shape[0]
    kept_first = jnp.where((device >> 1) % 2 == 0, 0, half)
    lows = (kept_first, half - kept_first)
    near_ref[...] = pick(bins_ref, device, lows, (kept_ref, by_x_ref), own, half)
    far_ref[...] = pick(bins_ref, device, lows[:1], (by_core_ref,), own, half)


def pick_early(device, bins, kept, by_x, by_core, own, half):
    vmem = pl.BlockSpec(memory_space=pltpu.VMEM)
    return pl.pallas_call(
        functools.partial(pick_kernel, half=half),
        in_specs=[pl.BlockSpec(memory_space=pltpu.SMEM)] + [vmem] * 4,
        out_shape=(rows_of(own), rows_of(own)),
        compiler_params=pltpu.CompilerParams(vmem_limit_bytes=VMEM_LIMIT),
        name="pick_early",
    )(device, bins, kept, by_x, by_core)


def owner_kernel(
    device_ref, bins_ref, owner_ref, begin_ref, span_ref,
    kept_ref, by_x_ref, by_core_ref, by_both_ref, near_ref, far_ref, inverse_ref, hi_ref, mid_ref, low_ref,
    weights_ref, out_ref,
    continuum_ref, mine_ref, mid_held_ref, low_held_ref, owner_held_ref, begins_ref, spans_ref, starts_ref,
    parts_sem, small_sem, *, chunk,
):
    own_slots = weights_ref.shape[0]
    own = begins_ref.shape[1]
    lines = begin_ref.shape[0]
    full_width = hi_ref.shape[1]
    half = owner_held_ref.shape[1] // 2
    inverse = inverse_ref[...]
    device = device_ref[0]
    own_lanes = pl.ds(pl.multiple_of(device * own, LANES), own)

    small_copies = [
        pltpu.make_async_copy(owner_ref, owner_held_ref, small_sem.at[1]),
        pltpu.make_async_copy(begin_ref.at[:, own_lanes], begins_ref, small_sem.at[2]),
        pltpu.make_async_copy(span_ref.at[:, own_lanes], spans_ref, small_sem.at[3]),
        pltpu.make_async_copy(begin_ref.at[:, own_lanes], starts_ref, small_sem.at[4]),
    ]
    part_copies = [
        pltpu.make_async_copy(mid_ref, mid_held_ref, parts_sem.at[0]),
        pltpu.make_async_copy(low_ref, low_held_ref, parts_sem.at[1]),
    ]
    for copy in small_copies + part_copies:
        copy.start()

    core_low = device % 2 == 0
    low_kept = (device >> 1) % 2 == 0

    def lane_halves(near, far):
        return jnp.where(core_low, near, far), jnp.where(core_low, far, near)

    def by_lanes(near, far):
        return jnp.concatenate(lane_halves(near, far), axis=1)

    kept_first = jnp.where(low_kept, 0, half)
    far = far_ref[...] + pick(bins_ref, device, (half - kept_first,), (by_both_ref,), own, half)
    spaxel_weights = dot_f32(by_lanes(near_ref[...], far), inverse, NN)

    hi, mid, low = split3(spaxel_weights)
    tiles = chunk // LANES
    for i in range(full_width // chunk):
        first = hi_ref[:, i * chunk : (i + 1) * chunk]
        value = dot(hi, first, NN) + (dot(mid, first, NN) + dot(low, first, NN))
        for t in range(tiles):
            continuum_ref[2 * (i * tiles + t)] = value[:, t * LANES : (t + 1) * LANES]
    for copy in small_copies + part_copies:
        copy.wait()

    for i in range(own_slots):
        picked_bin = owner_held_ref[0, device * own_slots + i]
        in_kept = (picked_bin >= half) == (kept_first > 0)
        row = pl.ds(picked_bin - jnp.where(picked_bin >= half, half, 0), 1)
        low, high = lane_halves(
            jnp.where(in_kept, kept_ref[row, :], by_x_ref[row, :]),
            jnp.where(in_kept, by_core_ref[row, :], by_both_ref[row, :]),
        )
        mine_ref[i : i + 1, :LANES] = low
        mine_ref[i : i + 1, LANES:] = high
    weights_ref[...] = dot_f32(mine_ref[...], inverse, NN)

    left_half = lax.broadcasted_iota(jnp.int32, (own, LANES), 1) < LANES // 2
    before = None
    for i in range(full_width // chunk):
        lanes = slice(i * chunk, (i + 1) * chunk)
        second, third = mid_held_ref[:, lanes], low_held_ref[:, lanes]
        value = dot(hi, second, NN) + (dot(mid, second, NN) + dot(hi, third, NN))
        for t in range(tiles):
            at = 2 * (i * tiles + t)
            tile = continuum_ref[at] + value[:, t * LANES : (t + 1) * LANES]
            continuum_ref[at] = tile
            turned = pltpu.roll(tile, LANES // 2, 1)
            if at:
                continuum_ref[at - 1] = jnp.where(left_half, before, turned)
            before = turned
    continuum_ref[2 * (full_width // LANES) - 1] = jnp.where(left_half, before, 0.0)

    begin = begins_ref[...]
    span = spans_ref[...].astype(F32)
    centre = 2.0 * (begin & (LANES // 2 - 1)).astype(F32) + span - 1.0
    rows_at = lax.broadcasted_iota(jnp.int32, (SUB, LANES), 0)
    at_row = [rows_at == r for r in range(SUB)]
    twice = 2.0 * lax.broadcasted_iota(jnp.int32, (LANES, own), 0).astype(F32)
    sums = [None] * (3 * lines)
    for j in range(lines):
        picks = []
        for g in range(own // SUB):
            rows = slice(g * SUB, (g + 1) * SUB)
            block = None
            for r in range(SUB):
                tile = continuum_ref[lax.shift_right_logical(starts_ref[j, g * SUB + r], 6), rows, :]
                block = tile if block is None else jnp.where(at_row[r], tile, block)
            picks.append(block)
        m = twice - centre[j : j + 1]
        masked = jnp.where(jnp.abs(m) < span[j : j + 1], jnp.concatenate(picks, axis=0).T, 0.0)
        weighted = masked * m
        for k, term in enumerate((masked, weighted, weighted * m)):
            sums[k * lines + j] = jnp.sum(term, axis=0, keepdims=True)
    continuum_sums = jnp.concatenate(sums, axis=0)

    own_rows = slice(half, half + 3 * lines)
    other_rows = slice(half + 3 * lines, half + 6 * lines)
    cube_sums = (kept_ref[own_rows, :] + by_x_ref[own_rows, :]) + (
        by_core_ref[other_rows, :] + by_both_ref[other_rows, :]
    )
    scale = jnp.concatenate([span, span * span, span * span * span], axis=0)
    out_ref[...] = (cube_sums - continuum_sums) / scale


def owned(device, bins, owner, begin, span, messages, inverse, parts, own_slots, own, chunk):
    vmem = pl.BlockSpec(memory_space=pltpu.VMEM)
    hbm = pl.BlockSpec(memory_space=pltpu.HBM)
    count, full_width = parts[0].shape
    lines = begin.shape[0]
    return pl.pallas_call(
        functools.partial(owner_kernel, chunk=chunk),
        in_specs=[pl.BlockSpec(memory_space=pltpu.SMEM)] + [vmem] + [hbm] * 3 + [vmem] * 8 + [hbm] * 2,
        out_shape=(
            jax.ShapeDtypeStruct((own_slots, count), F32),
            jax.ShapeDtypeStruct((3 * lines, own), F32),
        ),
        scratch_shapes=[
            pltpu.VMEM((2 * (full_width // LANES), own, LANES), F32),
            pltpu.VMEM((own_slots, count), F32),
            pltpu.VMEM((count, full_width), BF16),
            pltpu.VMEM((count, full_width), BF16),
            pltpu.SMEM(owner.shape, jnp.int32),
            pltpu.VMEM((lines, own), jnp.int32),
            pltpu.VMEM((lines, own), jnp.int32),
            pltpu.SMEM((lines, own), jnp.int32),
            pltpu.SemaphoreType.DMA((2,)),
            pltpu.SemaphoreType.DMA((5,)),
        ],
        compiler_params=pltpu.CompilerParams(vmem_limit_bytes=VMEM_LIMIT),
        name="owned",
    )(device, bins, owner, begin, span, *messages, inverse, *parts)


def shards(cube, templates, bin_id, owner_bins, line_start, line_width):
    devices = lax.axis_size("spax")
    device = lax.axis_index("spax")
    spaxels = cube.shape[0]
    total_bins = owner_bins.shape[0]
    count = templates.shape[0]
    lines = line_start.shape[0]
    own_spaxels = spaxels // devices
    own_slots = total_bins // devices
    here = device.reshape(1).astype(jnp.int32)
    pin = lambda x: pltpu.with_memory_space_constraint(x, pltpu.HBM)
    columns = pin(cube.T)
    begin, span = pin(line_start), pin(line_width)
    bins, owner = pin(bin_id[None, :]), pin(owner_bins[None, :])
    after = lax.optimization_barrier

    def swap(x, bit):
        return lax.ppermute(x, "spax", [(d, d ^ (1 << bit)) for d in range(devices)])

    keep, send, begins, spans, held, bins_held = project(here, bins, begin, span, columns, pin(templates), total_bins)
    windows = lambda start, stop, now: cube_windows(
        now, begins, spans, held, devices, start, stop, cube.shape[1]
    )
    arrived = swap(send, 0)
    left = devices // 2
    cut = left + devices * 3 // 16
    early = windows(left, cut, here)
    keep, arrived, early = after((keep, arrived, early))
    keep, send = split_slots(here, keep, arrived)
    keep, send, now = after((keep, send, here))
    arrived = swap(send, 1)
    late, next_sums = windows(cut, devices, now), windows(left // 2, left, now)
    keep, arrived, early, late, next_sums, templates = after((keep, arrived, early, late, next_sums, templates))
    slots = total_bins // 2
    message = rows_of(slots + left * 3 * lines)
    keep, send = in_vmem(join_kernel, (rows_of(slots), message), "join", keep, arrived, early, late)

    keep, send, now, templates = after((keep, send, here, templates))
    gram = first = None
    for bit in range(2, devices.bit_length() - 1):
        arrived = swap(send, bit)
        left //= 2
        last_step = bit == devices.bit_length() - 2
        sums = next_sums if gram is None else windows(0 if last_step else left, 2 * left, now)
        if gram is None:
            gram, scale, *parts = scaled_gram(pin(templates), 512)
            arrived, sums, gram = after((arrived, sums, gram))
        elif first is None:
            first = in_vmem(first_kernel, [rows_of(LANES)] * 3, "first", gram)
            arrived, sums, first = after((arrived, sums, first))
        message = rows_of(slots + left * 3 * lines)
        keep, send = in_vmem(
            functools.partial(step_kernel, slots=slots), (message, message), "step", keep, arrived, sums
        )
        if first is None:
            keep, send, now, gram = after((keep, send, here, gram))
        else:
            keep, send, now, first = after((keep, send, here, first))

    by_x = swap(send, 1)
    by_core = swap(keep, 0)
    inverse = in_vmem(finish_kernel, jax.ShapeDtypeStruct((count, count), F32), "finish", *first, scale)
    by_x, by_core, inverse = after((by_x, by_core, inverse))
    by_both = swap(by_x, 0)
    near, far = pick_early(here, bins_held, keep, by_x, by_core, own_spaxels, slots)
    by_both, near, far = after((by_both, near, far))
    messages = (keep, by_x, by_core, by_both, near, far)
    parts = [parts[0], pin(parts[1]), pin(parts[2])]
    return owned(here, bins_held, owner, begin, span, messages, inverse, parts, own_slots, own_spaxels, 512)


def solution(mesh):
    placed = (
        P("strips", "spax"),
        P(),
        P("strips"),
        P("strips"),
        P(None, "strips"),
        P(None, "strips"),
    )
    return jax.shard_map(
        shards,
        mesh=mesh,
        in_specs=placed,
        out_specs=(P(("strips", "spax"), None), P(None, ("strips", "spax"))),
        check_vma=False,
    )
```

```python
import functools

import jax
import jax.numpy as jnp
from jax import lax
from jax.experimental import pallas as pl
from jax.experimental.pallas import tpu as pltpu
from jax.sharding import PartitionSpec as P

HIGHEST = lax.Precision.HIGHEST
F32 = jnp.float32
BF16 = jnp.bfloat16
LANES = 128
SUB = 8
VMEM_LIMIT = 20 * 1024 * 1024

NT = (((1,), (1,)), ((), ()))
NN = (((1,), (0,)), ((), ()))


def split3(x):
    hi = x.astype(BF16)
    rest = x - hi.astype(F32)
    mid = rest.astype(BF16)
    low = (rest - mid.astype(F32)).astype(BF16)
    return hi, mid, low


def dot(a, b, dims):
    return lax.dot_general(a, b, dims, preferred_element_type=F32)


def dot_f32(a, b, dims):
    return lax.dot_general(a, b, dims, precision=HIGHEST, preferred_element_type=F32)


def template_window(width, full_width):
    return min(full_width, -(-(width + LANES - 1) // LANES) * LANES)


def project_kernel(
    device_ref, bins_ref, begin_ref, span_ref, cube_ref, templates_ref,
    keep_ref, send_ref, begins_ref, spans_ref, held_ref,
    bins_held_ref, sums_ref, parts_ref, window_ref, firsts_ref, cube_sem, small_sem, *, chunk,
):
    width, spaxels = cube_ref.shape
    total_bins = keep_ref.shape[0]
    full_width = templates_ref.shape[1]
    first = device_ref[0] * width
    window = window_ref.shape[1]
    base = pl.multiple_of(jnp.minimum(first // LANES * LANES, full_width - window), LANES)
    chunks = spaxels // chunk
    reach = chunk + SUB
    pieces = cube_sem.shape[0]

    def cube_copy(i):
        lanes = pl.ds(i * (spaxels // pieces), spaxels // pieces)
        return pltpu.make_async_copy(cube_ref.at[:, lanes], held_ref.at[pl.ds(0, width), lanes], cube_sem.at[i])

    bins_copy = pltpu.make_async_copy(bins_ref, bins_held_ref, small_sem.at[0])
    firsts_copy = pltpu.make_async_copy(bins_ref, firsts_ref, small_sem.at[1])
    window_copy = pltpu.make_async_copy(templates_ref.at[:, pl.ds(base, window)], window_ref, small_sem.at[2])
    line_copies = [
        pltpu.make_async_copy(begin_ref, begins_ref, small_sem.at[3]),
        pltpu.make_async_copy(span_ref, spans_ref, small_sem.at[4]),
    ]
    for copy in [bins_copy, firsts_copy] + [cube_copy(i) for i in range(pieces)] + [window_copy] + line_copies:
        copy.start()
    sums_ref[...] = jnp.zeros(sums_ref.shape, F32)
    joined = held_ref.shape[0] > width
    counted = sums_ref.shape[1] - COUNT_ROWS
    if joined:
        held_ref[width:, :] = jnp.ones((COUNT_ROWS, spaxels), F32)
    rows_at = lax.broadcasted_iota(jnp.int32, (reach, chunk), 0)
    bins_copy.wait()
    firsts_copy.wait()

    def low_bin(i):
        return pl.multiple_of(firsts_ref[0, i * chunk] // SUB * SUB, SUB)

    for i in range(chunks):
        if i % (chunks // pieces) == 0:
            cube_copy(i // (chunks // pieces)).wait()
        lanes = slice(i * chunk, (i + 1) * chunk)
        member = jnp.where(rows_at == bins_held_ref[:, lanes] - low_bin(i), 1.0, 0.0).astype(BF16)
        hi, mid, low = split3(held_ref[:, lanes])
        new = dot(member, hi, NT) + (dot(member, mid, NT) + dot(member, low, NT))
        if joined:
            parts_ref[i] = new
        else:
            parts_ref[i] = jnp.zeros(parts_ref.shape[1:], F32)
            parts_ref[i, :, :width] = new
            parts_ref[i, :, counted:] = dot(member, jnp.ones((COUNT_ROWS, chunk), BF16), NT)
    for i in range(chunks):
        sums_ref[pl.ds(low_bin(i), reach), :] += parts_ref[i]
    window_copy.wait()
    mine = pltpu.roll(window_ref[...], window - (first - base), 1)[:, :width]
    low_kept = device_ref[0] % 2 == 0
    block = min(total_bins, 512)
    for at in range(0, total_bins, block):
        rows = slice(at, at + block)
        means = sums_ref[rows, :width] / sums_ref[rows, counted : counted + 1]
        projections = dot_f32(means, mine, NT) * (1.0 / full_width)
        low, high = projections[:, :LANES], projections[:, LANES:]
        keep_ref[rows, :] = jnp.where(low_kept, low, high)
        send_ref[rows, :] = jnp.where(low_kept, high, low)
    for copy in line_copies:
        copy.wait()


COUNT_ROWS = 16


def project(device, bins, begin, span, cube, templates, total_bins):
    width, spaxels = cube.shape
    chunk = min(spaxels, 256)
    wide = -(-width // COUNT_ROWS) * COUNT_ROWS + COUNT_ROWS
    held = width if width % COUNT_ROWS else wide
    count, full_width = templates.shape
    return pl.pallas_call(
        functools.partial(project_kernel, chunk=chunk),
        in_specs=[pl.BlockSpec(memory_space=pltpu.SMEM)] + [pl.BlockSpec(memory_space=pltpu.HBM)] * 5,
        out_specs=[pl.BlockSpec(memory_space=pltpu.VMEM)] * 6,
        out_shape=[
            rows_of(total_bins),
            rows_of(total_bins),
            pltpu.VMEM(begin.shape, jnp.int32),
            pltpu.VMEM(span.shape, jnp.int32),
            pltpu.VMEM((held, spaxels), F32),
            pltpu.VMEM(bins.shape, jnp.int32),
        ],
        scratch_shapes=[
            pltpu.VMEM((total_bins + chunk + SUB, wide), F32),
            pltpu.VMEM((spaxels // chunk, chunk + SUB, wide), F32),
            pltpu.VMEM((count, template_window(width, full_width)), F32),
            pltpu.SMEM(bins.shape, jnp.int32),
            pltpu.SemaphoreType.DMA((min(spaxels // chunk, 2),)),
            pltpu.SemaphoreType.DMA((5,)),
        ],
        compiler_params=pltpu.CompilerParams(vmem_limit_bytes=VMEM_LIMIT),
        name="project",
    )(device, bins, begin, span, cube, templates)


def reciprocal(x):
    r = pl.reciprocal(x, approx=True)
    r = r * (2.0 - x * r)
    return r * (2.0 - x * r)


def eliminate(tile, start, stop):
    size = tile.shape[0]
    count = size // SUB
    lanes = lax.broadcasted_iota(jnp.int32, (SUB, size), 1)
    rows_at = lax.broadcasted_iota(jnp.int32, (SUB, size), 0)
    rows = [tile[i * SUB : (i + 1) * SUB, :] for i in range(count)]
    for k in range(start, stop):
        block = rows[k]
        first = k * SUB
        a = {}
        for i in range(SUB):
            for j in range(i, SUB):
                a[i, j] = jnp.broadcast_to(block[i : i + 1, first + j : first + j + 1], (SUB, size))

        def at(i, j):
            return (i, j) if i <= j else (j, i)

        for p in range(0, SUB, 2):
            q = p + 1
            pp, pq, qq = a[p, p], a[p, q], a[q, q]
            inverse = reciprocal(pp * qq - pq * pq)
            others = [i for i in range(SUB) if i not in (p, q)]
            old = {i: (a[at(i, p)], a[at(i, q)]) for i in others}
            new = {
                i: ((u * qq - v * pq) * inverse, (v * pp - u * pq) * inverse) for i, (u, v) in old.items()
            }
            for i in others:
                for j in others:
                    if i <= j:
                        a[i, j] = a[i, j] - new[i][0] * old[j][0] - new[i][1] * old[j][1]
            for i in others:
                a[at(i, p)], a[at(i, q)] = new[i]
            a[p, p], a[p, q], a[q, q] = -(qq * inverse), pq * inverse, -(pp * inverse)
        columns = []
        for j in range(SUB):
            column = a[at(0, j)]
            for i in range(1, SUB):
                column = jnp.where(rows_at == i, a[at(i, j)], column)
            columns.append(column)
        terms = [columns[j] * jnp.broadcast_to(block[j : j + 1, :], (SUB, size)) for j in range(SUB)]
        while len(terms) > 1:
            terms = [x + y for x, y in zip(terms[::2], terms[1::2])]
        swept = -terms[0]
        for j in range(SUB):
            swept = jnp.where(lanes == first + j, columns[j], swept)
        inside = (lanes >= first) & (lanes < first + SUB)
        spread_rows = [jnp.broadcast_to(swept[j : j + 1, :], (SUB, size)) for j in range(SUB)]
        order = list(range(k + 1, count)) + list(range(k))
        for i in order:
            terms = [
                jnp.broadcast_to(rows[i][:, first + j : first + j + 1], (SUB, size)) * spread_rows[j]
                for j in range(SUB)
            ]
            while len(terms) > 1:
                terms = [x + y for x, y in zip(terms[::2], terms[1::2])]
            rows[i] = jnp.where(inside, 0.0, rows[i]) - terms[0]
        rows[k] = swept
    return jnp.concatenate(rows, axis=0)


def gram_kernel(
    templates_ref, gram_ref, scale_ref, hi_ref, mid_ref, low_ref, held_ref, mid_held_ref, low_held_ref, sem, out_sem,
    *, chunk,
):
    count, full_width = templates_ref.shape

    def copy(i):
        lanes = pl.ds(i * chunk, chunk)
        return pltpu.make_async_copy(templates_ref.at[:, lanes], held_ref.at[:, lanes], sem.at[i])

    def out_copies(i):
        lanes = pl.ds(i * chunk, chunk)
        return [
            pltpu.make_async_copy(mid_held_ref.at[:, lanes], mid_ref.at[:, lanes], out_sem.at[0, i]),
            pltpu.make_async_copy(low_held_ref.at[:, lanes], low_ref.at[:, lanes], out_sem.at[1, i]),
        ]

    for i in range(full_width // chunk):
        copy(i).start()
    even = jnp.zeros((count, count), F32)
    mixed = jnp.zeros((count, count), F32)
    for i in range(full_width // chunk):
        copy(i).wait()
        lanes = slice(i * chunk, (i + 1) * chunk)
        hi, mid, low = split3(held_ref[:, lanes])
        hi_ref[:, lanes], mid_held_ref[:, lanes], low_held_ref[:, lanes] = hi, mid, low
        for out in out_copies(i):
            out.start()
        even = even + (dot(hi, hi, NT) + dot(mid, mid, NT))
        mixed = mixed + (dot(hi, mid, NT) + dot(hi, low, NT))
    gram = (even + (mixed + mixed.T)) * (1.0 / full_width)
    same = lax.broadcasted_iota(jnp.int32, gram.shape, 0) == lax.broadcasted_iota(jnp.int32, gram.shape, 1)
    diagonal = jnp.where(same, gram, 0.0)
    row = lax.rsqrt(jnp.sum(diagonal, axis=0, keepdims=True))
    column = lax.rsqrt(jnp.sum(diagonal, axis=1, keepdims=True))
    gram = gram * row * column
    scale_ref[...] = row
    gram_ref[...] = gram
    for i in range(full_width // chunk):
        for out in out_copies(i):
            out.wait()


def scaled_gram(templates, chunk):
    count, full_width = templates.shape
    vmem, hbm = (pl.BlockSpec(memory_space=space) for space in (pltpu.VMEM, pltpu.HBM))
    return pl.pallas_call(
        functools.partial(gram_kernel, chunk=chunk),
        in_specs=[hbm],
        out_specs=(vmem, vmem, vmem, hbm, hbm),
        out_shape=(
            jax.ShapeDtypeStruct((count, count), F32),
            jax.ShapeDtypeStruct((1, count), F32),
            pltpu.VMEM((count, full_width), BF16),
            pltpu.HBM((count, full_width), BF16),
            pltpu.HBM((count, full_width), BF16),
        ),
        scratch_shapes=[
            pltpu.VMEM((count, full_width), F32),
            pltpu.VMEM((count, full_width), BF16),
            pltpu.VMEM((count, full_width), BF16),
            pltpu.SemaphoreType.DMA((full_width // chunk,)),
            pltpu.SemaphoreType.DMA((2, full_width // chunk)),
        ],
        compiler_params=pltpu.CompilerParams(vmem_limit_bytes=VMEM_LIMIT),
        name="gram",
    )(templates)


STEPS = LANES // SUB
EARLY = 4


def first_kernel(gram_ref, first_ref, half_ref, second_ref):
    first = -eliminate(gram_ref[:LANES, :LANES], 0, STEPS)
    side = gram_ref[:LANES, LANES:]
    half = dot_f32(first, side, NN)
    first_ref[...] = first
    half_ref[...] = half
    second_ref[...] = eliminate(gram_ref[LANES:, LANES:] - dot_f32(side.T, half, NN), 0, EARLY)


def finish_kernel(first_ref, half_ref, second_ref, scale_ref, out_ref):
    first, half = first_ref[...], half_ref[...]
    last = -eliminate(second_ref[...], EARLY, STEPS)
    cross = dot_f32(half, last, NN)
    row = scale_ref[...]
    column = jnp.broadcast_to(row, (SUB, row.shape[1])).T[:, :1]
    near, far = row[:, :LANES], row[:, LANES:]
    out_ref[:LANES, :LANES] = (first + dot_f32(cross, half, NT)) * near * column[:LANES]
    out_ref[:LANES, LANES:] = -cross * far * column[:LANES]
    out_ref[LANES:, :LANES] = -cross.T * near * column[LANES:]
    out_ref[LANES:, LANES:] = last * far * column[LANES:]


def in_vmem(kernel, shapes, name, *arrays):
    return pl.pallas_call(
        kernel,
        out_shape=shapes,
        compiler_params=pltpu.CompilerParams(vmem_limit_bytes=VMEM_LIMIT),
        name=name,
    )(*arrays)


def window_sums(read, rows, first, begin, span):
    lines = begin.shape[0]
    sub = lax.broadcasted_iota(jnp.int32, (SUB, LANES), 0)
    spans = [jnp.broadcast_to(span[j : j + 1], (SUB, LANES)).astype(F32) for j in range(lines)]
    offsets = [
        (2 * (first + sub - jnp.broadcast_to(begin[j : j + 1], (SUB, LANES))) + 1).astype(F32) - spans[j]
        for j in range(lines)
    ]

    def add(block, shift, sums):
        size = block.shape[0]
        out = []
        for j in range(lines):
            m = offsets[j][:size] + shift
            masked = jnp.where(jnp.abs(m) < spans[j][:size], block, 0.0)
            weighted = masked * m
            out += [sums[3 * j] + masked, sums[3 * j + 1] + weighted, sums[3 * j + 2] + weighted * m]
        return out

    full = rows // SUB
    out = [jnp.zeros((1, LANES), F32)] * (3 * lines)
    if full:
        sums = [jnp.zeros((SUB, LANES), F32)] * (3 * lines)
        for i in range(full):
            sums = add(read(i * SUB, SUB), 2.0 * i * SUB, sums)
        out = [jnp.sum(x, axis=0, keepdims=True) for x in sums]
    if rows % SUB:
        sums = [jnp.zeros((rows % SUB, LANES), F32)] * (3 * lines)
        sums = add(read(full * SUB, rows % SUB), 2.0 * full * SUB, sums)
        out = [x + jnp.sum(y, axis=0, keepdims=True) for x, y in zip(out, sums)]
    return [out[3 * j + k] for k in range(3) for j in range(lines)]


def halving_order(devices):
    bits = devices.bit_length() - 1
    return list(range(2, bits)) + [1, 0]


def flips(position, devices):
    order = halving_order(devices)
    return sum(((position >> (len(order) - 1 - t)) & 1) << bit for t, bit in enumerate(order))


def cube_kernel(device_ref, begin_ref, span_ref, cube_ref, out_ref, *, devices, start, width):
    device = device_ref[0]
    rows = 3 * begin_ref.shape[0]

    def owner(i, carry):
        lanes = pl.ds(pl.multiple_of((device ^ flips(start + i, devices)) * LANES, LANES), LANES)
        sums = window_sums(
            lambda row, size: cube_ref[row : row + size, lanes],
            width,
            device * width,
            begin_ref[:, lanes],
            span_ref[:, lanes],
        )
        out_ref[pl.ds(pl.multiple_of(i * rows, SUB), rows), :] = jnp.concatenate(sums, axis=0)
        return carry

    lax.fori_loop(0, out_ref.shape[0] // rows, owner, 0)


def cube_windows(device, begin, span, cube, devices, start, stop, width):
    vmem = pl.BlockSpec(memory_space=pltpu.VMEM)
    return pl.pallas_call(
        functools.partial(cube_kernel, devices=devices, start=start, width=width),
        in_specs=[pl.BlockSpec(memory_space=pltpu.SMEM), vmem, vmem, vmem],
        out_shape=rows_of((stop - start) * 3 * begin.shape[0]),
        compiler_params=pltpu.CompilerParams(vmem_limit_bytes=VMEM_LIMIT),
        name="cube_windows",
    )(device, begin, span, cube)


def split_kernel(device_ref, x_ref, y_ref, keep_ref, send_ref):
    half = keep_ref.shape[0]
    total = x_ref[...] + y_ref[...]
    low_kept = (device_ref[0] >> 1) % 2 == 0
    keep_ref[...] = jnp.where(low_kept, total[:half], total[half:])
    send_ref[...] = jnp.where(low_kept, total[half:], total[:half])


def join_kernel(x_ref, y_ref, early_ref, late_ref, keep_ref, send_ref):
    slots, early = x_ref.shape[0], early_ref.shape[0]
    total = x_ref[...] + y_ref[...]
    keep_ref[...] = total
    send_ref[:slots, :] = total
    send_ref[slots : slots + early, :] = early_ref[...]
    send_ref[slots + early :, :] = late_ref[...]


def step_kernel(x_ref, y_ref, sums_ref, keep_ref, send_ref, *, slots):
    half = (y_ref.shape[0] - slots) // 2
    own = sums_ref.shape[0]
    total = x_ref[:slots, :] + y_ref[:slots, :]

    def gathered(first):
        value = y_ref[slots + first : slots + first + half, :]
        if x_ref.shape[0] > slots:
            value = value + x_ref[slots + first : slots + first + half, :]
        return value

    kept, sent = gathered(0), gathered(half) + sums_ref[own - half :, :]
    if own > half:
        kept = kept + sums_ref[:half, :]
    keep_ref[:slots, :] = total
    keep_ref[slots:, :] = kept
    send_ref[:slots, :] = total
    send_ref[slots:, :] = sent


def rows_of(count):
    return jax.ShapeDtypeStruct((count, LANES), F32)


def split_slots(device, x, y):
    vmem = pl.BlockSpec(memory_space=pltpu.VMEM)
    half = rows_of(x.shape[0] // 2)
    return pl.pallas_call(
        split_kernel,
        in_specs=[pl.BlockSpec(memory_space=pltpu.SMEM), vmem, vmem],
        out_shape=(half, half),
        compiler_params=pltpu.CompilerParams(vmem_limit_bytes=VMEM_LIMIT),
        name="split_slots",
    )(device, x, y)


def pick(bins_ref, device, lows, blocks, own, half):
    bins = bins_ref[:, pl.ds(pl.multiple_of(device * own, LANES), own)]
    bins = jnp.broadcast_to(bins, (SUB, own)).T[:, :1]
    total = None
    for low_bin, block in zip(lows, blocks):
        at = lax.broadcasted_iota(jnp.int32, (own, half), 1)
        member = jnp.where(at == bins - low_bin, 1.0, 0.0).astype(BF16)
        hi, mid, low = split3(block[:half, :])
        value = dot(member, hi, NN) + (dot(member, mid, NN) + dot(member, low, NN))
        total = value if total is None else total + value
    return total


def pick_kernel(device_ref, bins_ref, kept_ref, by_x_ref, by_core_ref, near_ref, far_ref, *, half):
    device = device_ref[0]
    own = near_ref.shape[0]
    kept_first = jnp.where((device >> 1) % 2 == 0, 0, half)
    lows = (kept_first, half - kept_first)
    near_ref[...] = pick(bins_ref, device, lows, (kept_ref, by_x_ref), own, half)
    far_ref[...] = pick(bins_ref, device, lows[:1], (by_core_ref,), own, half)


def pick_early(device, bins, kept, by_x, by_core, own, half):
    vmem = pl.BlockSpec(memory_space=pltpu.VMEM)
    return pl.pallas_call(
        functools.partial(pick_kernel, half=half),
        in_specs=[pl.BlockSpec(memory_space=pltpu.SMEM)] + [vmem] * 4,
        out_shape=(rows_of(own), rows_of(own)),
        compiler_params=pltpu.CompilerParams(vmem_limit_bytes=VMEM_LIMIT),
        name="pick_early",
    )(device, bins, kept, by_x, by_core)


def owner_kernel(
    device_ref, bins_ref, owner_ref, begin_ref, span_ref,
    kept_ref, by_x_ref, by_core_ref, by_both_ref, near_ref, far_ref, inverse_ref, hi_ref, mid_ref, low_ref,
    weights_ref, out_ref,
    continuum_ref, mine_ref, mid_held_ref, low_held_ref, owner_held_ref, begins_ref, spans_ref, starts_ref,
    parts_sem, small_sem, *, chunk,
):
    own_slots = weights_ref.shape[0]
    own = begins_ref.shape[1]
    lines = begin_ref.shape[0]
    full_width = hi_ref.shape[1]
    half = owner_held_ref.shape[1] // 2
    inverse = inverse_ref[...]
    device = device_ref[0]
    own_lanes = pl.ds(pl.multiple_of(device * own, LANES), own)

    small_copies = [
        pltpu.make_async_copy(owner_ref, owner_held_ref, small_sem.at[1]),
        pltpu.make_async_copy(begin_ref.at[:, own_lanes], begins_ref, small_sem.at[2]),
        pltpu.make_async_copy(span_ref.at[:, own_lanes], spans_ref, small_sem.at[3]),
        pltpu.make_async_copy(begin_ref.at[:, own_lanes], starts_ref, small_sem.at[4]),
    ]
    part_copies = [
        pltpu.make_async_copy(mid_ref, mid_held_ref, parts_sem.at[0]),
        pltpu.make_async_copy(low_ref, low_held_ref, parts_sem.at[1]),
    ]
    for copy in small_copies + part_copies:
        copy.start()

    core_low = device % 2 == 0
    low_kept = (device >> 1) % 2 == 0

    def lane_halves(near, far):
        return jnp.where(core_low, near, far), jnp.where(core_low, far, near)

    def by_lanes(near, far):
        return jnp.concatenate(lane_halves(near, far), axis=1)

    kept_first = jnp.where(low_kept, 0, half)
    far = far_ref[...] + pick(bins_ref, device, (half - kept_first,), (by_both_ref,), own, half)
    spaxel_weights = dot_f32(by_lanes(near_ref[...], far), inverse, NN)

    hi, mid, low = split3(spaxel_weights)
    tiles = chunk // LANES
    for i in range(full_width // chunk):
        first = hi_ref[:, i * chunk : (i + 1) * chunk]
        value = dot(hi, first, NN) + (dot(mid, first, NN) + dot(low, first, NN))
        for t in range(tiles):
            continuum_ref[i * tiles + t] = value[:, t * LANES : (t + 1) * LANES]
    for copy in small_copies + part_copies:
        copy.wait()

    for i in range(own_slots):
        picked_bin = owner_held_ref[0, device * own_slots + i]
        in_kept = (picked_bin >= half) == (kept_first > 0)
        row = pl.ds(picked_bin - jnp.where(picked_bin >= half, half, 0), 1)
        low, high = lane_halves(
            jnp.where(in_kept, kept_ref[row, :], by_x_ref[row, :]),
            jnp.where(in_kept, by_core_ref[row, :], by_both_ref[row, :]),
        )
        mine_ref[i : i + 1, :LANES] = low
        mine_ref[i : i + 1, LANES:] = high
    weights_ref[...] = dot_f32(mine_ref[...], inverse, NN)

    for i in range(full_width // chunk):
        lanes = slice(i * chunk, (i + 1) * chunk)
        second, third = mid_held_ref[:, lanes], low_held_ref[:, lanes]
        value = dot(hi, second, NN) + (dot(mid, second, NN) + dot(hi, third, NN))
        for t in range(tiles):
            continuum_ref[i * tiles + t] += value[:, t * LANES : (t + 1) * LANES]
    continuum_ref[full_width // LANES] = jnp.zeros((own, LANES), F32)

    begin = begins_ref[...]
    span = spans_ref[...].astype(F32)
    centre = 2.0 * (begin & (LANES - 1)).astype(F32) + span - 1.0
    rows_at = lax.broadcasted_iota(jnp.int32, (SUB, LANES), 0)
    at_row = [rows_at == r for r in range(SUB)]
    twice = 2.0 * lax.broadcasted_iota(jnp.int32, (LANES, own), 0).astype(F32)
    sums = [None] * (3 * lines)
    for j in range(lines):
        picks = ([], [])
        for g in range(own // SUB):
            rows = slice(g * SUB, (g + 1) * SUB)
            left = right = None
            for r in range(SUB):
                tile = lax.shift_right_logical(starts_ref[j, g * SUB + r], 7)
                a = continuum_ref[tile, rows, :]
                b = continuum_ref[tile + 1, rows, :]
                left = a if left is None else jnp.where(at_row[r], a, left)
                right = b if right is None else jnp.where(at_row[r], b, right)
            picks[0].append(left)
            picks[1].append(right)
        terms = None
        for side in range(2):
            block = jnp.concatenate(picks[side], axis=0).T
            m = twice + (2.0 * LANES * side - centre[j : j + 1])
            masked = jnp.where(jnp.abs(m) < span[j : j + 1], block, 0.0)
            weighted = masked * m
            new = [masked, weighted, weighted * m]
            terms = new if terms is None else [x + y for x, y in zip(terms, new)]
        for k in range(3):
            sums[k * lines + j] = jnp.sum(terms[k], axis=0, keepdims=True)
    continuum_sums = jnp.concatenate(sums, axis=0)

    own_rows = slice(half, half + 3 * lines)
    other_rows = slice(half + 3 * lines, half + 6 * lines)
    cube_sums = (kept_ref[own_rows, :] + by_x_ref[own_rows, :]) + (
        by_core_ref[other_rows, :] + by_both_ref[other_rows, :]
    )
    scale = jnp.concatenate([span, span * span, span * span * span], axis=0)
    out_ref[...] = (cube_sums - continuum_sums) / scale


def owned(device, bins, owner, begin, span, messages, inverse, parts, own_slots, own, chunk):
    vmem = pl.BlockSpec(memory_space=pltpu.VMEM)
    hbm = pl.BlockSpec(memory_space=pltpu.HBM)
    count, full_width = parts[0].shape
    lines = begin.shape[0]
    return pl.pallas_call(
        functools.partial(owner_kernel, chunk=chunk),
        in_specs=[pl.BlockSpec(memory_space=pltpu.SMEM)] + [vmem] + [hbm] * 3 + [vmem] * 8 + [hbm] * 2,
        out_shape=(
            jax.ShapeDtypeStruct((own_slots, count), F32),
            jax.ShapeDtypeStruct((3 * lines, own), F32),
        ),
        scratch_shapes=[
            pltpu.VMEM((full_width // LANES + 1, own, LANES), F32),
            pltpu.VMEM((own_slots, count), F32),
            pltpu.VMEM((count, full_width), BF16),
            pltpu.VMEM((count, full_width), BF16),
            pltpu.SMEM(owner.shape, jnp.int32),
            pltpu.VMEM((lines, own), jnp.int32),
            pltpu.VMEM((lines, own), jnp.int32),
            pltpu.SMEM((lines, own), jnp.int32),
            pltpu.SemaphoreType.DMA((2,)),
            pltpu.SemaphoreType.DMA((5,)),
        ],
        compiler_params=pltpu.CompilerParams(vmem_limit_bytes=VMEM_LIMIT),
        name="owned",
    )(device, bins, owner, begin, span, *messages, inverse, *parts)


def shards(cube, templates, bin_id, owner_bins, line_start, line_width):
    devices = lax.axis_size("spax")
    device = lax.axis_index("spax")
    spaxels = cube.shape[0]
    total_bins = owner_bins.shape[0]
    count = templates.shape[0]
    lines = line_start.shape[0]
    own_spaxels = spaxels // devices
    own_slots = total_bins // devices
    here = device.reshape(1).astype(jnp.int32)
    pin = lambda x: pltpu.with_memory_space_constraint(x, pltpu.HBM)
    columns = pin(cube.T)
    begin, span = pin(line_start), pin(line_width)
    bins, owner = pin(bin_id[None, :]), pin(owner_bins[None, :])
    after = lax.optimization_barrier

    def swap(x, bit):
        return lax.ppermute(x, "spax", [(d, d ^ (1 << bit)) for d in range(devices)])

    keep, send, begins, spans, held, bins_held = project(here, bins, begin, span, columns, pin(templates), total_bins)
    windows = lambda start, stop, now: cube_windows(
        now, begins, spans, held, devices, start, stop, cube.shape[1]
    )
    arrived = swap(send, 0)
    left = devices // 2
    cut = left + devices * 3 // 16
    early = windows(left, cut, here)
    keep, arrived, early = after((keep, arrived, early))
    keep, send = split_slots(here, keep, arrived)
    keep, send, now = after((keep, send, here))
    arrived = swap(send, 1)
    late, next_sums = windows(cut, devices, now), windows(left // 2, left, now)
    keep, arrived, early, late, next_sums, templates = after((keep, arrived, early, late, next_sums, templates))
    slots = total_bins // 2
    message = rows_of(slots + left * 3 * lines)
    keep, send = in_vmem(join_kernel, (rows_of(slots), message), "join", keep, arrived, early, late)

    keep, send, now, templates = after((keep, send, here, templates))
    gram = first = None
    for bit in range(2, devices.bit_length() - 1):
        arrived = swap(send, bit)
        left //= 2
        last_step = bit == devices.bit_length() - 2
        sums = next_sums if gram is None else windows(0 if last_step else left, 2 * left, now)
        if gram is None:
            gram, scale, *parts = scaled_gram(pin(templates), 512)
            arrived, sums, gram = after((arrived, sums, gram))
        elif first is None:
            first = in_vmem(first_kernel, [rows_of(LANES)] * 3, "first", gram)
            arrived, sums, first = after((arrived, sums, first))
        message = rows_of(slots + left * 3 * lines)
        keep, send = in_vmem(
            functools.partial(step_kernel, slots=slots), (message, message), "step", keep, arrived, sums
        )
        if first is None:
            keep, send, now, gram = after((keep, send, here, gram))
        else:
            keep, send, now, first = after((keep, send, here, first))

    by_x = swap(send, 1)
    by_core = swap(keep, 0)
    inverse = in_vmem(finish_kernel, jax.ShapeDtypeStruct((count, count), F32), "finish", *first, scale)
    by_x, by_core, inverse = after((by_x, by_core, inverse))
    by_both = swap(by_x, 0)
    near, far = pick_early(here, bins_held, keep, by_x, by_core, own_spaxels, slots)
    by_both, near, far = after((by_both, near, far))
    messages = (keep, by_x, by_core, by_both, near, far)
    parts = [parts[0], pin(parts[1]), pin(parts[2])]
    return owned(here, bins_held, owner, begin, span, messages, inverse, parts, own_slots, own_spaxels, 512)


def solution(mesh):
    placed = (
        P("strips", "spax"),
        P(),
        P("strips"),
        P("strips"),
        P(None, "strips"),
        P(None, "strips"),
    )
    return jax.shard_map(
        shards,
        mesh=mesh,
        in_specs=placed,
        out_specs=(P(("strips", "spax"), None), P(None, ("strips", "spax"))),
        check_vma=False,
    )
```
